128 devices in a mesh: section: 4 (over z), branch: 32 (over y, x, core).
Axes of the slice: x: 4, y: 4, z: 4, core: 2. Of those that a mesh axis runs over, the one named last changes fastest.
Arguments:
- layer_input: bfloat16 [4, 2, 4096, 4096], P('section', None, 'branch'), may hold values from -6 to 6
- cotangent: bfloat16 [2, 4096, 4096], P(None, 'branch'), may hold values from -6 to 6
- state_in: float32 [4, 2, 4096, 64], P('section', None, 'branch'), may hold values from -2 to 2
- state_out: float32 [4, 2, 4096, 64], P('section', None, 'branch'), may hold values from -2 to 2
- step_size: float32 [4, 2, 4096, 64], P('section', None, 'branch'), may hold values from 0.01 to 0.1
- saved_states: float32 [4, 2, 32, 64, 64, 64], P('section', None, 'branch'), may hold values from -6 to 6
- decay_rate: float32 [4, 64], P('section'), may hold values from 0.001 to 0.3
- skip_gain: float32 [4, 64], P('section'), may hold values from 0.5 to 1.5
- lengths: int32 [2, 16], replicated, may hold values from 32 to 128, as said below
Outputs:
- input_grad: bfloat16 [4, 2, 4096, 4096], P('section', None, 'branch')
- grad_state_in: float32 [4, 2, 4096, 64], P('section', None, 'branch')
- grad_state_out: float32 [4, 2, 4096, 64], P('section', None, 'branch')
- grad_step: float32 [4, 2, 4096, 64], P('section', None, 'branch')
- grad_decay: float32 [4, 64], P('section')
- grad_skip: float32 [4, 64], P('section')
The draws below stay inside these ranges and needn't reach their ends.
Inputs may be any that keep to these rules, and one draw needn't show every extreme that they name: lengths[m, j] counts the live tokens of completion j of family m; every family has a completion of exactly 128.
All inputs are finite; a program needn't handle non-finite values.
Results may differ from the reference program's by a relative error of at most 0.0058.
Values may be sent and summed in bfloat16 or wider, within the bound.
No kernel may reach another device: no remote copies, remote signals or barrier semaphores. Data moves between devices by JAX's collectives and lax.ppermute only.
A program may use at most 384 MiB of HBM per device.

```python
import math
import jax
import jax.numpy as jnp
from jax import lax

HEADS = 64
HEADDIM = 64
STATE = 64
ROWS = 128
MICRO = 2
SECTIONS = 4
WIDTH = 4096
SEGMENTS = 32
COMPLETIONS = 16
TOKENS = 4096


def draw_lengths(key, part):
    first, second = jax.random.split(jax.random.fold_in(key, 17))
    values = jax.random.randint(first, (MICRO, COMPLETIONS), ROWS // 4, ROWS + 1)
    picked = jax.random.randint(second, (MICRO, 1), 0, COMPLETIONS)
    return jnp.where(jnp.arange(COMPLETIONS)[None, :] == picked, ROWS, values).astype(jnp.int32)


def block_scale(rng, dims, cuts, low, high):
    gain = 1.0
    for dim, parts in cuts:
        draws = jax.random.uniform(jax.random.fold_in(jax.random.fold_in(rng, 6), dim), (parts,), jnp.float32, low / len(cuts), high / len(cuts))
        gain = gain * jnp.repeat(jnp.exp(draws), dims[dim] // parts).reshape((-1,) + (1,) * (len(dims) - 1 - dim))
    return gain


def noise(stream_key, dims, width, limit, shards=(), dtype=jnp.bfloat16):
    entries = jax.random.normal(stream_key, dims, jnp.float32) * width
    if len(shards) > 0:
        entries = block_scale(stream_key, dims, shards, -0.22, 0.18) * entries
    return jnp.clip(entries, min=-limit, max=limit).astype(dtype)


def setup_inputs(seed: int = 0) -> dict:
    seeds = jax.random.split(jax.random.key(seed), 10)
    return {
        "layer_input": noise(seeds[0], (SECTIONS, MICRO, TOKENS, WIDTH), 1.0, 6.0, ((0, 4), (2, 32))),
        "cotangent": noise(seeds[1], (MICRO, TOKENS, WIDTH), 1.0, 6.0, ((1, 32),)),
        "state_in": noise(seeds[2], (SECTIONS, MICRO, TOKENS, STATE), 0.3, 2.0, ((0, 4), (2, 32)), jnp.float32),
        "state_out": noise(seeds[3], (SECTIONS, MICRO, TOKENS, STATE), 0.3, 2.0, ((0, 4), (2, 32)), jnp.float32),
        "step_size": jnp.clip(jnp.exp(math.log(0.1) - 2.3025851 * jax.random.uniform(seeds[4], (SECTIONS, MICRO, TOKENS, HEADS), jnp.float32) ** block_scale(seeds[4], (SECTIONS, MICRO, TOKENS, HEADS), ((0, 4), (2, 32)), -0.2, 0.2)), 0.01, 0.1),
        "saved_states": noise(seeds[5], (SECTIONS, MICRO, SEGMENTS, HEADS, HEADDIM, STATE), 1.0, 6.0, ((0, 4), (2, 32)), jnp.float32),
        "decay_rate": jnp.clip(jnp.exp(math.log(0.3) - 5.7037825 * jax.random.uniform(seeds[6], (SECTIONS, HEADS), jnp.float32) ** block_scale(seeds[6], (SECTIONS, HEADS), ((0, 4),), -0.2, 0.2)), 0.001, 0.3),
        "skip_gain": jnp.clip(1.0 + 0.1 * jax.random.normal(seeds[7], (SECTIONS, HEADS), jnp.float32), 0.5, 1.5),
        "lengths": draw_lengths(jax.random.fold_in(seeds[9], 71), 0),
    }


HIGH = lax.Precision.HIGHEST

def decay_logs(step_rows, decay_vec):
    return jnp.cumsum(-decay_vec[None, :] * step_rows, axis=0)

def start_grad(upstream, out_rows, logdec):
    carried = jnp.exp(logdec)
    begin_grad = jnp.einsum('thp,tn->hpn', upstream * carried[:, :, None], out_rows, precision=HIGH)
    return (jnp.exp(logdec[-1]), begin_grad)

def local_terms(layer_x, upstream, in_rows, out_rows, step_rows, logdec):
    row_count = layer_x.shape[0]
    causal = jnp.arange(row_count)[:, None] >= jnp.arange(row_count)[None, :]
    lograte = logdec.T
    spread = lograte[:, :, None] - lograte[:, None, :]
    kernel = jnp.where(causal[None], jnp.exp(jnp.where(causal[None], spread, 0.0)), 0.0)
    affinity = jnp.dot(out_rows, in_rows.T, precision=HIGH)
    weighted = kernel * affinity[None]
    pair_grad = jnp.einsum('thp,uhp->htu', upstream, layer_x, precision=HIGH)
    scaled = kernel * pair_grad * step_rows.T[:, None, :]
    back_x = jnp.einsum('htu,thp->uhp', weighted, upstream, precision=HIGH)
    back_in = jnp.einsum('htu,tn->un', scaled, out_rows, precision=HIGH)
    back_out = jnp.einsum('htu,un->tn', scaled, in_rows, precision=HIGH)
    mixed_terms = scaled * affinity[None]
    back_log = (lax.optimization_barrier(jnp.sum(mixed_terms, axis=2)) - lax.optimization_barrier(jnp.sum(mixed_terms, axis=1))).T
    return (back_x, back_in, back_out, back_log)

def finish(layer_x, upstream, in_rows, out_rows, step_rows, logdec, decay_vec, gain_vec, saved_state, end_grad, local_part):
    back_x, back_in, back_out, back_log = local_part
    row_count = layer_x.shape[0]
    carried = jnp.exp(logdec)
    remain = jnp.exp(logdec[-1][None, :] - logdec)
    end_in = jnp.einsum('un,hpn->uhp', in_rows, end_grad, precision=HIGH)
    state_pull = back_x + remain[:, :, None] * end_in
    input_grad = gain_vec[None, :, None] * upstream + step_rows[:, :, None] * state_pull
    end_x = jnp.einsum('uhp,hpn->uhn', layer_x, end_grad, precision=HIGH)
    grad_in = back_in + jnp.einsum('uh,uhn->un', step_rows * remain, end_x, precision=HIGH)
    up_saved = jnp.einsum('thp,hpn->thn', upstream, saved_state, precision=HIGH)
    grad_out = back_out + jnp.einsum('th,thn->tn', carried, up_saved, precision=HIGH)
    read_saved = jnp.einsum('tn,hpn->thp', out_rows, saved_state, precision=HIGH)
    end_flow = step_rows * remain * lax.optimization_barrier(jnp.sum(layer_x * end_in, axis=2))
    last_term = jnp.exp(logdec[-1]) * lax.optimization_barrier(jnp.sum(end_grad * saved_state, axis=(1, 2))) + lax.optimization_barrier(jnp.sum(end_flow, axis=0))
    is_last = jnp.arange(row_count) == row_count - 1
    grad_log = back_log + carried * lax.optimization_barrier(jnp.sum(upstream * read_saved, axis=2)) - end_flow
    grad_log = grad_log + jnp.where(is_last[:, None], last_term[None, :], 0.0)
    grad_rate = jnp.cumsum(grad_log[::-1], axis=0)[::-1]
    grad_step = lax.optimization_barrier(jnp.sum(layer_x * state_pull, axis=2)) - decay_vec[None, :] * grad_rate
    decay_part = lax.optimization_barrier(jnp.sum(-step_rows * grad_rate, axis=0))
    skip_part = lax.optimization_barrier(jnp.sum(layer_x * upstream, axis=(0, 2)))
    return (input_grad, grad_in, grad_out, grad_step, decay_part, skip_part)

def reference(layer_input, cotangent, state_in, state_out, step_size, saved_states, decay_rate, skip_gain, lengths):
    prompt = SEGMENTS - COMPLETIONS
    grad_scale = 1.0 / math.sqrt(MICRO * TOKENS * HEADDIM)
    live_rows = jnp.arange(ROWS)[None, None, :] < lengths[:, :, None]
    keep_rows = jnp.concatenate([jnp.ones((MICRO, prompt, ROWS), bool), live_rows], axis=1)
    upstream_all = cotangent.astype(jnp.float32).reshape(MICRO, SEGMENTS, ROWS, HEADS, HEADDIM)
    upstream_all = jnp.where(keep_rows[:, :, :, None, None], upstream_all, 0.0)
    outs_input = [None] * SECTIONS
    outs_in = [None] * SECTIONS
    outs_out = [None] * SECTIONS
    outs_step = [None] * SECTIONS
    outs_decay = [None] * SECTIONS
    outs_skip = [None] * SECTIONS
    for section_at in range(SECTIONS - 1, -1, -1):
        decay_vec = decay_rate[section_at]
        gain_vec = skip_gain[section_at]
        list_input, list_in, list_out, list_step = ([], [], [], [])
        decay_acc = jnp.zeros((HEADS,), jnp.float32)
        skip_acc = jnp.zeros((HEADS,), jnp.float32)
        next_upstream = []
        for micro_at in range(MICRO):
            layer_x = layer_input[section_at, micro_at].astype(jnp.float32).reshape(SEGMENTS, ROWS, HEADS, HEADDIM)
            in_rows = state_in[section_at, micro_at].reshape(SEGMENTS, ROWS, STATE)
            out_rows = state_out[section_at, micro_at].reshape(SEGMENTS, ROWS, STATE)
            step_rows = step_size[section_at, micro_at].reshape(SEGMENTS, ROWS, HEADS)
            upstream = upstream_all[micro_at]
            logs = jax.vmap(decay_logs, (0, None))(step_rows, decay_vec)
            totals, begins = jax.vmap(start_grad)(upstream, out_rows, logs)
            fork_grad = lax.optimization_barrier(jnp.sum(begins[prompt:], axis=0))

            def chain_step(carry_grad, pieces):
                decay_total, begin_grad = pieces
                return (decay_total[:, None, None] * carry_grad + begin_grad, carry_grad)
            _, prompt_ends = lax.scan(chain_step, fork_grad, (totals[:prompt], begins[:prompt]), reverse=True)
            ends = jnp.concatenate([prompt_ends, jnp.zeros((COMPLETIONS, HEADS, HEADDIM, STATE), jnp.float32)], axis=0)

            def segment(pieces):
                seg_x, seg_up, seg_in, seg_out, seg_step, seg_log, seg_saved, seg_end = pieces
                local_part = local_terms(seg_x, seg_up, seg_in, seg_out, seg_step, seg_log)
                return finish(seg_x, seg_up, seg_in, seg_out, seg_step, seg_log, decay_vec, gain_vec, seg_saved, seg_end, local_part)
            results = lax.map(segment, (layer_x, upstream, in_rows, out_rows, step_rows, logs, saved_states[section_at, micro_at], ends))
            rounded = results[0].astype(jnp.bfloat16)
            list_input.append(rounded.reshape(TOKENS, WIDTH))
            list_in.append(results[1].reshape(TOKENS, STATE))
            list_out.append(results[2].reshape(TOKENS, STATE))
            list_step.append(results[3].reshape(TOKENS, HEADS))
            decay_acc = decay_acc + lax.optimization_barrier(jnp.sum(results[4], axis=0))
            skip_acc = skip_acc + lax.optimization_barrier(jnp.sum(results[5], axis=0))
            next_upstream.append(rounded.astype(jnp.float32))
        upstream_all = jnp.stack(next_upstream).reshape(MICRO, SEGMENTS, ROWS, HEADS, HEADDIM)
        outs_input[section_at] = jnp.stack(list_input)
        outs_in[section_at] = jnp.stack(list_in)
        outs_out[section_at] = jnp.stack(list_out)
        outs_step[section_at] = jnp.stack(list_step)
        outs_decay[section_at] = decay_acc * grad_scale
        outs_skip[section_at] = skip_acc * grad_scale
    return (jnp.stack(outs_input), jnp.stack(outs_in), jnp.stack(outs_out), jnp.stack(outs_step), jnp.stack(outs_decay), jnp.stack(outs_skip))
```

```python
import functools
import math

import jax
import jax.numpy as jnp
from jax import lax
from jax.experimental import pallas as pl
from jax.experimental.pallas import tpu as pltpu
from jax.sharding import PartitionSpec as P

F32 = jnp.float32
BF16 = jnp.bfloat16

SECTIONS = 4
FAMILIES = 2
ROWS = 128
STATE = 64
HEADDIM = 64
GROUP = 16
COLS = GROUP * HEADDIM
LANES = 128
CHUNK = 256
BRANCHES = 32
SEND_ROWS = 112
PACK_ROWS = FAMILIES * ROWS + 4 * GROUP
GRAD_ROWS = FAMILIES * (ROWS + GROUP)
VMEM_LIMIT = 48 * 1024 * 1024

NN = (((1,), (0,)), ((), ()))
NT = (((1,), (1,)), ((), ()))
TN = (((0,), (0,)), ((), ()))


def dot(a, b, dims):
    return lax.dot_general(a, b, dims, preferred_element_type=F32)


def split(a):
    high = a.astype(BF16)
    return high, (a - high.astype(F32)).astype(BF16)


def dot3(a, b, dims):
    return dot(a[0], b[0], dims) + dot(a[1], b[0], dims) + dot(a[0], b[1], dims)


def dot2(a, b, dims):
    return dot(a[0], b, dims) + dot(a[1], b, dims)


def lane_ids(shape):
    return lax.broadcasted_iota(jnp.int32, shape, len(shape) - 1)


def half(rolled, plain, side):
    lanes = lane_ids(plain.shape)
    if side == 0:
        return jnp.where(lanes < STATE, plain, 0.0)
    return jnp.where(lanes >= STATE, rolled, 0.0)


def expander():
    row = lax.broadcasted_iota(jnp.int32, (2 * GROUP, COLS), 0) & (GROUP - 1)
    col = lax.broadcasted_iota(jnp.int32, (2 * GROUP, COLS), 1) >> 6
    return jnp.where(row == col, 1.0, 0.0).astype(BF16)


def stack_split(a):
    high = a.astype(BF16).astype(F32)
    return jnp.concatenate([high, a - high], axis=0).astype(BF16)


class Layer:
    def __init__(self, pack_ref, layer, family):
        base = FAMILIES * ROWS
        both = pack_ref[layer, family * ROWS : (family + 1) * ROWS, :]
        turned = pltpu.roll(both, STATE, 1)
        self.b = (half(both, both, 0), half(turned, turned, 1))
        self.c = (half(turned, turned, 0), half(both, both, 1))
        self.step = pack_ref[layer, base + family * GROUP : base + (family + 1) * GROUP, :]
        self.decay = pack_ref[layer, base + 2 * GROUP : base + 3 * GROUP, :]
        gain = pack_ref[layer, base + 3 * GROUP : base + 4 * GROUP, :]
        row = lax.broadcasted_iota(jnp.int32, (ROWS, ROWS), 0)
        col = lax.broadcasted_iota(jnp.int32, (ROWS, ROWS), 1)
        self.row, self.col = row, col
        upper = jnp.where(row <= col, 1.0, 0.0).astype(BF16)
        drop = -self.decay * self.step
        first = drop.astype(BF16)
        rest = drop - first.astype(F32)
        second = rest.astype(BF16)
        third = (rest - second.astype(F32)).astype(BF16)
        logs = dot(first, upper, NN) + dot(second, upper, NN) + dot(third, upper, NN)
        carried = jnp.exp(logs)
        scale = self.step * jnp.exp(-logs)
        total = jnp.sum(jnp.where(lane_ids(carried.shape) == ROWS - 1, carried, 0.0), axis=1, keepdims=True)
        self.total = jnp.broadcast_to(total, (GROUP, LANES))
        self.carried2 = stack_split(carried)
        self.scale2 = stack_split(scale)
        self.gain2 = stack_split(gain)
        pulled = dot3(split(self.b[0]), split(self.c[0]), NT)
        self.pull = split(jnp.where(row <= col, pulled, 0.0))


def phase_a(family, upper_at, high, low, expand, send_ref):
    c_pair = split(jnp.concatenate([high.c[0], low.c[1]], axis=0))
    c_both = split(low.c[0] + low.c[1])
    b_both = high.b[0] + high.b[1]
    b_tile = jnp.concatenate([b_both] * (CHUNK // LANES), axis=1)
    lanes = lane_ids((STATE // 2, LANES))
    for chunk in range(COLS // CHUNK):
        cols = slice(chunk * CHUNK, (chunk + 1) * CHUNK)
        spread = expand[:, cols]
        carried = dot(high.carried2, spread, TN)
        scale = dot(high.scale2, spread, TN)
        gain = dot(high.gain2, spread, TN)
        low_carried = dot(low.carried2, spread, TN)
        upstream = upper_at(cols)
        hat = carried * upstream
        hat2 = split(hat)
        pulled = dot3(high.pull, hat2, NN)
        low_hat = low_carried * (gain * upstream + scale * pulled)
        low_hat2 = split(low_hat)
        both = tuple(jnp.concatenate([a, b], axis=0) for a, b in zip(hat2, low_hat2))
        begin = dot3(both, c_pair, TN).astype(BF16)
        response = split(low_carried * scale * b_tile)
        move = dot3(response, c_both, TN)
        for inner in range(CHUNK // HEADDIM):
            head = family * GROUP + chunk * (CHUNK // HEADDIM) + inner
            top = inner * HEADDIM
            send_ref[head, 0:HEADDIM, :] = begin[top : top + HEADDIM, :]
            first = move[top : top + 32, :]
            second = move[top + 32 : top + 64, :]
            send_ref[head, HEADDIM : HEADDIM + 32, :] = jnp.where(lanes < STATE, first, second).astype(BF16)
    totals = jnp.where(lane_ids((GROUP, LANES)) < STATE, high.total, low.total)
    total_high = totals.astype(BF16).astype(F32)
    total_low = totals - total_high
    place = lax.broadcasted_iota(jnp.int32, (16, LANES), 0)
    for inner in range(GROUP):
        one = jnp.broadcast_to(total_high[inner : inner + 1, :], (16, LANES))
        two = jnp.broadcast_to(total_low[inner : inner + 1, :], (16, LANES))
        block = jnp.where(place == 0, one, jnp.where(place == 1, two, 0.0))
        send_ref[family * GROUP + inner, 96:112, :] = block.astype(BF16)


def phase_b(family, side, upper_at, x_ref, s_ref, end_ref, layer, expand, put_grad):
    b, c = layer.b[side], layer.c[side]
    b2 = split(b)
    b_one, c_one = b2[0], c.astype(BF16)
    read = dot(c_one, b_one, NT)
    read = jnp.where(layer.row >= layer.col, read, 0.0).astype(BF16)
    pairs = jnp.zeros((ROWS, ROWS), F32)
    grad_out = jnp.zeros((ROWS, LANES), F32)
    grad_in = jnp.zeros((ROWS, LANES), F32)
    flow = jnp.zeros((GROUP, ROWS), F32)
    worth = jnp.zeros((GROUP, ROWS), F32)
    ending = jnp.zeros((GROUP, ROWS), F32)
    skips = jnp.zeros((GROUP, ROWS), F32)
    lanes = lane_ids((CHUNK, LANES))
    for chunk in range(COLS // CHUNK):
        cols = slice(chunk * CHUNK, (chunk + 1) * CHUNK)
        spread = expand[:, cols]
        one = spread[0:GROUP]
        carried = dot(layer.carried2, spread, TN)
        scale = dot(layer.scale2, spread, TN)
        gain = dot(layer.gain2, spread, TN)
        upstream = upper_at(cols)
        x = x_ref[family, :, cols].astype(F32)
        hat = carried * upstream
        hat2 = split(hat)
        hat_one = hat2[0]
        x_hat = scale * x
        x_one = x_hat.astype(BF16)
        per_chunk = CHUNK // HEADDIM
        first = family * GROUP + chunk * per_chunk
        ends = end_ref[first : first + per_chunk].reshape(CHUNK, LANES)
        top = (chunk % 2) * CHUNK
        packed = s_ref[family, top : top + CHUNK, :].astype(F32)
        if (chunk < 2) != (side == 0):
            packed = pltpu.roll(packed, STATE, 1)
        saved = jnp.where((lanes < STATE) == (side == 0), packed, 0.0)
        saved_one = saved.astype(BF16)
        end_in = dot2(b2, ends, NT)
        pulled = dot3(layer.pull, hat2, NN) + end_in
        put_grad(cols, (gain * upstream + scale * pulled).astype(BF16))
        forward = dot(read, x_one, NN) + dot(c_one, saved_one, NT)
        pairs = pairs + dot(hat_one, x_one, NT)
        grad_out = grad_out + dot(hat_one, saved_one, NN)
        grad_in = grad_in + dot(x_one, ends, NN)
        x_pulled = x_hat * pulled
        worth = worth + dot(one, x_pulled.astype(BF16), NT)
        flow = flow + dot(one, (hat * forward - x_pulled).astype(BF16), NT)
        ending = ending + dot(one, (x_hat * end_in).astype(BF16), NT)
        ending = ending + dot(one, (ends.astype(F32) * saved).astype(BF16), NN)
        skips = skips + dot(one, (x * upstream).astype(BF16), NT)
    pairs = jnp.where(layer.row >= layer.col, pairs, 0.0).astype(BF16)
    grad_out = grad_out + dot(pairs, b_one, NN)
    grad_in = grad_in + dot(pairs, c_one, TN)
    lanes = lane_ids((ROWS, LANES))
    if side == 0:
        grads = jnp.where(lanes < STATE, grad_in, pltpu.roll(grad_out, STATE, 1))
    else:
        grads = jnp.where(lanes < STATE, pltpu.roll(grad_in, STATE, 1), grad_out)
    later = jnp.where(layer.row >= layer.col, 1.0, 0.0).astype(BF16)
    rate = dot2(split(flow), later, NN) + jnp.sum(ending, axis=1, keepdims=True)
    grad_step = worth / layer.step - layer.decay * rate
    decay_part = jnp.sum(-layer.step * rate, axis=1, keepdims=True)
    skip_part = jnp.sum(skips, axis=1, keepdims=True)
    place = lane_ids((GROUP, LANES))
    small = jnp.where(place == 0, decay_part, jnp.where(place == 1, skip_part, 0.0))
    return grads, grad_step, small


def first_kernel(high_at, lengths_ref, cot_ref, pack_ref, send_ref, up_ref, cot_buf, sem):
    mine = lax.axis_index("section")
    branch = lax.axis_index("branch")
    at = pl.multiple_of(mine * COLS, COLS)
    copy = pltpu.make_async_copy(cot_ref.at[:, :, pl.ds(at, COLS)], cot_buf, sem)
    copy.start()
    expand = expander()
    copy.wait()
    for family in range(FAMILIES):
        slot = jnp.clip(branch - BRANCHES // 2, 0, BRANCHES // 2 - 1)
        limit = jnp.where(branch >= BRANCHES // 2, lengths_ref[family, slot], ROWS)

        def upper_at(cols):
            rows = lax.broadcasted_iota(jnp.int32, (ROWS, CHUNK), 0)
            value = jnp.where(rows < limit, cot_buf[family, :, cols].astype(F32), 0.0)
            up_ref[family, :, cols] = value.astype(BF16)
            return value

        high = Layer(pack_ref, high_at, family)
        low = Layer(pack_ref, high_at - 1, family)
        phase_a(family, upper_at, high, low, expand, send_ref)


def later_kernel(high_at, goes_on, *refs):
    pack_ref, up_ref, end_ref, own_x = refs[:4]
    x_refs, s_refs = refs[4:7], refs[7:11]
    outs = refs[11:]
    grad_refs, part_refs, small_ref = outs[0:4], outs[4:8], outs[8]
    rest = outs[9:]
    if goes_on:
        send_ref, next_ref = rest[0:2]
        rest = rest[2:]
    x_buf, s_buf, grad_buf, part_buf, x_sem, s_sem, grad_sem, part_sem = rest
    mine = lax.axis_index("section")
    at = pl.multiple_of(mine * COLS, COLS)
    sources = (own_x.at[0, :, :, pl.ds(at, COLS)],) + tuple(x_refs)
    for side in range(2):
        layer_at = high_at - side
        away = lax.rem(mine - layer_at + SECTIONS, SECTIONS)
        for k in range(SECTIONS):

            @pl.when(away == k)
            def _():
                pltpu.make_async_copy(sources[k], x_buf.at[side], x_sem.at[side]).start()
                pltpu.make_async_copy(s_refs[k], s_buf.at[side], s_sem.at[side]).start()

    expand = expander()
    for side in range(2):
        layer_at = high_at - side
        pltpu.make_async_copy(x_refs[0], x_buf.at[side], x_sem.at[side]).wait()
        pltpu.make_async_copy(s_refs[0], s_buf.at[side], s_sem.at[side]).wait()
        smalls = jnp.zeros((GROUP, LANES), F32)
        for family in range(FAMILIES):

            def upper_at(cols):
                if side == 0:
                    return up_ref[family, :, cols].astype(F32)
                return grad_buf[0, family, :, cols].astype(F32)

            def put_grad(cols, value):
                grad_buf[side, family, :, cols] = value

            layer = Layer(pack_ref, layer_at, family)
            grads, grad_step, small = phase_b(
                family, side, upper_at, x_buf.at[side], s_buf.at[side], end_ref, layer, expand, put_grad
            )
            part_buf[side, family * ROWS : (family + 1) * ROWS, :] = grads.astype(BF16)
            below = FAMILIES * ROWS + family * GROUP
            part_buf[side, below : below + GROUP, :] = grad_step.astype(BF16)
            smalls = smalls + small
        small_ref[side, :, :] = smalls
        ahead = lax.rem(layer_at - mine + SECTIONS, SECTIONS)
        for k in range(SECTIONS):

            @pl.when(ahead == k)
            def _():
                pltpu.make_async_copy(grad_buf.at[side], grad_refs[k], grad_sem.at[side]).start()
                pltpu.make_async_copy(part_buf.at[side], part_refs[k], part_sem.at[side]).start()

    if goes_on:
        next_ref[...] = grad_buf[1]
        for family in range(FAMILIES):

            def upper_at(cols):
                return grad_buf[1, family, :, cols].astype(F32)

            high = Layer(pack_ref, high_at - 2, family)
            low = Layer(pack_ref, high_at - 3, family)
            phase_a(family, upper_at, high, low, expand, send_ref)
    for side in range(2):
        pltpu.make_async_copy(grad_buf.at[side], grad_refs[0], grad_sem.at[side]).wait()
        pltpu.make_async_copy(part_buf.at[side], part_refs[0], part_sem.at[side]).wait()


def chain_kernel(got_ref, end_ref):
    lanes = lane_ids((STATE // 2, LANES))
    prompt = BRANCHES // 2
    fork = jnp.zeros((HEADDIM, LANES), F32)
    for at in range(prompt, BRANCHES):
        fork = fork + got_ref[at, 0:HEADDIM, :].astype(F32)
    plain, extra = fork, jnp.zeros((HEADDIM, LANES), F32)
    blank = jnp.zeros((STATE, LANES), F32)
    for at in range(prompt - 1, -1, -1):
        tail = got_ref[at, 96:112, :].astype(F32)
        total = tail[0:1, :] + tail[1:2, :]
        plain = total * plain
        extra = total * extra
        end_ref[at, :, :] = (plain + extra).astype(BF16)
        if at == 0:
            break
        packed = got_ref[at, HEADDIM : HEADDIM + 32, :].astype(F32)
        turned = pltpu.roll(packed, STATE, 1)
        move = jnp.concatenate(
            [jnp.where(lanes >= STATE, turned, 0.0), jnp.where(lanes >= STATE, packed, 0.0), blank], axis=0
        ).astype(BF16)
        extra = extra + dot2(split(plain), move, NN)
        plain = plain + got_ref[at, 0:HEADDIM, :].astype(F32)
    for at in range(prompt, BRANCHES):
        end_ref[at, :, :] = jnp.zeros((HEADDIM, LANES), BF16)


def pack_kernel(in_ref, out_ref, step_ref, decay_ref, gain_ref, pack_ref):
    base = FAMILIES * ROWS
    decay = jnp.transpose(jnp.broadcast_to(decay_ref[...], (LANES, SECTIONS * GROUP)))
    gain = jnp.transpose(jnp.broadcast_to(gain_ref[...], (LANES, SECTIONS * GROUP)))
    steps = [jnp.transpose(step_ref[0, family]) for family in range(FAMILIES)]
    both = [
        jnp.concatenate([in_ref[0, family], out_ref[0, family]], axis=1) for family in range(FAMILIES)
    ]
    for to in range(SECTIONS):
        heads = slice(to * GROUP, (to + 1) * GROUP)
        for family in range(FAMILIES):
            pack_ref[to, family * ROWS : (family + 1) * ROWS, :] = both[family]
            pack_ref[to, base + family * GROUP : base + (family + 1) * GROUP, :] = steps[family][heads]
        pack_ref[to, base + 2 * GROUP : base + 3 * GROUP, :] = decay[heads]
        pack_ref[to, base + 3 * GROUP : base + 4 * GROUP, :] = gain[heads]


def sort_kernel(at_ref, x1, x2, x3, s0, s1, s2, s3, o1, o2, o3, p0, p1, p2, p3):
    for x_ref, o_ref in ((x1, o1), (x2, o2), (x3, o3)):
        o_ref[0] = x_ref[0, 0]
    for s_ref, p_ref in ((s0, p0), (s1, p1), (s2, p2), (s3, p3)):
        whole = s_ref[0, 0, 0].reshape(COLS, STATE)
        p_ref[0] = jnp.concatenate([whole[: COLS // 2], whole[COLS // 2 :]], axis=1).astype(BF16)


def home_kernel(*refs):
    early_grads, late_grads = refs[0:4], refs[4:8]
    early_parts, late_parts = refs[8:12], refs[12:16]
    grad_ref, in_ref, out_ref, step_ref, part_buf, grad_sem, part_sem = refs[16:]
    mine = lax.axis_index("section")
    for is_early, grads, parts in ((True, early_grads, early_parts), (False, late_grads, late_parts)):

        @pl.when((mine >= 2) == is_early)
        def _():
            for k in range(SECTIONS):
                source = lax.rem(mine - k + SECTIONS, SECTIONS)
                at = pl.multiple_of(source * COLS, COLS)
                pltpu.make_async_copy(parts[k], part_buf.at[source], part_sem.at[k]).start()
                pltpu.make_async_copy(grads[k], grad_ref.at[0, :, :, pl.ds(at, COLS)], grad_sem.at[k]).start()

    for k in range(SECTIONS):
        pltpu.make_async_copy(early_parts[k], part_buf.at[k], part_sem.at[k]).wait()
    for family in range(FAMILIES):
        rows = slice(family * ROWS, (family + 1) * ROWS)
        total = part_buf[0, rows, :].astype(F32)
        for k in range(1, SECTIONS):
            total = total + part_buf[k, rows, :].astype(F32)
        in_ref[0, family] = total[:, 0:STATE]
        out_ref[0, family] = total[:, STATE:]
        below = FAMILIES * ROWS + family * GROUP
        steps = jnp.concatenate(
            [part_buf[k, below : below + GROUP, :].astype(F32) for k in range(SECTIONS)], axis=0
        )
        step_ref[0, family] = jnp.transpose(steps)
    for k in range(SECTIONS):
        pltpu.make_async_copy(early_grads[k], grad_ref.at[0, :, :, pl.ds(0, COLS)], grad_sem.at[k]).wait()


VM = pl.BlockSpec(memory_space=pltpu.VMEM)
SM = pl.BlockSpec(memory_space=pltpu.SMEM)
ANY = pl.BlockSpec(memory_space=pl.ANY)
PARAMS = pltpu.CompilerParams(vmem_limit_bytes=VMEM_LIMIT)


def shape(dims, dtype):
    return jax.ShapeDtypeStruct(dims, dtype)


def pack_small(state_in, state_out, step_size, decay_rate, skip_gain):
    return pl.pallas_call(
        pack_kernel,
        out_shape=shape((SECTIONS, PACK_ROWS, LANES), F32),
        in_specs=[VM] * 5,
        out_specs=VM,
        compiler_params=PARAMS,
        name="pack_small",
    )(state_in, state_out, step_size, decay_rate, skip_gain)


def sort_heads(layer_input, saved_states):
    mine = jnp.full((1,), lax.axis_index("section"), jnp.int32)

    def x_spec(k):
        return pl.BlockSpec(
            (1, 1, ROWS, COLS), lambda f, at: (0, f, 0, lax.rem(at[0] + k, SECTIONS))
        )

    def s_spec(k):
        return pl.BlockSpec(
            (1, 1, 1, GROUP, HEADDIM, STATE), lambda f, at: (0, f, 0, lax.rem(at[0] + k, SECTIONS), 0, 0)
        )

    x_out = pl.BlockSpec((1, ROWS, COLS), lambda f, at: (f, 0, 0))
    s_out = pl.BlockSpec((1, COLS // 2, LANES), lambda f, at: (f, 0, 0))
    outs = pl.pallas_call(
        sort_kernel,
        grid_spec=pltpu.PrefetchScalarGridSpec(
            num_scalar_prefetch=1,
            grid=(FAMILIES,),
            in_specs=[x_spec(1), x_spec(2), x_spec(3)] + [s_spec(k) for k in range(SECTIONS)],
            out_specs=[x_out] * 3 + [s_out] * 4,
        ),
        out_shape=[shape((FAMILIES, ROWS, COLS), BF16)] * 3 + [shape((FAMILIES, COLS // 2, LANES), BF16)] * 4,
        compiler_params=PARAMS,
        name="sort_heads",
    )(mine, layer_input, layer_input, layer_input, *([saved_states] * 4))
    return outs[:3], outs[3:]


def first_phase(high_at, lengths, cotangent, packs):
    return pl.pallas_call(
        functools.partial(first_kernel, high_at),
        out_shape=[
            shape((BRANCHES, SEND_ROWS, LANES), BF16),
            shape((FAMILIES, ROWS, COLS), BF16),
        ],
        in_specs=[SM, ANY, VM],
        out_specs=[VM, VM],
        scratch_shapes=[pltpu.VMEM((FAMILIES, ROWS, COLS), BF16), pltpu.SemaphoreType.DMA],
        compiler_params=PARAMS,
        name="first_phase",
    )(lengths, cotangent, packs)


def later_phase(high_at, goes_on, packs, upstream, ends, layer_input, xs, states):
    outs = [shape((FAMILIES, ROWS, COLS), BF16)] * 4
    outs += [shape((GRAD_ROWS, LANES), BF16)] * 4
    outs += [shape((2, GROUP, LANES), F32)]
    specs = [ANY] * 8 + [VM]
    if goes_on:
        outs += [shape((BRANCHES, SEND_ROWS, LANES), BF16), shape((FAMILIES, ROWS, COLS), BF16)]
        specs += [VM, VM]
    pair = pltpu.SemaphoreType.DMA((2,))
    return pl.pallas_call(
        functools.partial(later_kernel, high_at, goes_on),
        out_shape=outs,
        in_specs=[VM, VM, VM] + [ANY] * 8,
        out_specs=specs,
        scratch_shapes=[
            pltpu.VMEM((2, FAMILIES, ROWS, COLS), BF16),
            pltpu.VMEM((2, FAMILIES, COLS // 2, LANES), BF16),
            pltpu.VMEM((2, FAMILIES, ROWS, COLS), BF16),
            pltpu.VMEM((2, GRAD_ROWS, LANES), BF16),
            pair,
            pair,
            pair,
            pair,
        ],
        compiler_params=PARAMS,
        name="later_phase",
    )(packs, upstream, ends, layer_input, *xs, *states)


def chain(got):
    return pl.pallas_call(
        chain_kernel,
        out_shape=shape((BRANCHES, HEADDIM, LANES), BF16),
        in_specs=[VM],
        out_specs=VM,
        compiler_params=PARAMS,
        name="chain",
    )(got)


def home(early_grads, late_grads, early_parts, late_parts):
    return pl.pallas_call(
        home_kernel,
        out_shape=[
            shape((1, FAMILIES, ROWS, SECTIONS * COLS), BF16),
            shape((1, FAMILIES, ROWS, STATE), F32),
            shape((1, FAMILIES, ROWS, STATE), F32),
            shape((1, FAMILIES, ROWS, SECTIONS * GROUP), F32),
        ],
        in_specs=[ANY] * 16,
        out_specs=[ANY, VM, VM, VM],
        scratch_shapes=[
            pltpu.VMEM((SECTIONS, GRAD_ROWS, LANES), BF16),
            pltpu.SemaphoreType.DMA((SECTIONS,)),
            pltpu.SemaphoreType.DMA((SECTIONS,)),
        ],
        compiler_params=PARAMS,
        name="home",
    )(*early_grads, *late_grads, *early_parts, *late_parts)


def swap(value, axis):
    return lax.all_to_all(value, axis, 0, 0, tiled=True)


def send_on(value, k, targets):
    pairs = [(i, (i + k) % SECTIONS) for i in range(SECTIONS) if (i + k) % SECTIONS in targets]
    return lax.ppermute(value, "section", pairs)


def send_home(later, targets):
    grads = [later[0]] + [send_on(later[k], k, targets) for k in range(1, SECTIONS)]
    parts = [later[4]] + [send_on(later[4 + k], k, targets) for k in range(1, SECTIONS)]
    return grads, parts


def exchange(send):
    return swap(chain(swap(send, "branch")), "branch")


def shards(
    layer_input,
    cotangent,
    state_in,
    state_out,
    step_size,
    saved_states,
    decay_rate,
    skip_gain,
    lengths,
):
    grad_scale = 1.0 / math.sqrt(FAMILIES * ROWS * BRANCHES * HEADDIM)
    everyone = tuple(range(SECTIONS))
    packs = swap(pack_small(state_in, state_out, step_size, decay_rate, skip_gain), "section")
    packs, layer_input, saved_states = lax.optimization_barrier((packs, layer_input, saved_states))
    xs, states = sort_heads(layer_input, saved_states)
    xs = [send_on(xs[k - 1], k, everyone) for k in range(1, SECTIONS)]
    states = [states[0]] + [send_on(states[k], k, everyone) for k in range(1, SECTIONS)]
    send, upstream = first_phase(3, lengths, cotangent, packs)
    ends = exchange(send)
    early = later_phase(3, True, packs, upstream, ends, layer_input, xs, states)
    early_grads, early_parts = send_home(early, (2, 3))
    ends = exchange(early[9])
    late = later_phase(1, False, packs, early[10], ends, layer_input, xs, states)
    late_grads, late_parts = send_home(late, (0, 1))
    small = jnp.concatenate([early[8], late[8]], axis=0)[::-1, :, 0:2]
    small = jnp.transpose(small, (0, 2, 1)).reshape(1, 1, LANES)
    small = jnp.sum(swap(jnp.broadcast_to(small, (BRANCHES, 8, LANES)), "branch")[:, 0], axis=0)
    small = swap(small.reshape(SECTIONS, 2 * GROUP), "section").reshape(SECTIONS, 2, GROUP)
    small = small * grad_scale
    decay_sum = small[:, 0].reshape(1, SECTIONS * GROUP)
    skip_sum = small[:, 1].reshape(1, SECTIONS * GROUP)
    outs = home(early_grads, late_grads, early_parts, late_parts)
    return tuple(outs) + (decay_sum, skip_sum)


def solution(mesh):
    placed = (
        P("section", None, "branch", None),
        P(None, "branch", None),
        P("section", None, "branch", None),
        P("section", None, "branch", None),
        P("section", None, "branch", None),
        P("section", None, "branch", None, None, None),
        P("section", None),
        P("section", None),
        P(),
    )
    return jax.shard_map(
        shards,
        mesh=mesh,
        in_specs=placed,
        out_specs=(
            P("section", None, "branch", None),
            P("section", None, "branch", None),
            P("section", None, "branch", None),
            P("section", None, "branch", None),
            P("section", None),
            P("section", None),
        ),
        check_vma=False,
    )
```

```python
import functools
import math

import jax
import jax.numpy as jnp
from jax import lax
from jax.experimental import pallas as pl
from jax.experimental.pallas import tpu as pltpu
from jax.sharding import PartitionSpec as P

F32 = jnp.float32
BF16 = jnp.bfloat16

SECTIONS = 4
FAMILIES = 2
ROWS = 128
STATE = 64
HEADDIM = 64
GROUP = 16
COLS = GROUP * HEADDIM
LANES = 128
CHUNK = 256
BRANCHES = 32
SEND_ROWS = 112
PACK_ROWS = FAMILIES * ROWS + 4 * GROUP
GRAD_ROWS = FAMILIES * (ROWS + GROUP)
VMEM_LIMIT = 63 * 1024 * 1024

NN = (((1,), (0,)), ((), ()))
NT = (((1,), (1,)), ((), ()))
TN = (((0,), (0,)), ((), ()))


def dot(a, b, dims):
    return lax.dot_general(a, b, dims, preferred_element_type=F32)


def split(a):
    high = a.astype(BF16)
    return high, (a - high.astype(F32)).astype(BF16)


def dot3(a, b, dims):
    return dot(a[0], b[0], dims) + dot(a[1], b[0], dims) + dot(a[0], b[1], dims)


def dot2(a, b, dims):
    return dot(a[0], b, dims) + dot(a[1], b, dims)


def lane_ids(shape):
    return lax.broadcasted_iota(jnp.int32, shape, len(shape) - 1)


def half(rolled, plain, side):
    lanes = lane_ids(plain.shape)
    if side == 0:
        return jnp.where(lanes < STATE, plain, 0.0)
    return jnp.where(lanes >= STATE, rolled, 0.0)


def expander():
    row = lax.broadcasted_iota(jnp.int32, (2 * GROUP, COLS), 0) & (GROUP - 1)
    col = lax.broadcasted_iota(jnp.int32, (2 * GROUP, COLS), 1) >> 6
    return jnp.where(row == col, 1.0, 0.0).astype(BF16)


def stack_split(a):
    high = a.astype(BF16).astype(F32)
    return jnp.concatenate([high, a - high], axis=0).astype(BF16)


def fetch_packs(layers, pack_refs, pack_buf, sems):
    mine = lax.axis_index("section")
    for at in layers:
        away = lax.rem(mine - at + SECTIONS, SECTIONS)
        for k in range(SECTIONS):

            @pl.when(away == k)
            def _():
                pltpu.make_async_copy(pack_refs[k], pack_buf.at[at], sems.at[at]).start()


def wait_packs(layers, pack_refs, pack_buf, sems):
    for at in layers:
        pltpu.make_async_copy(pack_refs[0], pack_buf.at[at], sems.at[at]).wait()


class Layer:
    def __init__(self, pack_ref, layer, family):
        base = FAMILIES * ROWS
        both = pack_ref[layer, family * ROWS : (family + 1) * ROWS, :]
        turned = pltpu.roll(both, STATE, 1)
        self.b = (half(both, both, 0), half(turned, turned, 1))
        self.c = (half(turned, turned, 0), half(both, both, 1))
        self.step = pack_ref[layer, base + family * GROUP : base + (family + 1) * GROUP, :]
        self.decay = pack_ref[layer, base + 2 * GROUP : base + 3 * GROUP, :]
        gain = pack_ref[layer, base + 3 * GROUP : base + 4 * GROUP, :]
        row = lax.broadcasted_iota(jnp.int32, (ROWS, ROWS), 0)
        col = lax.broadcasted_iota(jnp.int32, (ROWS, ROWS), 1)
        self.row, self.col = row, col
        upper = jnp.where(row <= col, 1.0, 0.0).astype(BF16)
        drop = -self.decay * self.step
        first = drop.astype(BF16)
        rest = drop - first.astype(F32)
        second = rest.astype(BF16)
        third = (rest - second.astype(F32)).astype(BF16)
        logs = dot(first, upper, NN) + dot(second, upper, NN) + dot(third, upper, NN)
        carried = jnp.exp(logs)
        scale = self.step * jnp.exp(-logs)
        total = jnp.sum(jnp.where(lane_ids(carried.shape) == ROWS - 1, carried, 0.0), axis=1, keepdims=True)
        self.total = jnp.broadcast_to(total, (GROUP, LANES))
        self.carried2 = stack_split(carried)
        self.scale2 = stack_split(scale)
        self.gain2 = stack_split(gain)
        pulled = dot3(split(self.b[0]), split(self.c[0]), NT)
        self.pull = split(jnp.where(row <= col, pulled, 0.0))


def phase_a(family, upper_at, high, low, expand, send_ref):
    c_pair = split(jnp.transpose(jnp.concatenate([high.c[0], low.c[1]], axis=0)))
    c_both = split(jnp.transpose(low.c[0] + low.c[1]))
    b_both = high.b[0] + high.b[1]
    b_tile = jnp.concatenate([b_both] * (CHUNK // LANES), axis=1)
    lanes = lane_ids((STATE // 2, LANES))
    for chunk in range(COLS // CHUNK):
        cols = slice(chunk * CHUNK, (chunk + 1) * CHUNK)
        spread = expand[:, cols]
        carried = dot(high.carried2, spread, TN)
        scale = dot(high.scale2, spread, TN)
        gain = dot(high.gain2, spread, TN)
        low_carried = dot(low.carried2, spread, TN)
        upstream = upper_at(cols)
        hat = carried * upstream
        hat2 = split(hat)
        pulled = dot(high.pull[0], hat2[0], NN)
        low_hat = low_carried * (gain * upstream + scale * pulled)
        low_hat2 = split(low_hat)
        both = tuple(jnp.concatenate([a, b], axis=0) for a, b in zip(hat2, low_hat2))
        begin = jnp.transpose(dot3(c_pair, both, NN)).astype(BF16)
        response = split(low_carried * scale * b_tile)
        move = jnp.transpose(dot3(c_both, response, NN))
        for inner in range(CHUNK // HEADDIM):
            head = family * GROUP + chunk * (CHUNK // HEADDIM) + inner
            top = inner * HEADDIM
            send_ref[head, 0:HEADDIM, :] = begin[top : top + HEADDIM, :]
            first = move[top : top + 32, :]
            second = move[top + 32 : top + 64, :]
            send_ref[head, HEADDIM : HEADDIM + 32, :] = jnp.where(lanes < STATE, first, second).astype(BF16)
    totals = jnp.where(lane_ids((GROUP, LANES)) < STATE, high.total, low.total)
    total_high = totals.astype(BF16).astype(F32)
    total_low = totals - total_high
    place = lax.broadcasted_iota(jnp.int32, (16, LANES), 0)
    for inner in range(GROUP):
        one = jnp.broadcast_to(total_high[inner : inner + 1, :], (16, LANES))
        two = jnp.broadcast_to(total_low[inner : inner + 1, :], (16, LANES))
        block = jnp.where(place == 0, one, jnp.where(place == 1, two, 0.0))
        send_ref[family * GROUP + inner, 96:112, :] = block.astype(BF16)


def phase_b(family, side, layer, upper_at, end_ref, expand, put_grad):
    b2 = split(layer.b[side])
    per_chunk = CHUNK // HEADDIM
    for chunk in range(COLS // CHUNK):
        cols = slice(chunk * CHUNK, (chunk + 1) * CHUNK)
        spread = expand[:, cols]
        carried = dot(layer.carried2, spread, TN)
        scale = dot(layer.scale2, spread, TN)
        gain = dot(layer.gain2, spread, TN)
        upstream = upper_at(cols)
        first = family * GROUP + chunk * per_chunk
        ends = end_ref[first : first + per_chunk].reshape(CHUNK, LANES)
        pulled = dot(layer.pull[0], (carried * upstream).astype(BF16), NN) + dot2(b2, ends, NT)
        put_grad(cols, (gain * upstream + scale * pulled).astype(BF16))


def phase_c(family, side, layer, upper_at, x_ref, s_ref, end_ref, expand):
    b_one, c_one = layer.b[side].astype(BF16), layer.c[side].astype(BF16)
    pull = layer.pull[0]
    read = dot(c_one, b_one, NT)
    read = jnp.where(layer.row >= layer.col, read, 0.0).astype(BF16)
    pairs = jnp.zeros((ROWS, ROWS), F32)
    grad_out = jnp.zeros((ROWS, LANES), F32)
    grad_in = jnp.zeros((ROWS, LANES), F32)
    flow = jnp.zeros((GROUP, ROWS), F32)
    worth = jnp.zeros((GROUP, ROWS), F32)
    ending = jnp.zeros((GROUP, ROWS), F32)
    skips = jnp.zeros((GROUP, ROWS), F32)
    lanes = lane_ids((CHUNK, LANES))
    per_chunk = CHUNK // HEADDIM
    for chunk in range(COLS // CHUNK):
        cols = slice(chunk * CHUNK, (chunk + 1) * CHUNK)
        spread = expand[:, cols]
        one = spread[0:GROUP]
        carried = dot(layer.carried2, spread, TN)
        scale = dot(layer.scale2, spread, TN)
        upstream = upper_at(cols)
        x = x_ref[family, :, cols].astype(F32)
        hat = carried * upstream
        hat_one = hat.astype(BF16)
        x_hat = scale * x
        x_one = x_hat.astype(BF16)
        first = family * GROUP + chunk * per_chunk
        ends = end_ref[first : first + per_chunk].reshape(CHUNK, LANES)
        top = (chunk % 2) * CHUNK
        packed = s_ref[family, top : top + CHUNK, :].astype(F32)
        if (chunk < 2) != (side == 0):
            packed = pltpu.roll(packed, STATE, 1)
        saved = jnp.where((lanes < STATE) == (side == 0), packed, 0.0)
        saved_one = saved.astype(BF16)
        end_in = dot(b_one, ends, NT)
        pulled = dot(pull, hat_one, NN) + end_in
        forward = dot(read, x_one, NN) + dot(c_one, saved_one, NT)
        pairs = pairs + dot(hat_one, x_one, NT)
        grad_out = grad_out + dot(hat_one, saved_one, NN)
        grad_in = grad_in + dot(x_one, ends, NN)
        x_pulled = x_hat * pulled
        worth = worth + dot(one, x_pulled.astype(BF16), NT)
        flow = flow + dot(one, (hat * forward - x_pulled).astype(BF16), NT)
        ending = ending + dot(one, (x_hat * end_in).astype(BF16), NT)
        ending = ending + dot(one, (ends.astype(F32) * saved).astype(BF16), NN)
        skips = skips + dot(one, (x * upstream).astype(BF16), NT)
    pairs = jnp.where(layer.row >= layer.col, pairs, 0.0).astype(BF16)
    grad_out = grad_out + dot(pairs, b_one, NN)
    grad_in = grad_in + dot(pairs, c_one, TN)
    lanes = lane_ids((ROWS, LANES))
    if side == 0:
        grads = jnp.where(lanes < STATE, grad_in, pltpu.roll(grad_out, STATE, 1))
    else:
        grads = jnp.where(lanes < STATE, pltpu.roll(grad_in, STATE, 1), grad_out)
    later = jnp.where(layer.row >= layer.col, 1.0, 0.0).astype(BF16)
    rate = dot2(split(flow), later, NN) + jnp.sum(ending, axis=1, keepdims=True)
    grad_step = worth / layer.step - layer.decay * rate
    decay_part = jnp.sum(-layer.step * rate, axis=1, keepdims=True)
    skip_part = jnp.sum(skips, axis=1, keepdims=True)
    place = lane_ids((GROUP, LANES))
    small = jnp.where(place == 0, decay_part, jnp.where(place == 1, skip_part, 0.0))
    return grads, grad_step, small


def first_kernel(high_at, after, *refs):
    lengths_ref, cot_ref = refs[:2]
    pack_refs = refs[2:6]
    send_ref, up_ref, cot_buf, send_buf, pack_ref, sems, pack_sem = refs[6 + after :]
    layers = (high_at, high_at - 1)
    fetch_packs(layers, pack_refs, pack_ref, pack_sem)
    mine = lax.axis_index("section")
    branch = lax.axis_index("branch")
    at = pl.multiple_of(mine * COLS, COLS)
    copy = pltpu.make_async_copy(cot_ref.at[:, :, pl.ds(at, COLS)], cot_buf, sems.at[3])
    copy.start()
    expand = expander()
    wait_packs(layers, pack_refs, pack_ref, pack_sem)
    copy.wait()
    copies = []
    for family in range(FAMILIES):
        slot = jnp.clip(branch - BRANCHES // 2, 0, BRANCHES // 2 - 1)
        limit = jnp.where(branch >= BRANCHES // 2, lengths_ref[family, slot], ROWS)

        def upper_at(cols):
            rows = lax.broadcasted_iota(jnp.int32, (ROWS, CHUNK), 0)
            value = jnp.where(rows < limit, cot_buf[family, :, cols].astype(F32), 0.0)
            cot_buf[family, :, cols] = value.astype(BF16)
            return value

        high = Layer(pack_ref, high_at, family)
        low = Layer(pack_ref, high_at - 1, family)
        phase_a(family, upper_at, high, low, expand, send_buf)
        heads = pl.ds(family * GROUP, GROUP)
        copies.append(pltpu.make_async_copy(send_buf.at[heads], send_ref.at[heads], sems.at[family]))
        copies[-1].start()
    copies.append(pltpu.make_async_copy(cot_buf, up_ref, sems.at[2]))
    copies[-1].start()
    for copy in copies:
        copy.wait()


def later_kernel(high_at, goes_on, after, *refs):
    pack_refs = refs[:4]
    up_ref, end_ref = refs[4:6]
    refs = refs[6 + after :]
    grad_refs, keep_refs = refs[0:4], refs[4:6]
    rest = refs[6:]
    if goes_on:
        send_ref, grad_buf, up_buf, end_buf, pack_ref, grad_sem, keep_sem, in_sem, pack_sem, send_buf, send_sem = rest
    else:
        grad_buf, up_buf, end_buf, pack_ref, grad_sem, keep_sem, in_sem, pack_sem = rest
    layers = range(high_at, high_at - (4 if goes_on else 2), -1)
    fetch_packs(layers[:2], pack_refs, pack_ref, pack_sem)
    ins = [
        pltpu.make_async_copy(up_ref, up_buf, in_sem.at[0]),
        pltpu.make_async_copy(end_ref, end_buf, in_sem.at[1]),
    ]
    for copy in ins:
        copy.start()
    fetch_packs(layers[2:], pack_refs, pack_ref, pack_sem)
    mine = lax.axis_index("section")
    expand = expander()
    wait_packs(layers[:2], pack_refs, pack_ref, pack_sem)
    for copy in ins:
        copy.wait()
    for side in range(2):
        layer_at = high_at - side
        for family in range(FAMILIES):

            def upper_at(cols):
                if side == 0:
                    return up_buf[family, :, cols].astype(F32)
                return grad_buf[0, family, :, cols].astype(F32)

            def put_grad(cols, value):
                grad_buf[side, family, :, cols] = value

            layer = Layer(pack_ref, layer_at, family)
            phase_b(family, side, layer, upper_at, end_buf, expand, put_grad)
        ahead = lax.rem(layer_at - mine + SECTIONS, SECTIONS)
        for k in range(SECTIONS):

            @pl.when(ahead == k)
            def _():
                pltpu.make_async_copy(grad_buf.at[side], grad_refs[k], grad_sem.at[side]).start()

    copies = [pltpu.make_async_copy(grad_buf.at[side], keep_refs[side], keep_sem.at[side]) for side in range(2)]
    for copy in copies:
        copy.start()
    if goes_on:
        wait_packs(layers[2:], pack_refs, pack_ref, pack_sem)
        for family in range(FAMILIES):

            def upper_at(cols):
                return grad_buf[1, family, :, cols].astype(F32)

            high = Layer(pack_ref, high_at - 2, family)
            low = Layer(pack_ref, high_at - 3, family)
            phase_a(family, upper_at, high, low, expand, send_buf)
            heads = pl.ds(family * GROUP, GROUP)
            copies.append(pltpu.make_async_copy(send_buf.at[heads], send_ref.at[heads], send_sem.at[family]))
            copies[-1].start()
    for copy in copies:
        copy.wait()
    for side in range(2):
        pltpu.make_async_copy(grad_buf.at[side], grad_refs[0], grad_sem.at[side]).wait()


def other_kernel(high_at, sides, after, *refs):
    pack_refs, up_refs = refs[:4], refs[4:6]
    end_ref, own_x = refs[6:8]
    x_refs, s_refs = refs[8:11], refs[11:15]
    held_ref, small_refs = refs[15], refs[16:18]
    refs = refs[18 + after :]
    last = 1 in sides
    part_refs, rest = (refs[:4], refs[4:]) if last else (refs[:1], refs[1:])
    rate_ref, rest = rest[0], rest[1:]
    x_buf, s_buf, up_buf, end_buf, part_buf, pack_ref, x_sem, s_sem, up_sem, part_sem, end_sem, pack_sem = rest
    mine = lax.axis_index("section")
    at = pl.multiple_of(mine * COLS, COLS)
    sources = (own_x.at[0, :, :, pl.ds(at, COLS)],) + tuple(x_refs)
    layers = [high_at - side for side in sides]
    fetch_packs(layers, pack_refs, pack_ref, pack_sem)
    ends = pltpu.make_async_copy(end_ref, end_buf, end_sem.at[0])
    ends.start()
    for side in sides:
        away = lax.rem(mine - (high_at - side) + SECTIONS, SECTIONS)
        pltpu.make_async_copy(up_refs[side], up_buf.at[side], up_sem.at[side]).start()
        for k in range(SECTIONS):

            @pl.when(away == k)
            def _():
                pltpu.make_async_copy(sources[k], x_buf.at[side], x_sem.at[side]).start()
                pltpu.make_async_copy(s_refs[k], s_buf.at[side], s_sem.at[side]).start()

    if sides == (1,):
        held = pltpu.make_async_copy(held_ref, part_buf.at[0], part_sem.at[0])
        held.start()
    expand = expander()
    wait_packs(layers, pack_refs, pack_ref, pack_sem)
    ends.wait()
    smalls_of = []
    for side in sides:
        pltpu.make_async_copy(up_refs[side], up_buf.at[side], up_sem.at[side]).wait()
        pltpu.make_async_copy(x_refs[0], x_buf.at[side], x_sem.at[side]).wait()
        pltpu.make_async_copy(s_refs[0], s_buf.at[side], s_sem.at[side]).wait()
        smalls = jnp.zeros((GROUP, LANES), F32)
        for family in range(FAMILIES):

            def upper_at(cols):
                return up_buf[side, family, :, cols].astype(F32)

            layer = Layer(pack_ref, high_at - side, family)
            grads, grad_step, small = phase_c(
                family, side, layer, upper_at, x_buf.at[side], s_buf.at[side], end_buf, expand
            )
            part_buf[side, family * ROWS : (family + 1) * ROWS, :] = grads.astype(BF16)
            below = FAMILIES * ROWS + family * GROUP
            part_buf[side, below : below + GROUP, :] = grad_step.astype(BF16)
            smalls = smalls + small
        smalls_of.append(smalls)
    if len(sides) == 1:
        rate_ref[...] = smalls_of[0]
    else:
        blocks = smalls_of[::-1] + [small_refs[1][...], small_refs[0][...]]
        turned = jnp.transpose(jnp.concatenate(blocks + [jnp.zeros((STATE, LANES), F32)], axis=0))
        row = turned[0:1] + pltpu.roll(turned[1:2], STATE, 1)
        rate_ref[...] = jnp.broadcast_to(row[None], (BRANCHES, 1, LANES))
    if not last:
        copy = pltpu.make_async_copy(part_buf.at[0], part_refs[0], part_sem.at[0])
        copy.start()
        copy.wait()
        return
    if sides == (1,):
        held.wait()
    for side in range(2):
        ahead = lax.rem(high_at - side - mine + SECTIONS, SECTIONS)
        for k in range(SECTIONS):

            @pl.when(ahead == k)
            def _():
                pltpu.make_async_copy(part_buf.at[side], part_refs[k], part_sem.at[side]).start()

    for side in range(2):
        pltpu.make_async_copy(part_buf.at[side], part_refs[0], part_sem.at[side]).wait()


def chain_kernel(*refs):
    got_ref, end_ref = refs[0], refs[-1]
    lanes = lane_ids((STATE // 2, LANES))
    prompt = BRANCHES // 2
    fork = jnp.zeros((HEADDIM, LANES), F32)
    for at in range(prompt, BRANCHES):
        fork = fork + got_ref[at, 0:HEADDIM, :].astype(F32)
    plain, extra = fork, jnp.zeros((HEADDIM, LANES), F32)
    blank = jnp.zeros((STATE, LANES), F32)
    for at in range(prompt - 1, -1, -1):
        tail = got_ref[at, 96:112, :].astype(F32)
        total = tail[0:1, :] + tail[1:2, :]
        plain = total * plain
        extra = total * extra
        end_ref[at, :, :] = (plain + extra).astype(BF16)
        if at == 0:
            break
        packed = got_ref[at, HEADDIM : HEADDIM + 32, :].astype(F32)
        turned = pltpu.roll(packed, STATE, 1)
        move = jnp.concatenate(
            [jnp.where(lanes >= STATE, turned, 0.0), jnp.where(lanes >= STATE, packed, 0.0), blank], axis=0
        ).astype(BF16)
        extra = extra + dot2(split(plain), move, NN)
        plain = plain + got_ref[at, 0:HEADDIM, :].astype(F32)
    for at in range(prompt, BRANCHES):
        end_ref[at, :, :] = jnp.zeros((HEADDIM, LANES), BF16)


def pack_kernel(*refs):
    sources, decay_ref, gain_ref = refs[0:3], refs[3], refs[4]
    pack_refs = refs[5:9]
    in_ref, out_ref, step_ref, both_ref, rate_ref, sems, send_sems = refs[9:]
    copies = [
        pltpu.make_async_copy(source.at[0], to, sems.at[at])
        for at, (source, to) in enumerate(zip(sources, (in_ref, out_ref, step_ref)))
    ]
    for copy in copies:
        copy.start()
    mine = lax.axis_index("section")
    base = FAMILIES * ROWS
    rate_ref[0] = jnp.transpose(jnp.broadcast_to(decay_ref[...], (LANES, SECTIONS * GROUP)))
    rate_ref[1] = jnp.transpose(jnp.broadcast_to(gain_ref[...], (LANES, SECTIONS * GROUP)))
    for copy in copies:
        copy.wait()
    for k in range(SECTIONS):
        heads = pl.ds(pl.multiple_of(lax.rem(mine + k, SECTIONS) * GROUP, GROUP), GROUP)
        for family in range(FAMILIES):
            both_ref[k, base + family * GROUP : base + (family + 1) * GROUP, :] = step_ref[family, heads, :]
        both_ref[k, base + 2 * GROUP : base + 3 * GROUP, :] = rate_ref[0, heads, :]
        both_ref[k, base + 3 * GROUP : base + 4 * GROUP, :] = rate_ref[1, heads, :]
    for family in range(FAMILIES):
        turned = jnp.transpose(jnp.concatenate([in_ref[family], out_ref[family]], axis=0))
        for k in range(SECTIONS):
            both_ref[k, family * ROWS : (family + 1) * ROWS, :] = turned
    copies = []
    for k in range(SECTIONS):
        copies.append(pltpu.make_async_copy(both_ref.at[k], pack_refs[k], send_sems.at[k]))
        copies[-1].start()
    for copy in copies:
        copy.wait()


def sort_kernel(at_ref, x1, x2, x3, s0, s1, s2, s3, o1, o2, o3, p0, p1, p2, p3):
    for x_ref, o_ref in ((x1, o1), (x2, o2), (x3, o3)):
        o_ref[0] = x_ref[0, 0]
    for s_ref, p_ref in ((s0, p0), (s1, p1), (s2, p2), (s3, p3)):
        whole = s_ref[0, 0, 0].reshape(COLS, STATE)
        p_ref[0] = jnp.concatenate([whole[: COLS // 2], whole[COLS // 2 :]], axis=1).astype(BF16)


def fetch_home(early, late, to, sems):
    mine = lax.axis_index("section")
    for is_early, pieces in ((True, early), (False, late)):

        @pl.when((mine >= 2) == is_early)
        def _():
            for k in range(SECTIONS):
                source = lax.rem(mine - k + SECTIONS, SECTIONS)
                pltpu.make_async_copy(pieces[k], to(source), sems.at[k]).start()

    for k in range(SECTIONS):
        pltpu.make_async_copy(early[k], to(k), sems.at[k]).wait()


def home_small_kernel(*refs):
    early, late = refs[0:4], refs[4:8]
    in_ref, out_ref, step_ref, part_buf, part_sem = refs[8:]
    fetch_home(early, late, lambda source: part_buf.at[source], part_sem)
    for family in range(FAMILIES):
        rows = slice(family * ROWS, (family + 1) * ROWS)
        total = part_buf[0, rows, :].astype(F32)
        for k in range(1, SECTIONS):
            total = total + part_buf[k, rows, :].astype(F32)
        turned = jnp.transpose(total)
        in_ref[0, family] = turned[0:STATE]
        out_ref[0, family] = turned[STATE:]
        below = FAMILIES * ROWS + family * GROUP
        for k in range(SECTIONS):
            step_ref[0, family, k * GROUP : (k + 1) * GROUP, :] = part_buf[k, below : below + GROUP, :].astype(F32)


def home_grad_kernel(*refs):
    early, late = refs[0:4], refs[4:8]
    grad_ref, grad_buf, grad_sem = refs[8:]
    fetch_home(early, late, lambda source: grad_buf.at[:, :, pl.ds(source * COLS, COLS)], grad_sem)
    out = pltpu.make_async_copy(grad_buf, grad_ref.at[0], grad_sem.at[0])
    out.start()
    out.wait()


def rate_sum_kernel(scale, *refs):
    got_ref, sum_ref = refs[0], refs[-1]
    total = got_ref[0]
    for at in range(1, BRANCHES):
        total = total + got_ref[at]
    sum_ref[...] = jnp.broadcast_to((total * scale)[None], (SECTIONS, 1, LANES))


def rate_home_kernel(got_ref, decay_ref, skip_ref):
    mine = lax.axis_index("section")
    section = (lane_ids((8, LANES)) & (STATE - 1)) >> 4
    total = jnp.zeros((8, LANES), F32)
    for at in range(SECTIONS):
        row = jnp.broadcast_to(got_ref[at], (8, LANES))
        shift = lax.rem(at - mine + SECTIONS, SECTIONS) * GROUP
        ahead, behind = pltpu.roll(row, shift, 1), pltpu.roll(row, shift + STATE, 1)
        low = (lane_ids((8, LANES)) & (STATE - 1)) >= shift
        total = jnp.where(section == at, jnp.where(low, ahead, behind), total)
    decay_ref[...] = total[0:1, 0:STATE]
    skip_ref[...] = total[0:1, STATE:]


VM = pl.BlockSpec(memory_space=pltpu.VMEM)
SM = pl.BlockSpec(memory_space=pltpu.SMEM)
ANY = pl.BlockSpec(memory_space=pl.ANY)
HBM = pl.BlockSpec(memory_space=pltpu.HBM)
PARAMS = pltpu.CompilerParams(vmem_limit_bytes=VMEM_LIMIT)
SMALL_PARAMS = pltpu.CompilerParams(vmem_limit_bytes=32 * 1024 * 1024)


PACKS = pltpu.VMEM((SECTIONS, PACK_ROWS, LANES), F32)


def shape(dims, dtype):
    return jax.ShapeDtypeStruct(dims, dtype)


def cost(flops):
    return pl.CostEstimate(flops=flops, bytes_accessed=4_000_000, transcendentals=0)


def sems(count):
    return pltpu.SemaphoreType.DMA((count,))


def pack_small(state_in, state_out, step_size, decay_rate, skip_gain):
    turned = [jnp.transpose(value, (0, 1, 3, 2)) for value in (state_in, state_out, step_size)]
    return pl.pallas_call(
        pack_kernel,
        out_shape=[shape((PACK_ROWS, LANES), F32)] * SECTIONS,
        in_specs=[ANY] * 3 + [VM] * 2,
        out_specs=[HBM] * SECTIONS,
        scratch_shapes=[
            pltpu.VMEM((FAMILIES, STATE, ROWS), F32),
            pltpu.VMEM((FAMILIES, STATE, ROWS), F32),
            pltpu.VMEM((FAMILIES, SECTIONS * GROUP, ROWS), F32),
            pltpu.VMEM((SECTIONS, PACK_ROWS, LANES), F32),
            pltpu.VMEM((2, SECTIONS * GROUP, LANES), F32),
            sems(3),
            sems(4),
        ],
        compiler_params=PARAMS,
        name="pack_small",
    )(*turned, decay_rate, skip_gain)


def sort_heads(layer_input, saved_states):
    mine = jnp.full((1,), lax.axis_index("section"), jnp.int32)

    def x_spec(k):
        return pl.BlockSpec(
            (1, 1, ROWS, COLS), lambda f, at: (0, f, 0, lax.rem(at[0] + k, SECTIONS))
        )

    def s_spec(k):
        return pl.BlockSpec(
            (1, 1, 1, GROUP, HEADDIM, STATE), lambda f, at: (0, f, 0, lax.rem(at[0] + k, SECTIONS), 0, 0)
        )

    x_out = pl.BlockSpec((1, ROWS, COLS), lambda f, at: (f, 0, 0))
    s_out = pl.BlockSpec((1, COLS // 2, LANES), lambda f, at: (f, 0, 0))
    outs = pl.pallas_call(
        sort_kernel,
        grid_spec=pltpu.PrefetchScalarGridSpec(
            num_scalar_prefetch=1,
            grid=(FAMILIES,),
            in_specs=[x_spec(1), x_spec(2), x_spec(3)] + [s_spec(k) for k in range(SECTIONS)],
            out_specs=[x_out] * 3 + [s_out] * 4,
        ),
        out_shape=[shape((FAMILIES, ROWS, COLS), BF16)] * 3 + [shape((FAMILIES, COLS // 2, LANES), BF16)] * 4,
        compiler_params=PARAMS,
        cost_estimate=cost(4_000_000_000),
        name="sort_heads",
    )(mine, layer_input, layer_input, layer_input, *([saved_states] * 4))
    return outs[:3], outs[3:]


def first_phase(high_at, lengths, cotangent, packs, after):
    return pl.pallas_call(
        functools.partial(first_kernel, high_at, len(after)),
        out_shape=[
            shape((BRANCHES, SEND_ROWS, LANES), BF16),
            shape((FAMILIES, ROWS, COLS), BF16),
        ],
        in_specs=[SM] + [ANY] * (5 + len(after)),
        out_specs=[HBM, HBM],
        scratch_shapes=[
            pltpu.VMEM((FAMILIES, ROWS, COLS), BF16),
            pltpu.VMEM((BRANCHES, SEND_ROWS, LANES), BF16),
            PACKS,
            sems(4),
            sems(4),
        ],
        compiler_params=PARAMS,
        name="first_phase",
    )(lengths, cotangent, *packs, *after)


def later_phase(high_at, goes_on, packs, upstream, ends, after):
    outs = [shape((FAMILIES, ROWS, COLS), BF16)] * 4
    outs += [shape((FAMILIES, ROWS, COLS), BF16)] * 2
    scratch = [
        pltpu.VMEM((2, FAMILIES, ROWS, COLS), BF16),
        pltpu.VMEM((FAMILIES, ROWS, COLS), BF16),
        pltpu.VMEM((BRANCHES, HEADDIM, LANES), BF16),
        PACKS,
        sems(2),
        sems(2),
        sems(2),
        sems(4),
    ]
    if goes_on:
        outs += [shape((BRANCHES, SEND_ROWS, LANES), BF16)]
        scratch += [pltpu.VMEM((BRANCHES, SEND_ROWS, LANES), BF16), sems(2)]
    return pl.pallas_call(
        functools.partial(later_kernel, high_at, goes_on, len(after)),
        out_shape=outs,
        in_specs=[ANY] * (6 + len(after)),
        out_specs=[HBM] * len(outs),
        scratch_shapes=scratch,
        compiler_params=PARAMS,
        name="later_phase",
    )(*packs, upstream, ends, *after)


def other_phase(high_at, sides, packs, ups, ends, layer_input, xs, states, held, smalls, after):
    count = 4 if 1 in sides else 1
    return pl.pallas_call(
        functools.partial(other_kernel, high_at, sides, len(after)),
        out_shape=[shape((GRAD_ROWS, LANES), BF16)] * count
        + [shape((GROUP, LANES), F32) if len(sides) == 1 else shape((BRANCHES, 1, LANES), F32)],
        in_specs=[ANY] * 16 + [VM] * 2 + [ANY] * len(after),
        out_specs=[HBM] * count + [VM],
        scratch_shapes=[
            pltpu.VMEM((2, FAMILIES, ROWS, COLS), BF16),
            pltpu.VMEM((2, FAMILIES, COLS // 2, LANES), BF16),
            pltpu.VMEM((2, FAMILIES, ROWS, COLS), BF16),
            pltpu.VMEM((BRANCHES, HEADDIM, LANES), BF16),
            pltpu.VMEM((2, GRAD_ROWS, LANES), BF16),
            PACKS,
            sems(2),
            sems(2),
            sems(2),
            sems(2),
            sems(1),
            sems(4),
        ],
        compiler_params=PARAMS,
        cost_estimate=cost(6_000_000_000 * len(sides)),
        name="other_phase",
    )(*packs, *ups, ends, layer_input, *xs, *states, held, *smalls, *after)


def chain(got, after):
    return pl.pallas_call(
        chain_kernel,
        out_shape=shape((BRANCHES, HEADDIM, LANES), BF16),
        in_specs=[VM] + [ANY] * len(after),
        out_specs=VM,
        compiler_params=SMALL_PARAMS,
        name="chain",
    )(got, *after)


def home_small(early, late):
    return pl.pallas_call(
        home_small_kernel,
        out_shape=[
            shape((1, FAMILIES, STATE, ROWS), F32),
            shape((1, FAMILIES, STATE, ROWS), F32),
            shape((1, FAMILIES, SECTIONS * GROUP, ROWS), F32),
        ],
        in_specs=[ANY] * 8,
        out_specs=[VM] * 3,
        scratch_shapes=[pltpu.VMEM((SECTIONS, GRAD_ROWS, LANES), BF16), sems(SECTIONS)],
        compiler_params=PARAMS,
        name="home_small",
    )(*early, *late)


def home_grad(early, late):
    return pl.pallas_call(
        home_grad_kernel,
        out_shape=shape((1, FAMILIES, ROWS, SECTIONS * COLS), BF16),
        in_specs=[ANY] * 8,
        out_specs=HBM,
        scratch_shapes=[pltpu.VMEM((FAMILIES, ROWS, SECTIONS * COLS), BF16), sems(SECTIONS)],
        compiler_params=PARAMS,
        cost_estimate=cost(3_000_000_000),
        name="home_grad",
    )(*early, *late)


def rate_sum(got, scale, after):
    return pl.pallas_call(
        functools.partial(rate_sum_kernel, scale),
        out_shape=shape((SECTIONS, 1, LANES), F32),
        in_specs=[VM] + [ANY] * len(after),
        out_specs=VM,
        compiler_params=SMALL_PARAMS,
        name="rate_sum",
    )(got, *after)


def rate_home(got):
    return pl.pallas_call(
        rate_home_kernel,
        out_shape=[shape((1, SECTIONS * GROUP), F32)] * 2,
        in_specs=[VM],
        out_specs=[VM] * 2,
        compiler_params=SMALL_PARAMS,
        name="rate_home",
    )(got)


def swap(value, axis):
    return lax.all_to_all(value, axis, 0, 0, tiled=True)


def send_on(value, k, targets):
    pairs = [(i, (i + k) % SECTIONS) for i in range(SECTIONS) if (i + k) % SECTIONS in targets]
    return lax.ppermute(value, "section", pairs)


def send_home(pieces, targets):
    return [pieces[0]] + [send_on(pieces[k], k, targets) for k in range(1, SECTIONS)]


def exchange(send, after):
    return swap(chain(swap(send, "branch"), after), "branch")


def shards(
    layer_input,
    cotangent,
    state_in,
    state_out,
    step_size,
    saved_states,
    decay_rate,
    skip_gain,
    lengths,
):
    grad_scale = 1.0 / math.sqrt(FAMILIES * ROWS * BRANCHES * HEADDIM)
    everyone = tuple(range(SECTIONS))
    packs = pack_small(state_in, state_out, step_size, decay_rate, skip_gain)
    packs = [packs[0]] + [send_on(packs[k], k, everyone) for k in range(1, SECTIONS)]
    sorted_xs, sorted_states = sort_heads(layer_input, saved_states)
    xs = [send_on(sorted_xs[k - 1], k, everyone) for k in range(1, SECTIONS)]
    states = [sorted_states[0]] + [send_on(sorted_states[k], k, everyone) for k in range(1, SECTIONS)]
    top, upstream = first_phase(3, lengths, cotangent, packs, [sorted_states[0]])
    ends = exchange(top, [])
    early = later_phase(3, True, packs, upstream, ends, xs + states[1:])
    early_grads = send_home(early[:4], (2, 3))
    ups = (upstream, early[4])
    blank = jnp.zeros((GROUP, LANES), F32)
    held, small_a = other_phase(3, (0,), packs, ups, ends, layer_input, xs, states, packs[0], [blank, blank], [])
    got = swap(early[6], "branch")
    next_ends = swap(chain(got, [held]), "branch")
    *early_parts, small_b = other_phase(
        3, (1,), packs, ups, ends, layer_input, xs, states, held, [small_a, small_a], []
    )
    early_parts = send_home(early_parts, (2, 3))
    late = later_phase(1, False, packs, early[5], next_ends, early_grads[1:])
    late_grads = send_home(late[:4], (0, 1))
    ups = (early[5], late[4])
    *late_parts, rates = other_phase(
        1, (0, 1), packs, ups, next_ends, layer_input, xs, states, packs[0], [small_a, small_b], early_parts[1:]
    )
    late_parts = send_home(late_parts, (0, 1))
    others = home_small(early_parts, late_parts)
    rates = rate_sum(swap(rates, "branch"), grad_scale, late_parts[1:])
    rates = rate_home(swap(rates, "section"))
    others = tuple(jnp.transpose(value, (0, 1, 3, 2)) for value in others)
    return (home_grad(early_grads, late_grads),) + others + tuple(rates)


def solution(mesh):
    placed = (
        P("section", None, "branch", None),
        P(None, "branch", None),
        P("section", None, "branch", None),
        P("section", None, "branch", None),
        P("section", None, "branch", None),
        P("section", None, "branch", None, None, None),
        P("section", None),
        P("section", None),
        P(),
    )
    return jax.shard_map(
        shards,
        mesh=mesh,
        in_specs=placed,
        out_specs=(
            P("section", None, "branch", None),
            P("section", None, "branch", None),
            P("section", None, "branch", None),
            P("section", None, "branch", None),
            P("section", None),
            P("section", None),
        ),
        check_vma=False,
    )
```

```python
import functools
import math

import jax
import jax.numpy as jnp
from jax import lax
from jax.experimental import pallas as pl
from jax.experimental.pallas import tpu as pltpu
from jax.sharding import PartitionSpec as P

F32 = jnp.float32
BF16 = jnp.bfloat16

SECTIONS = 4
FAMILIES = 2
ROWS = 128
STATE = 64
HEADDIM = 64
GROUP = 16
COLS = GROUP * HEADDIM
LANES = 128
CHUNK = 256
PER_CHUNK = CHUNK // HEADDIM
BRANCHES = 32
SEND_ROWS = 112
PACK_ROWS = FAMILIES * ROWS + 4 * GROUP
GRAD_ROWS = FAMILIES * (ROWS + GROUP)
HOME_ROWS = GRAD_ROWS + 16
SAVED_ROWS = COLS + COLS // 2
VMEM_LIMIT = 63 * 1024 * 1024

NN = (((1,), (0,)), ((), ()))
NT = (((1,), (1,)), ((), ()))
TN = (((0,), (0,)), ((), ()))


def dot(a, b, dims):
    return lax.dot_general(a, b, dims, preferred_element_type=F32)


def split(a):
    high = a.astype(BF16)
    return high, (a - high.astype(F32)).astype(BF16)


def dot3(a, b, dims):
    return dot(a[0], b[0], dims) + dot(a[1], b[0], dims) + dot(a[0], b[1], dims)


def dot2(a, b, dims):
    return dot(a[0], b, dims) + dot(a[1], b, dims)


def lane_ids(shape):
    return lax.broadcasted_iota(jnp.int32, shape, len(shape) - 1)


def half(rolled, plain, side):
    lanes = lane_ids(plain.shape)
    if side == 0:
        return jnp.where(lanes < STATE, plain, 0.0)
    return jnp.where(lanes >= STATE, rolled, 0.0)


def by_head(value, chunk):
    first = chunk * PER_CHUNK
    return jnp.concatenate(
        [jnp.broadcast_to(value[first + at : first + at + 1, :], (HEADDIM, LANES)) for at in range(PER_CHUNK)], axis=0
    )


def head_sums(value):
    return jnp.sum(value.reshape(PER_CHUNK, HEADDIM, LANES), axis=1)


def fetch_packs(layers, pack_refs, pack_buf, sems):
    mine = lax.axis_index("section")
    for at in layers:
        away = lax.rem(mine - at + SECTIONS, SECTIONS)
        for k in range(SECTIONS):

            @pl.when(away == k)
            def _():
                pltpu.make_async_copy(pack_refs[k], pack_buf.at[at], sems.at[at]).start()


def wait_packs(layers, pack_refs, pack_buf, sems):
    for at in layers:
        pltpu.make_async_copy(pack_refs[0], pack_buf.at[at], sems.at[at]).wait()


class Layer:
    def __init__(self, pack_ref, layer, family):
        base = FAMILIES * ROWS
        both = pack_ref[layer, family * ROWS : (family + 1) * ROWS, :]
        turned = pltpu.roll(both, STATE, 1)
        self.b = (half(both, both, 0), half(turned, turned, 1))
        self.c = (half(turned, turned, 0), half(both, both, 1))
        self.step = pack_ref[layer, base + family * GROUP : base + (family + 1) * GROUP, :]
        self.decay = pack_ref[layer, base + 2 * GROUP : base + 3 * GROUP, :]
        gain = pack_ref[layer, base + 3 * GROUP : base + 4 * GROUP, :]
        row = lax.broadcasted_iota(jnp.int32, (ROWS, ROWS), 0)
        col = lax.broadcasted_iota(jnp.int32, (ROWS, ROWS), 1)
        self.row, self.col = row, col
        upper = jnp.where(row <= col, 1.0, 0.0).astype(BF16)
        drop = -self.decay * self.step
        first = drop.astype(BF16)
        rest = drop - first.astype(F32)
        second = rest.astype(BF16)
        third = (rest - second.astype(F32)).astype(BF16)
        logs = dot(first, upper, NN) + dot(second, upper, NN) + dot(third, upper, NN)
        carried = jnp.exp(logs)
        scale = self.step * jnp.exp(-logs)
        total = jnp.sum(jnp.where(lane_ids(carried.shape) == ROWS - 1, carried, 0.0), axis=1, keepdims=True)
        self.total = jnp.broadcast_to(total, (GROUP, LANES))
        self.carried, self.scale, self.gain = carried, scale, gain
        read = dot3(split(self.c[0]), split(self.b[0]), NT)
        self.read = jnp.where(row >= col, read, 0.0)


def phase_a(family, upper_at, high, low, send_ref):
    c_pair = split(jnp.concatenate([high.c[0], low.c[1]], axis=0))
    c_both = split(low.c[0] + low.c[1])
    b_turned = jnp.transpose(high.b[0])[0:STATE]
    b_tile = jnp.concatenate([b_turned] * PER_CHUNK, axis=0)
    read = high.read.astype(BF16)
    mixed = low.carried * high.scale
    lanes = lane_ids((STATE // 2, LANES))
    for chunk in range(COLS // CHUNK):
        rows = slice(chunk * CHUNK, (chunk + 1) * CHUNK)
        upstream = upper_at(rows)
        hat2 = split(by_head(high.carried, chunk) * upstream)
        pulled = dot(hat2[0], read, NN)
        low_up = by_head(high.gain, chunk) * upstream + by_head(high.scale, chunk) * pulled
        low_hat2 = split(by_head(low.carried, chunk) * low_up)
        both = tuple(jnp.concatenate([a, b], axis=1) for a, b in zip(hat2, low_hat2))
        begin = dot3(both, c_pair, NN).astype(BF16)
        move = dot3(split(by_head(mixed, chunk) * b_tile), c_both, NN)
        for inner in range(PER_CHUNK):
            head = family * GROUP + chunk * PER_CHUNK + inner
            top = inner * HEADDIM
            send_ref[head, 0:HEADDIM, :] = begin[top : top + HEADDIM, :]
            first = move[top : top + 32, :]
            second = move[top + 32 : top + 64, :]
            send_ref[head, HEADDIM : HEADDIM + 32, :] = jnp.where(lanes < STATE, first, second).astype(BF16)
    totals = jnp.where(lane_ids((GROUP, LANES)) < STATE, high.total, low.total)
    total_high = totals.astype(BF16).astype(F32)
    total_low = totals - total_high
    place = lax.broadcasted_iota(jnp.int32, (16, LANES), 0)
    for inner in range(GROUP):
        one = jnp.broadcast_to(total_high[inner : inner + 1, :], (16, LANES))
        two = jnp.broadcast_to(total_low[inner : inner + 1, :], (16, LANES))
        block = jnp.where(place == 0, one, jnp.where(place == 1, two, 0.0))
        send_ref[family * GROUP + inner, 96:112, :] = block.astype(BF16)


def phase_b(family, side, layer, upper_at, end_ref, put_grad):
    b2 = split(jnp.transpose(layer.b[side]))
    weights = jnp.concatenate([layer.read.astype(BF16), b2[0]], axis=0)
    for chunk in range(COLS // CHUNK):
        rows = slice(chunk * CHUNK, (chunk + 1) * CHUNK)
        upstream = upper_at(rows)
        first = family * GROUP + chunk * PER_CHUNK
        ends = end_ref[first : first + PER_CHUNK].reshape(CHUNK, LANES)
        hat = (by_head(layer.carried, chunk) * upstream).astype(BF16)
        pulled = dot(jnp.concatenate([hat, ends], axis=1), weights, NN) + dot(ends, b2[1], NN)
        grad = by_head(layer.gain, chunk) * upstream + by_head(layer.scale, chunk) * pulled
        put_grad(rows, grad.astype(BF16))


def phase_c(family, side, layer, upper_at, saved_ref, end_ref):
    b_one, c_one = layer.b[side].astype(BF16), layer.c[side].astype(BF16)
    b_turned = jnp.transpose(layer.b[side]).astype(BF16)
    read = layer.read.astype(BF16)
    weights = jnp.concatenate([jnp.transpose(layer.read), jnp.transpose(layer.c[side])], axis=0).astype(BF16)
    left = jnp.zeros((ROWS, ROWS + LANES), F32)
    grad_in = jnp.zeros((ROWS, LANES), F32)
    flow, worth, ending, skips = [], [], [], []
    lanes = lane_ids((CHUNK, LANES))
    for chunk in range(COLS // CHUNK):
        rows = slice(chunk * CHUNK, (chunk + 1) * CHUNK)
        upstream = upper_at(rows)
        x = saved_ref[family, rows, :].astype(F32)
        hat = by_head(layer.carried, chunk) * upstream
        hat_one = hat.astype(BF16)
        x_hat = by_head(layer.scale, chunk) * x
        x_one = x_hat.astype(BF16)
        first = family * GROUP + chunk * PER_CHUNK
        ends = end_ref[first : first + PER_CHUNK].reshape(CHUNK, LANES)
        top = COLS + (chunk % 2) * CHUNK
        packed = saved_ref[family, top : top + CHUNK, :].astype(F32)
        if (chunk < 2) != (side == 0):
            packed = pltpu.roll(packed, STATE, 1)
        saved = jnp.where((lanes < STATE) == (side == 0), packed, 0.0)
        x_saved = jnp.concatenate([x_one, saved.astype(BF16)], axis=1)
        end_in = dot(ends, b_turned, NN)
        pulled = dot(hat_one, read, NN) + end_in
        forward = dot(x_saved, weights, NN)
        left = left + dot(hat_one, x_saved, TN)
        grad_in = grad_in + dot(x_one, ends, TN)
        x_pulled = x_hat * pulled
        worth.append(head_sums(x_pulled))
        flow.append(head_sums(hat * forward - x_pulled))
        ending.append(head_sums(x_hat * end_in + ends.astype(F32) * saved))
        skips.append(head_sums(x * upstream))
    flow, worth, ending, skips = (jnp.concatenate(part, axis=0) for part in (flow, worth, ending, skips))
    pairs, grad_out = left[:, 0:ROWS], left[:, ROWS:]
    pairs = jnp.where(layer.row >= layer.col, pairs, 0.0).astype(BF16)
    grad_out = grad_out + dot(pairs, b_one, NN)
    grad_in = grad_in + dot(pairs, c_one, TN)
    lanes = lane_ids((ROWS, LANES))
    if side == 0:
        grads = jnp.where(lanes < STATE, grad_in, pltpu.roll(grad_out, STATE, 1))
    else:
        grads = jnp.where(lanes < STATE, pltpu.roll(grad_in, STATE, 1), grad_out)
    later = jnp.where(layer.row >= layer.col, 1.0, 0.0).astype(BF16)
    rate = dot2(split(flow), later, NN) + jnp.sum(ending, axis=1, keepdims=True)
    grad_step = worth / layer.step - layer.decay * rate
    decay_part = jnp.sum(-layer.step * rate, axis=1, keepdims=True)
    skip_part = jnp.sum(skips, axis=1, keepdims=True)
    place = lane_ids((GROUP, LANES))
    small = jnp.where(place == 0, decay_part, jnp.where(place == 1, skip_part, 0.0))
    return grads, grad_step, small


def first_kernel(high_at, after, *refs):
    lengths_ref, cot_ref = refs[:2]
    pack_refs = refs[2:6]
    send_ref, up_ref, cot_buf, up_buf, send_buf, pack_ref, sems, pack_sem = refs[6 + after :]
    layers = (high_at, high_at - 1)
    fetch_packs(layers, pack_refs, pack_ref, pack_sem)
    mine = lax.axis_index("section")
    branch = lax.axis_index("branch")
    at = pl.multiple_of(mine * COLS, COLS)
    copy = pltpu.make_async_copy(cot_ref.at[:, :, pl.ds(at, COLS)], cot_buf, sems.at[3])
    copy.start()
    wait_packs(layers, pack_refs, pack_ref, pack_sem)
    copy.wait()
    copies = []
    for family in range(FAMILIES):
        slot = jnp.clip(branch - BRANCHES // 2, 0, BRANCHES // 2 - 1)
        limit = jnp.where(branch >= BRANCHES // 2, lengths_ref[family, slot], ROWS)

        def upper_at(rows):
            at = lane_ids((CHUNK, ROWS))
            value = jnp.where(at < limit, jnp.transpose(cot_buf[family, :, rows].astype(F32)), 0.0)
            up_buf[family, rows, :] = value.astype(BF16)
            return value

        high = Layer(pack_ref, high_at, family)
        low = Layer(pack_ref, high_at - 1, family)
        phase_a(family, upper_at, high, low, send_buf)
        heads = pl.ds(family * GROUP, GROUP)
        copies.append(pltpu.make_async_copy(send_buf.at[heads], send_ref.at[heads], sems.at[family]))
        copies[-1].start()
    copies.append(pltpu.make_async_copy(up_buf, up_ref, sems.at[2]))
    copies[-1].start()
    for copy in copies:
        copy.wait()


def later_kernel(high_at, goes_on, after, *refs):
    pack_refs = refs[:4]
    up_ref, end_ref = refs[4:6]
    refs = refs[6 + after :]
    grad_refs, keep_refs = refs[0:4], refs[4:6]
    rest = refs[6:]
    if goes_on:
        send_ref, grad_buf, up_buf, end_buf, pack_ref, grad_sem, keep_sem, in_sem, pack_sem, send_buf, send_sem = rest
    else:
        grad_buf, up_buf, end_buf, pack_ref, grad_sem, keep_sem, in_sem, pack_sem = rest
    layers = range(high_at, high_at - (4 if goes_on else 2), -1)
    fetch_packs(layers[:2], pack_refs, pack_ref, pack_sem)
    ins = [
        pltpu.make_async_copy(up_ref, up_buf, in_sem.at[0]),
        pltpu.make_async_copy(end_ref, end_buf, in_sem.at[1]),
    ]
    for copy in ins:
        copy.start()
    fetch_packs(layers[2:], pack_refs, pack_ref, pack_sem)
    mine = lax.axis_index("section")
    wait_packs(layers[:2], pack_refs, pack_ref, pack_sem)
    for copy in ins:
        copy.wait()
    for side in range(2):
        layer_at = high_at - side
        for family in range(FAMILIES):

            def upper_at(rows):
                if side == 0:
                    return up_buf[family, rows, :].astype(F32)
                return grad_buf[0, family, rows, :].astype(F32)

            def put_grad(rows, value):
                grad_buf[side, family, rows, :] = value

            layer = Layer(pack_ref, layer_at, family)
            phase_b(family, side, layer, upper_at, end_buf, put_grad)
        ahead = lax.rem(layer_at - mine + SECTIONS, SECTIONS)
        for k in range(SECTIONS):

            @pl.when(ahead == k)
            def _():
                pltpu.make_async_copy(grad_buf.at[side], grad_refs[k], grad_sem.at[side]).start()

    copies = [pltpu.make_async_copy(grad_buf.at[side], keep_refs[side], keep_sem.at[side]) for side in range(2)]
    for copy in copies:
        copy.start()
    if goes_on:
        wait_packs(layers[2:], pack_refs, pack_ref, pack_sem)
        for family in range(FAMILIES):

            def upper_at(rows):
                return grad_buf[1, family, rows, :].astype(F32)

            high = Layer(pack_ref, high_at - 2, family)
            low = Layer(pack_ref, high_at - 3, family)
            phase_a(family, upper_at, high, low, send_buf)
            heads = pl.ds(family * GROUP, GROUP)
            copies.append(pltpu.make_async_copy(send_buf.at[heads], send_ref.at[heads], send_sem.at[family]))
            copies[-1].start()
    for copy in copies:
        copy.wait()
    for side in range(2):
        pltpu.make_async_copy(grad_buf.at[side], grad_refs[0], grad_sem.at[side]).wait()


def other_kernel(high_at, sides, after, *refs):
    pack_refs, up_refs, end_ref, saved_refs = refs[:4], refs[4:6], refs[6], refs[7:11]
    refs = refs[11:]
    final = len(sides) == 2
    if final:
        held_refs, small_refs, refs = refs[0:2], refs[2:4], refs[4:]
    refs = refs[after:]
    part_refs, refs = (refs[:4], refs[4:]) if final else (refs[:1], refs[1:])
    rate_ref, saved_buf, up_buf, end_buf, part_buf, pack_ref = refs[:6]
    saved_sem, up_sem, part_sem, end_sem, pack_sem = refs[6:]
    mine = lax.axis_index("section")
    layers = [high_at - side for side in sides]
    fetch_packs(layers, pack_refs, pack_ref, pack_sem)
    ends = pltpu.make_async_copy(end_ref, end_buf, end_sem.at[0])
    ends.start()
    for side in sides:
        away = lax.rem(mine - (high_at - side) + SECTIONS, SECTIONS)
        pltpu.make_async_copy(up_refs[side], up_buf.at[side], up_sem.at[side]).start()
        for k in range(SECTIONS):

            @pl.when(away == k)
            def _():
                pltpu.make_async_copy(saved_refs[k], saved_buf.at[side], saved_sem.at[side]).start()

    def hand_on(source, layer_at):
        to = [part.at[pl.ds(0, GRAD_ROWS)] for part in part_refs] if final else part_refs
        copies = [pltpu.make_async_copy(source, part, part_sem.at[layer_at]) for part in to]
        if final:
            ahead = lax.rem(layer_at - mine + SECTIONS, SECTIONS)
            for k in range(SECTIONS):

                @pl.when(ahead == k)
                def _():
                    copies[k].start()
        else:
            copies[0].start()
        moved.append(copies[0])

    moved = []
    if final:
        for side in range(2):
            hand_on(held_refs[side], high_at + 2 - side)
    wait_packs(layers, pack_refs, pack_ref, pack_sem)
    ends.wait()
    smalls_of = []
    for side in sides:
        pltpu.make_async_copy(up_refs[side], up_buf.at[side], up_sem.at[side]).wait()
        pltpu.make_async_copy(saved_refs[0], saved_buf.at[side], saved_sem.at[side]).wait()
        smalls = jnp.zeros((GROUP, LANES), F32)
        for family in range(FAMILIES):

            def upper_at(rows):
                return up_buf[side, family, rows, :].astype(F32)

            layer = Layer(pack_ref, high_at - side, family)
            grads, grad_step, small = phase_c(family, side, layer, upper_at, saved_buf.at[side], end_buf)
            part_buf[side, family * ROWS : (family + 1) * ROWS, :] = grads.astype(BF16)
            below = FAMILIES * ROWS + family * GROUP
            part_buf[side, below : below + GROUP, :] = grad_step.astype(BF16)
            smalls = smalls + small
        hand_on(part_buf.at[side], high_at - side)
        smalls_of.append(smalls)
    if final:
        blocks = smalls_of[::-1] + [small_refs[1][...], small_refs[0][...]]
        turned = jnp.transpose(jnp.concatenate(blocks + [jnp.zeros((STATE, LANES), F32)], axis=0))
        row = turned[0:1] + pltpu.roll(turned[1:2], STATE, 1)
        rate_ref[...] = jnp.broadcast_to(row[None], (BRANCHES, 1, LANES))
    else:
        rate_ref[...] = smalls_of[0]
    for copy in moved:
        copy.wait()


def chain_kernel(*refs):
    got_ref, end_ref = refs[0], refs[-1]
    lanes = lane_ids((STATE // 2, LANES))
    prompt = BRANCHES // 2
    fork = jnp.zeros((HEADDIM, LANES), F32)
    for at in range(prompt, BRANCHES):
        fork = fork + got_ref[at, 0:HEADDIM, :].astype(F32)
    plain, extra = fork, jnp.zeros((HEADDIM, LANES), F32)
    blank = jnp.zeros((STATE, LANES), F32)
    for at in range(prompt - 1, -1, -1):
        tail = got_ref[at, 96:112, :].astype(F32)
        total = tail[0:1, :] + tail[1:2, :]
        plain = total * plain
        extra = total * extra
        end_ref[at, :, :] = (plain + extra).astype(BF16)
        if at == 0:
            break
        packed = got_ref[at, HEADDIM : HEADDIM + 32, :].astype(F32)
        turned = pltpu.roll(packed, STATE, 1)
        move = jnp.concatenate(
            [jnp.where(lanes >= STATE, turned, 0.0), jnp.where(lanes >= STATE, packed, 0.0), blank], axis=0
        ).astype(BF16)
        extra = extra + dot2(split(plain), move, NN)
        plain = plain + got_ref[at, 0:HEADDIM, :].astype(F32)
    for at in range(prompt, BRANCHES):
        end_ref[at, :, :] = jnp.zeros((HEADDIM, LANES), BF16)


def pack_kernel(*refs):
    sources, decay_ref, gain_ref = refs[0:3], refs[3], refs[4]
    pack_refs = refs[5:9]
    in_ref, out_ref, step_ref, both_ref, rate_ref, sems, send_sems = refs[9:]
    copies = [
        pltpu.make_async_copy(source.at[0], to, sems.at[at])
        for at, (source, to) in enumerate(zip(sources, (in_ref, out_ref, step_ref)))
    ]
    for copy in copies:
        copy.start()
    mine = lax.axis_index("section")
    base = FAMILIES * ROWS
    rate_ref[0] = jnp.transpose(jnp.broadcast_to(decay_ref[...], (LANES, SECTIONS * GROUP)))
    rate_ref[1] = jnp.transpose(jnp.broadcast_to(gain_ref[...], (LANES, SECTIONS * GROUP)))
    for copy in copies:
        copy.wait()
    for k in range(SECTIONS):
        heads = pl.ds(pl.multiple_of(lax.rem(mine + k, SECTIONS) * GROUP, GROUP), GROUP)
        for family in range(FAMILIES):
            both_ref[k, base + family * GROUP : base + (family + 1) * GROUP, :] = step_ref[family, heads, :]
        both_ref[k, base + 2 * GROUP : base + 3 * GROUP, :] = rate_ref[0, heads, :]
        both_ref[k, base + 3 * GROUP : base + 4 * GROUP, :] = rate_ref[1, heads, :]
    for family in range(FAMILIES):
        turned = jnp.transpose(jnp.concatenate([in_ref[family], out_ref[family]], axis=0))
        for k in range(SECTIONS):
            both_ref[k, family * ROWS : (family + 1) * ROWS, :] = turned
    copies = []
    for k in range(SECTIONS):
        copies.append(pltpu.make_async_copy(both_ref.at[k], pack_refs[k], send_sems.at[k]))
        copies[-1].start()
    for copy in copies:
        copy.wait()


def sort_kernel(at_ref, *refs):
    for x_ref, s_ref, o_ref in zip(refs[0:4], refs[4:8], refs[8:12]):
        o_ref[0, 0:COLS] = jnp.transpose(x_ref[0, 0])
        whole = s_ref[0, 0, 0].reshape(COLS, STATE)
        o_ref[0, COLS:SAVED_ROWS] = jnp.concatenate([whole[: COLS // 2], whole[COLS // 2 :]], axis=1).astype(BF16)


def fetch_home(early, late, to, sems):
    mine = lax.axis_index("section")
    for is_early, pieces in ((True, early), (False, late)):

        @pl.when((mine >= 2) == is_early)
        def _():
            for k in range(SECTIONS):
                source = lax.rem(mine - k + SECTIONS, SECTIONS)
                pltpu.make_async_copy(pieces[k], to(source), sems.at[k]).start()

    for k in range(SECTIONS):
        pltpu.make_async_copy(early[k], to(k), sems.at[k]).wait()


def home_small_kernel(*refs):
    piece_refs = refs[:4]
    in_ref, out_ref, step_ref, decay_ref, skip_ref, part_ref, part_sem = refs[4:]
    mine = lax.axis_index("section")
    for k in range(SECTIONS):
        source = lax.rem(mine - k + SECTIONS, SECTIONS)
        pltpu.make_async_copy(piece_refs[k], part_ref.at[source], part_sem.at[k]).start()
    for k in range(SECTIONS):
        pltpu.make_async_copy(piece_refs[k], part_ref.at[k], part_sem.at[k]).wait()
    for family in range(FAMILIES):
        rows = slice(family * ROWS, (family + 1) * ROWS)
        total = part_ref[0, rows, :].astype(F32)
        for k in range(1, SECTIONS):
            total = total + part_ref[k, rows, :].astype(F32)
        turned = jnp.transpose(total)
        in_ref[0, family] = turned[0:STATE]
        out_ref[0, family] = turned[STATE:]
        below = FAMILIES * ROWS + family * GROUP
        for k in range(SECTIONS):
            step_ref[0, family, k * GROUP : (k + 1) * GROUP, :] = part_ref[k, below : below + GROUP, :].astype(F32)
    section = (lane_ids((8, LANES)) & (STATE - 1)) >> 4
    total = jnp.zeros((8, LANES), F32)
    for at in range(SECTIONS):
        tail = part_ref[at, GRAD_ROWS:HOME_ROWS, :].astype(F32)
        row = jnp.broadcast_to(tail[0:1] + tail[1:2], (8, LANES))
        shift = lax.rem(at - mine + SECTIONS, SECTIONS) * GROUP
        ahead, behind = pltpu.roll(row, shift, 1), pltpu.roll(row, shift + STATE, 1)
        low = (lane_ids((8, LANES)) & (STATE - 1)) >= shift
        total = jnp.where(section == at, jnp.where(low, ahead, behind), total)
    decay_ref[...] = total[0:1, 0:STATE]
    skip_ref[...] = total[0:1, STATE:]


def home_grad_kernel(*refs):
    early, late = refs[0:4], refs[4:8]
    grad_ref, turned_buf, grad_buf, grad_sem, out_sem = refs[8:]
    fetch_home(early, late, lambda source: turned_buf.at[source], grad_sem)
    outs = []
    for source in range(SECTIONS):
        cols = slice(source * COLS, (source + 1) * COLS)
        for family in range(FAMILIES):
            grad_buf[family, :, cols] = jnp.transpose(turned_buf[source, family])
        outs.append(
            pltpu.make_async_copy(
                grad_buf.at[:, :, pl.ds(source * COLS, COLS)],
                grad_ref.at[0, :, :, pl.ds(source * COLS, COLS)],
                out_sem.at[source],
            )
        )
        outs[-1].start()
    for out in outs:
        out.wait()


def rate_sum_kernel(scale, *refs):
    got_ref, part_refs, buf, sems = refs[0], refs[5:9], refs[9], refs[10]
    total = got_ref[0]
    for at in range(1, BRANCHES):
        total = total + got_ref[at]
    total = jnp.broadcast_to(total * scale, (16, LANES))
    high = total.astype(BF16).astype(F32)
    place = lax.broadcasted_iota(jnp.int32, (16, LANES), 0)
    buf[...] = jnp.where(place == 0, high, jnp.where(place == 1, total - high, 0.0)).astype(BF16)
    copies = [
        pltpu.make_async_copy(buf, part_refs[to].at[pl.ds(GRAD_ROWS, 16)], sems.at[to]) for to in range(SECTIONS)
    ]
    for copy in copies:
        copy.start()
    for copy in copies:
        copy.wait()


VM = pl.BlockSpec(memory_space=pltpu.VMEM)
SM = pl.BlockSpec(memory_space=pltpu.SMEM)
ANY = pl.BlockSpec(memory_space=pl.ANY)
HBM = pl.BlockSpec(memory_space=pltpu.HBM)
PARAMS = pltpu.CompilerParams(vmem_limit_bytes=VMEM_LIMIT)
SMALL_PARAMS = pltpu.CompilerParams(vmem_limit_bytes=32 * 1024 * 1024)


PACKS = pltpu.VMEM((SECTIONS, PACK_ROWS, LANES), F32)


def shape(dims, dtype):
    return jax.ShapeDtypeStruct(dims, dtype)


def cost(flops):
    return pl.CostEstimate(flops=flops, bytes_accessed=4_000_000, transcendentals=0)


def sems(count):
    return pltpu.SemaphoreType.DMA((count,))


def pack_small(state_in, state_out, step_size, decay_rate, skip_gain):
    turned = [jnp.transpose(value, (0, 1, 3, 2)) for value in (state_in, state_out, step_size)]
    return pl.pallas_call(
        pack_kernel,
        out_shape=[shape((PACK_ROWS, LANES), F32)] * SECTIONS,
        in_specs=[ANY] * 3 + [VM] * 2,
        out_specs=[HBM] * SECTIONS,
        scratch_shapes=[
            pltpu.VMEM((FAMILIES, STATE, ROWS), F32),
            pltpu.VMEM((FAMILIES, STATE, ROWS), F32),
            pltpu.VMEM((FAMILIES, SECTIONS * GROUP, ROWS), F32),
            pltpu.VMEM((SECTIONS, PACK_ROWS, LANES), F32),
            pltpu.VMEM((2, SECTIONS * GROUP, LANES), F32),
            sems(3),
            sems(4),
        ],
        compiler_params=PARAMS,
        name="pack_small",
    )(*turned, decay_rate, skip_gain)


def sort_heads(layer_input, saved_states):
    mine = jnp.full((1,), lax.axis_index("section"), jnp.int32)

    def x_spec(k):
        return pl.BlockSpec(
            (1, 1, ROWS, COLS), lambda f, at: (0, f, 0, lax.rem(at[0] + k, SECTIONS))
        )

    def s_spec(k):
        return pl.BlockSpec(
            (1, 1, 1, GROUP, HEADDIM, STATE), lambda f, at: (0, f, 0, lax.rem(at[0] + k, SECTIONS), 0, 0)
        )

    return pl.pallas_call(
        sort_kernel,
        grid_spec=pltpu.PrefetchScalarGridSpec(
            num_scalar_prefetch=1,
            grid=(FAMILIES,),
            in_specs=[x_spec(k) for k in range(SECTIONS)] + [s_spec(k) for k in range(SECTIONS)],
            out_specs=[pl.BlockSpec((1, SAVED_ROWS, LANES), lambda f, at: (f, 0, 0))] * SECTIONS,
        ),
        out_shape=[shape((FAMILIES, SAVED_ROWS, LANES), BF16)] * SECTIONS,
        compiler_params=PARAMS,
        cost_estimate=cost(4_000_000_000),
        name="sort_heads",
    )(mine, *([layer_input] * SECTIONS), *([saved_states] * SECTIONS))


def first_phase(high_at, lengths, cotangent, packs, after):
    return pl.pallas_call(
        functools.partial(first_kernel, high_at, len(after)),
        out_shape=[
            shape((BRANCHES, SEND_ROWS, LANES), BF16),
            shape((FAMILIES, COLS, ROWS), BF16),
        ],
        in_specs=[SM] + [ANY] * (5 + len(after)),
        out_specs=[HBM, HBM],
        scratch_shapes=[
            pltpu.VMEM((FAMILIES, ROWS, COLS), BF16),
            pltpu.VMEM((FAMILIES, COLS, ROWS), BF16),
            pltpu.VMEM((BRANCHES, SEND_ROWS, LANES), BF16),
            PACKS,
            sems(4),
            sems(4),
        ],
        compiler_params=PARAMS,
        name="first_phase",
    )(lengths, cotangent, *packs, *after)


def later_phase(high_at, goes_on, packs, upstream, ends, after):
    outs = [shape((FAMILIES, COLS, ROWS), BF16)] * 4
    outs += [shape((FAMILIES, COLS, ROWS), BF16)] * 2
    scratch = [
        pltpu.VMEM((2, FAMILIES, COLS, ROWS), BF16),
        pltpu.VMEM((FAMILIES, COLS, ROWS), BF16),
        pltpu.VMEM((BRANCHES, HEADDIM, LANES), BF16),
        PACKS,
        sems(2),
        sems(2),
        sems(2),
        sems(4),
    ]
    if goes_on:
        outs += [shape((BRANCHES, SEND_ROWS, LANES), BF16)]
        scratch += [pltpu.VMEM((BRANCHES, SEND_ROWS, LANES), BF16), sems(2)]
    return pl.pallas_call(
        functools.partial(later_kernel, high_at, goes_on, len(after)),
        out_shape=outs,
        in_specs=[ANY] * (6 + len(after)),
        out_specs=[HBM] * len(outs),
        scratch_shapes=scratch,
        compiler_params=PARAMS,
        name="later_phase",
    )(*packs, upstream, ends, *after)


def other_phase(high_at, sides, packs, ups, ends, saved, held, after):
    final = len(sides) == 2
    if final:
        outs = [shape((HOME_ROWS, LANES), BF16)] * SECTIONS + [shape((BRANCHES, 1, LANES), F32)]
    else:
        outs = [shape((GRAD_ROWS, LANES), BF16), shape((GROUP, LANES), F32)]
    return pl.pallas_call(
        functools.partial(other_kernel, high_at, sides, len(after)),
        out_shape=outs,
        in_specs=[ANY] * 11 + ([ANY, ANY, VM, VM] if final else []) + [ANY] * len(after),
        out_specs=[HBM] * (len(outs) - 1) + [VM],
        scratch_shapes=[
            pltpu.VMEM((2, FAMILIES, SAVED_ROWS, LANES), BF16),
            pltpu.VMEM((2, FAMILIES, COLS, ROWS), BF16),
            pltpu.VMEM((BRANCHES, HEADDIM, LANES), BF16),
            pltpu.VMEM((2, GRAD_ROWS, LANES), BF16),
            PACKS,
            sems(2),
            sems(2),
            sems(4),
            sems(1),
            sems(4),
        ],
        compiler_params=PARAMS,
        cost_estimate=cost(6_000_000_000 * len(sides)),
        name="other_phase",
    )(*packs, *ups, ends, *saved, *held, *after)


def chain(got, after):
    return pl.pallas_call(
        chain_kernel,
        out_shape=shape((BRANCHES, HEADDIM, LANES), BF16),
        in_specs=[VM] + [ANY] * len(after),
        out_specs=VM,
        compiler_params=SMALL_PARAMS,
        name="chain",
    )(got, *after)


def home_small(parts):
    return pl.pallas_call(
        home_small_kernel,
        out_shape=[
            shape((1, FAMILIES, STATE, ROWS), F32),
            shape((1, FAMILIES, STATE, ROWS), F32),
            shape((1, FAMILIES, SECTIONS * GROUP, ROWS), F32),
            shape((1, SECTIONS * GROUP), F32),
            shape((1, SECTIONS * GROUP), F32),
        ],
        in_specs=[ANY] * 4,
        out_specs=[VM] * 5,
        scratch_shapes=[pltpu.VMEM((SECTIONS, HOME_ROWS, LANES), BF16), sems(SECTIONS)],
        compiler_params=PARAMS,
        name="home_small",
    )(*parts)


def home_grad(early, late):
    return pl.pallas_call(
        home_grad_kernel,
        out_shape=shape((1, FAMILIES, ROWS, SECTIONS * COLS), BF16),
        in_specs=[ANY] * 8,
        out_specs=HBM,
        scratch_shapes=[
            pltpu.VMEM((SECTIONS, FAMILIES, COLS, ROWS), BF16),
            pltpu.VMEM((FAMILIES, ROWS, SECTIONS * COLS), BF16),
            sems(SECTIONS),
            sems(SECTIONS),
        ],
        compiler_params=PARAMS,
        cost_estimate=cost(3_000_000_000),
        name="home_grad",
    )(*early, *late)


def rate_sum(got, parts, scale):
    return pl.pallas_call(
        functools.partial(rate_sum_kernel, scale),
        out_shape=[shape((HOME_ROWS, LANES), BF16)] * SECTIONS,
        in_specs=[VM] + [HBM] * SECTIONS,
        out_specs=[HBM] * SECTIONS,
        scratch_shapes=[pltpu.VMEM((16, LANES), BF16), sems(SECTIONS)],
        input_output_aliases={1 + k: k for k in range(SECTIONS)},
        compiler_params=PARAMS,
        name="rate_sum",
    )(got, *parts)


def swap(value, axis):
    return lax.all_to_all(value, axis, 0, 0, tiled=True)


def send_on(value, k, targets):
    pairs = [(i, (i + k) % SECTIONS) for i in range(SECTIONS) if (i + k) % SECTIONS in targets]
    return lax.ppermute(value, "section", pairs)


def send_home(pieces, targets):
    return [pieces[0]] + [send_on(pieces[k], k, targets) for k in range(1, SECTIONS)]


def exchange(send, after):
    return swap(chain(swap(send, "branch"), after), "branch")


def shards(
    layer_input,
    cotangent,
    state_in,
    state_out,
    step_size,
    saved_states,
    decay_rate,
    skip_gain,
    lengths,
):
    grad_scale = 1.0 / math.sqrt(FAMILIES * ROWS * BRANCHES * HEADDIM)
    everyone = tuple(range(SECTIONS))
    packs = pack_small(state_in, state_out, step_size, decay_rate, skip_gain)
    packs = [packs[0]] + [send_on(packs[k], k, everyone) for k in range(1, SECTIONS)]
    saved = sort_heads(layer_input, saved_states)
    top, upstream = first_phase(3, lengths, cotangent, packs, [saved[0]])
    saved = [saved[0]] + [send_on(saved[k], k, everyone) for k in range(1, SECTIONS)]
    ends = exchange(top, [])
    early = later_phase(3, True, packs, upstream, ends, [saved[1], saved[3]])
    early_grads = send_home(early[:4], (2, 3))
    ups = (upstream, early[4])
    part_a, small_a = other_phase(3, (0,), packs, ups, ends, saved, [], [])
    next_ends = exchange(early[6], [part_a])
    part_b, small_b = other_phase(3, (1,), packs, ups, ends, saved, [], [])
    late = later_phase(1, False, packs, early[5], next_ends, early_grads[1:] + [part_b])
    late_grads = send_home(late[:4], (0, 1))
    ups = (early[5], late[4])
    *parts, rates = other_phase(1, (0, 1), packs, ups, next_ends, saved, [part_a, part_b, small_a, small_b], [])
    parts = send_home(rate_sum(swap(rates, "branch"), parts, grad_scale), everyone)
    *others, decay_sum, skip_sum = home_small(parts)
    others = tuple(jnp.transpose(value, (0, 1, 3, 2)) for value in others)
    return (home_grad(early_grads, late_grads),) + others + (decay_sum, skip_sum)


def solution(mesh):
    placed = (
        P("section", None, "branch", None),
        P(None, "branch", None),
        P("section", None, "branch", None),
        P("section", None, "branch", None),
        P("section", None, "branch", None),
        P("section", None, "branch", None, None, None),
        P("section", None),
        P("section", None),
        P(),
    )
    return jax.shard_map(
        shards,
        mesh=mesh,
        in_specs=placed,
        out_specs=(
            P("section", None, "branch", None),
            P("section", None, "branch", None),
            P("section", None, "branch", None),
            P("section", None, "branch", None),
            P("section", None),
            P("section", None),
        ),
        check_vma=False,
    )
```

```python
import functools
import math

import jax
import jax.numpy as jnp
from jax import lax
from jax.experimental import pallas as pl
from jax.experimental.pallas import tpu as pltpu
from jax.sharding import PartitionSpec as P

F32 = jnp.float32
BF16 = jnp.bfloat16

SECTIONS = 4
FAMILIES = 2
ROWS = 128
STATE = 64
HEADDIM = 64
GROUP = 16
COLS = GROUP * HEADDIM
LANES = 128
CHUNK = 256
PER_CHUNK = CHUNK // HEADDIM
BRANCHES = 32
SEND_ROWS = 112
PACK_ROWS = FAMILIES * ROWS + 4 * GROUP
GRAD_ROWS = FAMILIES * (ROWS + GROUP)
HOME_ROWS = GRAD_ROWS + 16
SAVED_ROWS = COLS + COLS // 2
VMEM_LIMIT = 63 * 1024 * 1024

NN = (((1,), (0,)), ((), ()))
NT = (((1,), (1,)), ((), ()))
TN = (((0,), (0,)), ((), ()))


def dot(a, b, dims):
    return lax.dot_general(a, b, dims, preferred_element_type=F32)


def split(a):
    high = a.astype(BF16)
    return high, (a - high.astype(F32)).astype(BF16)


def dot3(a, b, dims):
    return dot(a[0], b[0], dims) + dot(a[1], b[0], dims) + dot(a[0], b[1], dims)


def dot2(a, b, dims):
    return dot(a[0], b, dims) + dot(a[1], b, dims)


def lane_ids(shape):
    return lax.broadcasted_iota(jnp.int32, shape, len(shape) - 1)


def half(rolled, plain, side):
    lanes = lane_ids(plain.shape)
    if side == 0:
        return jnp.where(lanes < STATE, plain, 0.0)
    return jnp.where(lanes >= STATE, rolled, 0.0)


def by_head(value, chunk):
    first = chunk * PER_CHUNK
    return jnp.concatenate(
        [jnp.broadcast_to(value[first + at : first + at + 1, :], (HEADDIM, LANES)) for at in range(PER_CHUNK)], axis=0
    )


def head_sums(value):
    return jnp.sum(value.reshape(PER_CHUNK, HEADDIM, LANES), axis=1)


def fetch_packs(layers, pack_refs, pack_buf, sems):
    mine = lax.axis_index("section")
    for at in layers:
        away = lax.rem(mine - at + SECTIONS, SECTIONS)
        for k in range(SECTIONS):

            @pl.when(away == k)
            def _():
                pltpu.make_async_copy(pack_refs[k], pack_buf.at[at], sems.at[at]).start()


def wait_packs(layers, pack_refs, pack_buf, sems):
    for at in layers:
        pltpu.make_async_copy(pack_refs[0], pack_buf.at[at], sems.at[at]).wait()


class Layer:
    def __init__(self, pack_ref, layer, family):
        base = FAMILIES * ROWS
        both = pack_ref[layer, family * ROWS : (family + 1) * ROWS, :]
        turned = pltpu.roll(both, STATE, 1)
        self.b = (half(both, both, 0), half(turned, turned, 1))
        self.c = (half(turned, turned, 0), half(both, both, 1))
        self.step = pack_ref[layer, base + family * GROUP : base + (family + 1) * GROUP, :]
        self.decay = pack_ref[layer, base + 2 * GROUP : base + 3 * GROUP, :]
        gain = pack_ref[layer, base + 3 * GROUP : base + 4 * GROUP, :]
        row = lax.broadcasted_iota(jnp.int32, (ROWS, ROWS), 0)
        col = lax.broadcasted_iota(jnp.int32, (ROWS, ROWS), 1)
        self.row, self.col = row, col
        upper = jnp.where(row <= col, 1.0, 0.0).astype(BF16)
        drop = -self.decay * self.step
        first = drop.astype(BF16)
        rest = drop - first.astype(F32)
        second = rest.astype(BF16)
        third = (rest - second.astype(F32)).astype(BF16)
        logs = dot(first, upper, NN) + dot(second, upper, NN) + dot(third, upper, NN)
        carried = jnp.exp(logs)
        scale = self.step * jnp.exp(-logs)
        total = jnp.sum(jnp.where(lane_ids(carried.shape) == ROWS - 1, carried, 0.0), axis=1, keepdims=True)
        self.total = jnp.broadcast_to(total, (GROUP, LANES))
        self.carried, self.scale, self.gain = carried, scale, gain
        read = dot3(split(self.c[0]), split(self.b[0]), NT)
        self.read = jnp.where(row >= col, read, 0.0)


def phase_a(family, upper_at, high, low, send_ref):
    c_pair = split(jnp.concatenate([high.c[0], low.c[1]], axis=0))
    c_both = split(low.c[0] + low.c[1])
    b_turned = jnp.transpose(high.b[0])[0:STATE]
    b_tile = jnp.concatenate([b_turned] * PER_CHUNK, axis=0)
    read = high.read.astype(BF16)
    mixed = low.carried * high.scale
    lanes = lane_ids((STATE // 2, LANES))
    for chunk in range(COLS // CHUNK):
        rows = slice(chunk * CHUNK, (chunk + 1) * CHUNK)
        upstream = upper_at(rows)
        hat2 = split(by_head(high.carried, chunk) * upstream)
        pulled = dot(hat2[0], read, NN)
        low_up = by_head(high.gain, chunk) * upstream + by_head(high.scale, chunk) * pulled
        low_hat2 = split(by_head(low.carried, chunk) * low_up)
        both = tuple(jnp.concatenate([a, b], axis=1) for a, b in zip(hat2, low_hat2))
        begin = dot3(both, c_pair, NN).astype(BF16)
        move = dot3(split(by_head(mixed, chunk) * b_tile), c_both, NN)
        for inner in range(PER_CHUNK):
            head = family * GROUP + chunk * PER_CHUNK + inner
            top = inner * HEADDIM
            send_ref[head, 0:HEADDIM, :] = begin[top : top + HEADDIM, :]
            first = move[top : top + 32, :]
            second = move[top + 32 : top + 64, :]
            send_ref[head, HEADDIM : HEADDIM + 32, :] = jnp.where(lanes < STATE, first, second).astype(BF16)
    totals = jnp.where(lane_ids((GROUP, LANES)) < STATE, high.total, low.total)
    total_high = totals.astype(BF16).astype(F32)
    total_low = totals - total_high
    place = lax.broadcasted_iota(jnp.int32, (16, LANES), 0)
    for inner in range(GROUP):
        one = jnp.broadcast_to(total_high[inner : inner + 1, :], (16, LANES))
        two = jnp.broadcast_to(total_low[inner : inner + 1, :], (16, LANES))
        block = jnp.where(place == 0, one, jnp.where(place == 1, two, 0.0))
        send_ref[family * GROUP + inner, 96:112, :] = block.astype(BF16)


def phase_b(family, side, layer, upper_at, end_ref, put_grad):
    b2 = split(jnp.transpose(layer.b[side]))
    weights = jnp.concatenate([layer.read.astype(BF16), b2[0]], axis=0)
    for chunk in range(COLS // CHUNK):
        rows = slice(chunk * CHUNK, (chunk + 1) * CHUNK)
        upstream = upper_at(rows)
        first = family * GROUP + chunk * PER_CHUNK
        ends = end_ref[first : first + PER_CHUNK].reshape(CHUNK, LANES)
        hat = (by_head(layer.carried, chunk) * upstream).astype(BF16)
        pulled = dot(jnp.concatenate([hat, ends], axis=1), weights, NN) + dot(ends, b2[1], NN)
        grad = by_head(layer.gain, chunk) * upstream + by_head(layer.scale, chunk) * pulled
        put_grad(rows, grad.astype(BF16))


def phase_c(family, side, layer, upper_at, saved_ref, end_ref, want):
    grads = grad_step = small = None
    b_one, c_one = layer.b[side].astype(BF16), layer.c[side].astype(BF16)
    b_turned = jnp.transpose(layer.b[side]).astype(BF16)
    read = layer.read.astype(BF16)
    weights = jnp.concatenate([jnp.transpose(layer.read), jnp.transpose(layer.c[side])], axis=0).astype(BF16)
    left = jnp.zeros((ROWS, ROWS + LANES), F32)
    grad_in = jnp.zeros((ROWS, LANES), F32)
    flow, worth, ending, skips = [], [], [], []
    lanes = lane_ids((CHUNK, LANES))
    for chunk in range(COLS // CHUNK):
        rows = slice(chunk * CHUNK, (chunk + 1) * CHUNK)
        upstream = upper_at(rows)
        x = saved_ref[family, rows, :].astype(F32)
        hat = by_head(layer.carried, chunk) * upstream
        hat_one = hat.astype(BF16)
        x_hat = by_head(layer.scale, chunk) * x
        x_one = x_hat.astype(BF16)
        first = family * GROUP + chunk * PER_CHUNK
        ends = end_ref[first : first + PER_CHUNK].reshape(CHUNK, LANES)
        top = COLS + (chunk % 2) * CHUNK
        packed = saved_ref[family, top : top + CHUNK, :].astype(F32)
        if (chunk < 2) != (side == 0):
            packed = pltpu.roll(packed, STATE, 1)
        saved = jnp.where((lanes < STATE) == (side == 0), packed, 0.0)
        x_saved = jnp.concatenate([x_one, saved.astype(BF16)], axis=1)
        if "grads" in want:
            left = left + dot(hat_one, x_saved, TN)
            grad_in = grad_in + dot(x_one, ends, TN)
        if "rates" not in want:
            continue
        end_in = dot(ends, b_turned, NN)
        pulled = dot(hat_one, read, NN) + end_in
        forward = dot(x_saved, weights, NN)
        x_pulled = x_hat * pulled
        worth.append(head_sums(x_pulled))
        flow.append(head_sums(hat * forward - x_pulled))
        ending.append(head_sums(x_hat * end_in + ends.astype(F32) * saved))
        skips.append(head_sums(x * upstream))
    if "grads" in want:
        pairs, grad_out = left[:, 0:ROWS], left[:, ROWS:]
        pairs = jnp.where(layer.row >= layer.col, pairs, 0.0).astype(BF16)
        grad_out = grad_out + dot(pairs, b_one, NN)
        grad_in = grad_in + dot(pairs, c_one, TN)
        lanes = lane_ids((ROWS, LANES))
        if side == 0:
            grads = jnp.where(lanes < STATE, grad_in, pltpu.roll(grad_out, STATE, 1))
        else:
            grads = jnp.where(lanes < STATE, pltpu.roll(grad_in, STATE, 1), grad_out)
    if "rates" in want:
        flow, worth, ending, skips = (jnp.concatenate(part, axis=0) for part in (flow, worth, ending, skips))
        later = jnp.where(layer.row >= layer.col, 1.0, 0.0).astype(BF16)
        rate = dot2(split(flow), later, NN) + jnp.sum(ending, axis=1, keepdims=True)
        grad_step = worth / layer.step - layer.decay * rate
        decay_part = jnp.sum(-layer.step * rate, axis=1, keepdims=True)
        skip_part = jnp.sum(skips, axis=1, keepdims=True)
        place = lane_ids((GROUP, LANES))
        small = jnp.where(place == 0, decay_part, jnp.where(place == 1, skip_part, 0.0))
    return grads, grad_step, small


def first_kernel(high_at, after, *refs):
    lengths_ref, cot_ref = refs[:2]
    pack_refs = refs[2:6]
    send_ref, up_ref, cot_buf, up_buf, send_buf, pack_ref, sems, pack_sem = refs[6 + after :]
    layers = (high_at, high_at - 1)
    fetch_packs(layers, pack_refs, pack_ref, pack_sem)
    mine = lax.axis_index("section")
    branch = lax.axis_index("branch")
    at = pl.multiple_of(mine * COLS, COLS)
    copy = pltpu.make_async_copy(cot_ref.at[:, :, pl.ds(at, COLS)], cot_buf, sems.at[3])
    copy.start()
    wait_packs(layers, pack_refs, pack_ref, pack_sem)
    ready = [[Layer(pack_ref, at, family) for at in layers] for family in range(FAMILIES)]
    copy.wait()
    copies = []
    for family in range(FAMILIES):
        slot = jnp.clip(branch - BRANCHES // 2, 0, BRANCHES // 2 - 1)
        limit = jnp.where(branch >= BRANCHES // 2, lengths_ref[family, slot], ROWS)

        def upper_at(rows):
            at = lane_ids((CHUNK, ROWS))
            value = jnp.where(at < limit, jnp.transpose(cot_buf[family, :, rows].astype(F32)), 0.0)
            up_buf[family, rows, :] = value.astype(BF16)
            return value

        phase_a(family, upper_at, *ready[family], send_buf)
        heads = pl.ds(family * GROUP, GROUP)
        copies.append(pltpu.make_async_copy(send_buf.at[heads], send_ref.at[heads], sems.at[family]))
        copies[-1].start()
    copies.append(pltpu.make_async_copy(up_buf, up_ref, sems.at[2]))
    copies[-1].start()
    for copy in copies:
        copy.wait()


def later_kernel(high_at, goes_on, after, *refs):
    pack_refs = refs[:4]
    up_ref, end_ref = refs[4:6]
    refs = refs[6 + after :]
    grad_refs, keep_refs = refs[0:4], refs[4:6]
    rest = refs[6:]
    if goes_on:
        send_ref, grad_buf, up_buf, end_buf, pack_ref, grad_sem, keep_sem, in_sem, pack_sem, send_buf, send_sem = rest
    else:
        grad_buf, up_buf, end_buf, pack_ref, grad_sem, keep_sem, in_sem, pack_sem = rest
    layers = range(high_at, high_at - (4 if goes_on else 2), -1)
    fetch_packs(layers[:2], pack_refs, pack_ref, pack_sem)
    ins = [
        pltpu.make_async_copy(up_ref, up_buf, in_sem.at[0]),
        pltpu.make_async_copy(end_ref, end_buf, in_sem.at[1]),
    ]
    for copy in ins:
        copy.start()
    fetch_packs(layers[2:], pack_refs, pack_ref, pack_sem)
    mine = lax.axis_index("section")
    wait_packs(layers[:2], pack_refs, pack_ref, pack_sem)
    ready = {at: Layer(pack_ref, high_at - at[0], at[1]) for at in ((0, 0), (0, 1))}
    for copy in ins:
        copy.wait()
    for side in range(2):
        layer_at = high_at - side
        for family in range(FAMILIES):

            def upper_at(rows):
                if side == 0:
                    return up_buf[family, rows, :].astype(F32)
                return grad_buf[0, family, rows, :].astype(F32)

            def put_grad(rows, value):
                grad_buf[side, family, rows, :] = value

            layer = ready.get((side, family)) or Layer(pack_ref, layer_at, family)
            phase_b(family, side, layer, upper_at, end_buf, put_grad)
        ahead = lax.rem(layer_at - mine + SECTIONS, SECTIONS)
        for k in range(SECTIONS):

            @pl.when(ahead == k)
            def _():
                pltpu.make_async_copy(grad_buf.at[side], grad_refs[k], grad_sem.at[side]).start()

    copies = [pltpu.make_async_copy(grad_buf.at[side], keep_refs[side], keep_sem.at[side]) for side in range(2)]
    for copy in copies:
        copy.start()
    if goes_on:
        wait_packs(layers[2:], pack_refs, pack_ref, pack_sem)
        for family in range(FAMILIES):

            def upper_at(rows):
                return grad_buf[1, family, rows, :].astype(F32)

            high = Layer(pack_ref, high_at - 2, family)
            low = Layer(pack_ref, high_at - 3, family)
            phase_a(family, upper_at, high, low, send_buf)
            heads = pl.ds(family * GROUP, GROUP)
            copies.append(pltpu.make_async_copy(send_buf.at[heads], send_ref.at[heads], send_sem.at[family]))
            copies[-1].start()
    for copy in copies:
        copy.wait()
    for side in range(2):
        pltpu.make_async_copy(grad_buf.at[side], grad_refs[0], grad_sem.at[side]).wait()


def other_kernel(high_at, sides, want, after, *refs):
    pack_refs, up_refs, end_ref, saved_refs = refs[:4], refs[4:6], refs[6], refs[7:11]
    refs = refs[11:]
    final = want == ("grads",)
    if final:
        held_refs, steps_ref, refs = refs[0:2], refs[2], refs[3:]
    elif len(sides) == 2:
        small_refs, refs = refs[0:2], refs[2:]
    refs = refs[after:]
    part_refs, refs = (refs[:4], refs[4:]) if final else (refs[:1], refs[1:])
    if not final:
        rate_ref, refs = refs[0], refs[1:]
    saved_buf, up_buf, end_buf, part_buf, pack_ref = refs[:5]
    saved_sem, up_sem, part_sem, end_sem, pack_sem = refs[5:]
    mine = lax.axis_index("section")
    layers = [high_at - side for side in sides]
    fetch_packs(layers, pack_refs, pack_ref, pack_sem)
    ends = pltpu.make_async_copy(end_ref, end_buf, end_sem.at[0])
    ends.start()
    for side in sides:
        away = lax.rem(mine - (high_at - side) + SECTIONS, SECTIONS)
        pltpu.make_async_copy(up_refs[side], up_buf.at[side], up_sem.at[side]).start()
        for k in range(SECTIONS):

            @pl.when(away == k)
            def _():
                pltpu.make_async_copy(saved_refs[k], saved_buf.at[side], saved_sem.at[side]).start()

    def hand_on(source, layer_at):
        to = [part.at[pl.ds(0, GRAD_ROWS)] for part in part_refs] if final else part_refs
        copies = [pltpu.make_async_copy(source, part, part_sem.at[layer_at]) for part in to]
        if final:
            ahead = lax.rem(layer_at - mine + SECTIONS, SECTIONS)
            for k in range(SECTIONS):

                @pl.when(ahead == k)
                def _():
                    copies[k].start()
        else:
            copies[0].start()
        moved.append(copies[0])

    moved = []
    steps = slice(FAMILIES * ROWS, GRAD_ROWS)
    if final:
        for side in range(2):
            hand_on(held_refs[side], high_at + 2 - side)
            pltpu.make_async_copy(steps_ref.at[side], part_buf.at[side, steps], end_sem.at[1 + side]).start()
    wait_packs(layers, pack_refs, pack_ref, pack_sem)
    ready = [Layer(pack_ref, layers[0], family) for family in range(FAMILIES)]
    ends.wait()
    smalls_of = []
    for side in sides:
        pltpu.make_async_copy(up_refs[side], up_buf.at[side], up_sem.at[side]).wait()
        pltpu.make_async_copy(saved_refs[0], saved_buf.at[side], saved_sem.at[side]).wait()
        smalls = jnp.zeros((GROUP, LANES), F32)
        for family in range(FAMILIES):

            def upper_at(rows):
                return up_buf[side, family, rows, :].astype(F32)

            layer = ready[family] if side == sides[0] else Layer(pack_ref, high_at - side, family)
            grads, grad_step, small = phase_c(family, side, layer, upper_at, saved_buf.at[side], end_buf, want)
            if "grads" in want:
                part_buf[side, family * ROWS : (family + 1) * ROWS, :] = grads.astype(BF16)
            if "rates" in want:
                below = FAMILIES * ROWS + family * GROUP
                part_buf[side, below : below + GROUP, :] = grad_step.astype(BF16)
                smalls = smalls + small
        if final:
            pltpu.make_async_copy(steps_ref.at[side], part_buf.at[side, steps], end_sem.at[1 + side]).wait()
        if "grads" in want:
            hand_on(part_buf.at[side], high_at - side)
        else:
            moved.append(pltpu.make_async_copy(part_buf.at[side, steps], part_refs[0].at[side], part_sem.at[side]))
            moved[-1].start()
        smalls_of.append(smalls)
    if final:
        pass
    elif len(sides) == 2:
        blocks = smalls_of[::-1] + [small_refs[1][...], small_refs[0][...]]
        turned = jnp.transpose(jnp.concatenate(blocks + [jnp.zeros((STATE, LANES), F32)], axis=0))
        row = turned[0:1] + pltpu.roll(turned[1:2], STATE, 1)
        rate_ref[...] = jnp.broadcast_to(row[None], (BRANCHES, 1, LANES))
    else:
        rate_ref[...] = smalls_of[0]
    for copy in moved:
        copy.wait()


def chain_kernel(*refs):
    got_ref, end_ref = refs[0], refs[-1]
    lanes = lane_ids((STATE // 2, LANES))
    prompt = BRANCHES // 2
    fork = jnp.zeros((HEADDIM, LANES), F32)
    for at in range(prompt, BRANCHES):
        fork = fork + got_ref[at, 0:HEADDIM, :].astype(F32)
    plain, extra = fork, jnp.zeros((HEADDIM, LANES), F32)
    blank = jnp.zeros((STATE, LANES), F32)
    for at in range(prompt - 1, -1, -1):
        tail = got_ref[at, 96:112, :].astype(F32)
        total = tail[0:1, :] + tail[1:2, :]
        plain = total * plain
        extra = total * extra
        end_ref[at, :, :] = (plain + extra).astype(BF16)
        if at == 0:
            break
        packed = got_ref[at, HEADDIM : HEADDIM + 32, :].astype(F32)
        turned = pltpu.roll(packed, STATE, 1)
        move = jnp.concatenate(
            [jnp.where(lanes >= STATE, turned, 0.0), jnp.where(lanes >= STATE, packed, 0.0), blank], axis=0
        ).astype(BF16)
        extra = extra + dot2(split(plain), move, NN)
        plain = plain + got_ref[at, 0:HEADDIM, :].astype(F32)
    for at in range(prompt, BRANCHES):
        end_ref[at, :, :] = jnp.zeros((HEADDIM, LANES), BF16)


def pack_kernel(*refs):
    sources, decay_ref, gain_ref = refs[0:3], refs[3], refs[4]
    pack_refs = refs[5:9]
    in_ref, out_ref, step_ref, both_ref, rate_ref, sems, send_sems = refs[9:]
    copies = [
        pltpu.make_async_copy(source.at[0], to, sems.at[at])
        for at, (source, to) in enumerate(zip(sources, (in_ref, out_ref, step_ref)))
    ]
    for copy in copies:
        copy.start()
    mine = lax.axis_index("section")
    base = FAMILIES * ROWS
    rate_ref[0] = jnp.transpose(jnp.broadcast_to(decay_ref[...], (LANES, SECTIONS * GROUP)))
    rate_ref[1] = jnp.transpose(jnp.broadcast_to(gain_ref[...], (LANES, SECTIONS * GROUP)))
    for copy in copies:
        copy.wait()
    for k in range(SECTIONS):
        heads = pl.ds(pl.multiple_of(lax.rem(mine + k, SECTIONS) * GROUP, GROUP), GROUP)
        for family in range(FAMILIES):
            both_ref[k, base + family * GROUP : base + (family + 1) * GROUP, :] = step_ref[family, heads, :]
        both_ref[k, base + 2 * GROUP : base + 3 * GROUP, :] = rate_ref[0, heads, :]
        both_ref[k, base + 3 * GROUP : base + 4 * GROUP, :] = rate_ref[1, heads, :]
    for family in range(FAMILIES):
        turned = jnp.transpose(jnp.concatenate([in_ref[family], out_ref[family]], axis=0))
        for k in range(SECTIONS):
            both_ref[k, family * ROWS : (family + 1) * ROWS, :] = turned
    copies = []
    for k in range(SECTIONS):
        copies.append(pltpu.make_async_copy(both_ref.at[k], pack_refs[k], send_sems.at[k]))
        copies[-1].start()
    for copy in copies:
        copy.wait()


def sort_kernel(at_ref, *refs):
    for x_ref, s_ref, o_ref in zip(refs[0:4], refs[4:8], refs[8:12]):
        o_ref[0, 0:COLS] = jnp.transpose(x_ref[0, 0])
        whole = s_ref[0, 0, 0].reshape(COLS, STATE)
        o_ref[0, COLS:SAVED_ROWS] = jnp.concatenate([whole[: COLS // 2], whole[COLS // 2 :]], axis=1).astype(BF16)


def fetch_home(early, late, to, sems):
    mine = lax.axis_index("section")
    for is_early, pieces in ((True, early), (False, late)):

        @pl.when((mine >= 2) == is_early)
        def _():
            for k in range(SECTIONS):
                source = lax.rem(mine - k + SECTIONS, SECTIONS)
                pltpu.make_async_copy(pieces[k], to(source), sems.at[k]).start()

    for k in range(SECTIONS):
        pltpu.make_async_copy(early[k], to(k), sems.at[k]).wait()


def home_small_kernel(*refs):
    piece_refs = refs[:4]
    in_ref, out_ref, step_ref, decay_ref, skip_ref, part_ref, part_sem = refs[-7:]
    mine = lax.axis_index("section")
    for k in range(SECTIONS):
        source = lax.rem(mine - k + SECTIONS, SECTIONS)
        pltpu.make_async_copy(piece_refs[k], part_ref.at[source], part_sem.at[k]).start()
    for k in range(SECTIONS):
        pltpu.make_async_copy(piece_refs[k], part_ref.at[k], part_sem.at[k]).wait()
    for family in range(FAMILIES):
        rows = slice(family * ROWS, (family + 1) * ROWS)
        total = part_ref[0, rows, :].astype(F32)
        for k in range(1, SECTIONS):
            total = total + part_ref[k, rows, :].astype(F32)
        turned = jnp.transpose(total)
        in_ref[0, family] = turned[0:STATE]
        out_ref[0, family] = turned[STATE:]
        below = FAMILIES * ROWS + family * GROUP
        for k in range(SECTIONS):
            step_ref[0, family, k * GROUP : (k + 1) * GROUP, :] = part_ref[k, below : below + GROUP, :].astype(F32)
    section = (lane_ids((8, LANES)) & (STATE - 1)) >> 4
    total = jnp.zeros((8, LANES), F32)
    for at in range(SECTIONS):
        tail = part_ref[at, GRAD_ROWS:HOME_ROWS, :].astype(F32)
        row = jnp.broadcast_to(tail[0:1] + tail[1:2], (8, LANES))
        shift = lax.rem(at - mine + SECTIONS, SECTIONS) * GROUP
        ahead, behind = pltpu.roll(row, shift, 1), pltpu.roll(row, shift + STATE, 1)
        low = (lane_ids((8, LANES)) & (STATE - 1)) >= shift
        total = jnp.where(section == at, jnp.where(low, ahead, behind), total)
    decay_ref[...] = total[0:1, 0:STATE]
    skip_ref[...] = total[0:1, STATE:]


def home_grad_kernel(*refs):
    early, late = refs[0:4], refs[4:8]
    grad_ref, turned_buf, grad_buf, grad_sem, out_sem = refs[8:]
    fetch_home(early, late, lambda source: turned_buf.at[source], grad_sem)
    outs = []
    for source in range(SECTIONS):
        cols = slice(source * COLS, (source + 1) * COLS)
        for family in range(FAMILIES):
            grad_buf[family, :, cols] = jnp.transpose(turned_buf[source, family])
        outs.append(
            pltpu.make_async_copy(
                grad_buf.at[:, :, pl.ds(source * COLS, COLS)],
                grad_ref.at[0, :, :, pl.ds(source * COLS, COLS)],
                out_sem.at[source],
            )
        )
        outs[-1].start()
    for out in outs:
        out.wait()


def rate_sum_kernel(scale, *refs):
    got_ref, part_refs, buf, sems = refs[0], refs[5:9], refs[9], refs[10]
    total = got_ref[0]
    for at in range(1, BRANCHES):
        total = total + got_ref[at]
    total = jnp.broadcast_to(total * scale, (16, LANES))
    high = total.astype(BF16).astype(F32)
    place = lax.broadcasted_iota(jnp.int32, (16, LANES), 0)
    buf[...] = jnp.where(place == 0, high, jnp.where(place == 1, total - high, 0.0)).astype(BF16)
    copies = [
        pltpu.make_async_copy(buf, part_refs[to].at[pl.ds(GRAD_ROWS, 16)], sems.at[to]) for to in range(SECTIONS)
    ]
    for copy in copies:
        copy.start()
    for copy in copies:
        copy.wait()


ALL = ("grads", "rates")
VM = pl.BlockSpec(memory_space=pltpu.VMEM)
SM = pl.BlockSpec(memory_space=pltpu.SMEM)
ANY = pl.BlockSpec(memory_space=pl.ANY)
HBM = pl.BlockSpec(memory_space=pltpu.HBM)
PARAMS = pltpu.CompilerParams(vmem_limit_bytes=VMEM_LIMIT)
SMALL_PARAMS = pltpu.CompilerParams(vmem_limit_bytes=32 * 1024 * 1024)


PACKS = pltpu.VMEM((SECTIONS, PACK_ROWS, LANES), F32)


def shape(dims, dtype):
    return jax.ShapeDtypeStruct(dims, dtype)


def cost(flops):
    return pl.CostEstimate(flops=flops, bytes_accessed=4_000_000, transcendentals=0)


def sems(count):
    return pltpu.SemaphoreType.DMA((count,))


def pack_small(state_in, state_out, step_size, decay_rate, skip_gain):
    turned = [jnp.transpose(value, (0, 1, 3, 2)) for value in (state_in, state_out, step_size)]
    return pl.pallas_call(
        pack_kernel,
        out_shape=[shape((PACK_ROWS, LANES), F32)] * SECTIONS,
        in_specs=[ANY] * 3 + [VM] * 2,
        out_specs=[HBM] * SECTIONS,
        scratch_shapes=[
            pltpu.VMEM((FAMILIES, STATE, ROWS), F32),
            pltpu.VMEM((FAMILIES, STATE, ROWS), F32),
            pltpu.VMEM((FAMILIES, SECTIONS * GROUP, ROWS), F32),
            pltpu.VMEM((SECTIONS, PACK_ROWS, LANES), F32),
            pltpu.VMEM((2, SECTIONS * GROUP, LANES), F32),
            sems(3),
            sems(4),
        ],
        compiler_params=PARAMS,
        name="pack_small",
    )(*turned, decay_rate, skip_gain)


def sort_heads(layer_input, saved_states):
    mine = jnp.full((1,), lax.axis_index("section"), jnp.int32)

    def x_spec(k):
        return pl.BlockSpec(
            (1, 1, ROWS, COLS), lambda f, at: (0, f, 0, lax.rem(at[0] + k, SECTIONS))
        )

    def s_spec(k):
        return pl.BlockSpec(
            (1, 1, 1, GROUP, HEADDIM, STATE), lambda f, at: (0, f, 0, lax.rem(at[0] + k, SECTIONS), 0, 0)
        )

    return pl.pallas_call(
        sort_kernel,
        grid_spec=pltpu.PrefetchScalarGridSpec(
            num_scalar_prefetch=1,
            grid=(FAMILIES,),
            in_specs=[x_spec(k) for k in range(SECTIONS)] + [s_spec(k) for k in range(SECTIONS)],
            out_specs=[pl.BlockSpec((1, SAVED_ROWS, LANES), lambda f, at: (f, 0, 0))] * SECTIONS,
        ),
        out_shape=[shape((FAMILIES, SAVED_ROWS, LANES), BF16)] * SECTIONS,
        compiler_params=PARAMS,
        cost_estimate=cost(4_000_000_000),
        name="sort_heads",
    )(mine, *([layer_input] * SECTIONS), *([saved_states] * SECTIONS))


def first_phase(high_at, lengths, cotangent, packs, after):
    return pl.pallas_call(
        functools.partial(first_kernel, high_at, len(after)),
        out_shape=[
            shape((BRANCHES, SEND_ROWS, LANES), BF16),
            shape((FAMILIES, COLS, ROWS), BF16),
        ],
        in_specs=[SM] + [ANY] * (5 + len(after)),
        out_specs=[HBM, HBM],
        scratch_shapes=[
            pltpu.VMEM((FAMILIES, ROWS, COLS), BF16),
            pltpu.VMEM((FAMILIES, COLS, ROWS), BF16),
            pltpu.VMEM((BRANCHES, SEND_ROWS, LANES), BF16),
            PACKS,
            sems(4),
            sems(4),
        ],
        compiler_params=PARAMS,
        name="first_phase",
    )(lengths, cotangent, *packs, *after)


def later_phase(high_at, goes_on, packs, upstream, ends, after):
    outs = [shape((FAMILIES, COLS, ROWS), BF16)] * 4
    outs += [shape((FAMILIES, COLS, ROWS), BF16)] * 2
    scratch = [
        pltpu.VMEM((2, FAMILIES, COLS, ROWS), BF16),
        pltpu.VMEM((FAMILIES, COLS, ROWS), BF16),
        pltpu.VMEM((BRANCHES, HEADDIM, LANES), BF16),
        PACKS,
        sems(2),
        sems(2),
        sems(2),
        sems(4),
    ]
    if goes_on:
        outs += [shape((BRANCHES, SEND_ROWS, LANES), BF16)]
        scratch += [pltpu.VMEM((BRANCHES, SEND_ROWS, LANES), BF16), sems(2)]
    return pl.pallas_call(
        functools.partial(later_kernel, high_at, goes_on, len(after)),
        out_shape=outs,
        in_specs=[ANY] * (6 + len(after)),
        out_specs=[HBM] * len(outs),
        scratch_shapes=scratch,
        compiler_params=PARAMS,
        name="later_phase",
    )(*packs, upstream, ends, *after)


def other_phase(high_at, sides, want, packs, ups, ends, saved, held, after):
    if want == ("grads",):
        outs = [shape((HOME_ROWS, LANES), BF16)] * SECTIONS
        extra, specs = [ANY] * 3, [HBM] * SECTIONS
    elif len(sides) == 2:
        outs = [shape((2, FAMILIES * GROUP, LANES), BF16), shape((BRANCHES, 1, LANES), F32)]
        extra, specs = [VM] * 2, [HBM, VM]
    else:
        outs = [shape((GRAD_ROWS, LANES), BF16), shape((GROUP, LANES), F32)]
        extra, specs = [], [HBM, VM]
    return pl.pallas_call(
        functools.partial(other_kernel, high_at, sides, want, len(after)),
        out_shape=outs,
        in_specs=[ANY] * 11 + extra + [ANY] * len(after),
        out_specs=specs,
        scratch_shapes=[
            pltpu.VMEM((2, FAMILIES, SAVED_ROWS, LANES), BF16),
            pltpu.VMEM((2, FAMILIES, COLS, ROWS), BF16),
            pltpu.VMEM((BRANCHES, HEADDIM, LANES), BF16),
            pltpu.VMEM((2, GRAD_ROWS, LANES), BF16),
            PACKS,
            sems(2),
            sems(2),
            sems(4),
            sems(3),
            sems(4),
        ],
        compiler_params=PARAMS,
        cost_estimate=cost(6_000_000_000 if len(want) == 2 else 5_000_000_000),
        name="other_phase",
    )(*packs, *ups, ends, *saved, *held, *after)


def chain(got, after):
    return pl.pallas_call(
        chain_kernel,
        out_shape=shape((BRANCHES, HEADDIM, LANES), BF16),
        in_specs=[VM] + [ANY] * len(after),
        out_specs=VM,
        compiler_params=SMALL_PARAMS,
        name="chain",
    )(got, *after)


def home_small(parts, after):
    return pl.pallas_call(
        home_small_kernel,
        out_shape=[
            shape((1, FAMILIES, STATE, ROWS), F32),
            shape((1, FAMILIES, STATE, ROWS), F32),
            shape((1, FAMILIES, SECTIONS * GROUP, ROWS), F32),
            shape((1, SECTIONS * GROUP), F32),
            shape((1, SECTIONS * GROUP), F32),
        ],
        in_specs=[ANY] * (4 + len(after)),
        out_specs=[VM] * 5,
        scratch_shapes=[pltpu.VMEM((SECTIONS, HOME_ROWS, LANES), BF16), sems(SECTIONS)],
        compiler_params=PARAMS,
        name="home_small",
    )(*parts, *after)


def home_grad(early, late):
    return pl.pallas_call(
        home_grad_kernel,
        out_shape=shape((1, FAMILIES, ROWS, SECTIONS * COLS), BF16),
        in_specs=[ANY] * 8,
        out_specs=HBM,
        scratch_shapes=[
            pltpu.VMEM((SECTIONS, FAMILIES, COLS, ROWS), BF16),
            pltpu.VMEM((FAMILIES, ROWS, SECTIONS * COLS), BF16),
            sems(SECTIONS),
            sems(SECTIONS),
        ],
        compiler_params=PARAMS,
        cost_estimate=cost(3_000_000_000),
        name="home_grad",
    )(*early, *late)


def rate_sum(got, parts, scale):
    return pl.pallas_call(
        functools.partial(rate_sum_kernel, scale),
        out_shape=[shape((HOME_ROWS, LANES), BF16)] * SECTIONS,
        in_specs=[VM] + [HBM] * SECTIONS,
        out_specs=[HBM] * SECTIONS,
        scratch_shapes=[pltpu.VMEM((16, LANES), BF16), sems(SECTIONS)],
        input_output_aliases={1 + k: k for k in range(SECTIONS)},
        compiler_params=PARAMS,
        name="rate_sum",
    )(got, *parts)


def swap(value, axis):
    return lax.all_to_all(value, axis, 0, 0, tiled=True)


def send_on(value, k, targets):
    pairs = [(i, (i + k) % SECTIONS) for i in range(SECTIONS) if (i + k) % SECTIONS in targets]
    return lax.ppermute(value, "section", pairs)


def send_home(pieces, targets):
    return [pieces[0]] + [send_on(pieces[k], k, targets) for k in range(1, SECTIONS)]


def exchange(send, after):
    return swap(chain(swap(send, "branch"), after), "branch")


def shards(
    layer_input,
    cotangent,
    state_in,
    state_out,
    step_size,
    saved_states,
    decay_rate,
    skip_gain,
    lengths,
):
    grad_scale = 1.0 / math.sqrt(FAMILIES * ROWS * BRANCHES * HEADDIM)
    everyone = tuple(range(SECTIONS))
    packs = pack_small(state_in, state_out, step_size, decay_rate, skip_gain)
    packs = [packs[0]] + [send_on(packs[k], k, everyone) for k in range(1, SECTIONS)]
    saved = sort_heads(layer_input, saved_states)
    top, upstream = first_phase(3, lengths, cotangent, packs, [saved[0]])
    saved = [saved[0]] + [send_on(saved[k], k, everyone) for k in range(1, SECTIONS)]
    ends = exchange(top, [])
    early = later_phase(3, True, packs, upstream, ends, [saved[1], saved[3]])
    early_grads = send_home(early[:4], (2, 3))
    ups = (upstream, early[4])
    part_a, small_a = other_phase(3, (0,), ALL, packs, ups, ends, saved, [], [])
    next_ends = exchange(early[6], [])
    part_b, small_b = other_phase(3, (1,), ALL, packs, ups, ends, saved, [], [])
    late = later_phase(1, False, packs, early[5], next_ends, early_grads[1:] + [part_b])
    late_grads = send_home(late[:4], (0, 1))
    ups = (early[5], late[4])
    steps, rates = other_phase(1, (0, 1), ("rates",), packs, ups, next_ends, saved, [small_a, small_b], [])
    parts = other_phase(1, (0, 1), ("grads",), packs, ups, next_ends, saved, [part_a, part_b, steps], [])
    parts = send_home(rate_sum(swap(rates, "branch"), parts, grad_scale), everyone)
    grad = home_grad(early_grads, late_grads)
    *others, decay_sum, skip_sum = home_small(parts, [grad])
    others = tuple(jnp.transpose(value, (0, 1, 3, 2)) for value in others)
    return (grad,) + others + (decay_sum, skip_sum)


def solution(mesh):
    placed = (
        P("section", None, "branch", None),
        P(None, "branch", None),
        P("section", None, "branch", None),
        P("section", None, "branch", None),
        P("section", None, "branch", None),
        P("section", None, "branch", None, None, None),
        P("section", None),
        P("section", None),
        P(),
    )
    return jax.shard_map(
        shards,
        mesh=mesh,
        in_specs=placed,
        out_specs=(
            P("section", None, "branch", None),
            P("section", None, "branch", None),
            P("section", None, "branch", None),
            P("section", None, "branch", None),
            P("section", None),
            P("section", None),
        ),
        check_vma=False,
    )
```

```python
import functools
import math

import jax
import jax.numpy as jnp
from jax import lax
from jax.experimental import pallas as pl
from jax.experimental.pallas import tpu as pltpu
from jax.sharding import PartitionSpec as P

F32 = jnp.float32
BF16 = jnp.bfloat16

SECTIONS = 4
FAMILIES = 2
ROWS = 128
STATE = 64
HEADDIM = 64
GROUP = 16
COLS = GROUP * HEADDIM
LANES = 128
CHUNK = 256
PER_CHUNK = CHUNK // HEADDIM
BRANCHES = 32
SEND_ROWS = 112
PACK_ROWS = FAMILIES * ROWS + 4 * GROUP
GRAD_ROWS = FAMILIES * (ROWS + GROUP)
HOME_ROWS = GRAD_ROWS + 16
SAVED_ROWS = COLS + COLS // 2
VMEM_LIMIT = 63 * 1024 * 1024

NN = (((1,), (0,)), ((), ()))
NT = (((1,), (1,)), ((), ()))
TN = (((0,), (0,)), ((), ()))


def dot(a, b, dims):
    return lax.dot_general(a, b, dims, preferred_element_type=F32)


def split(a):
    high = a.astype(BF16)
    return high, (a - high.astype(F32)).astype(BF16)


def dot3(a, b, dims):
    return dot(a[0], b[0], dims) + dot(a[1], b[0], dims) + dot(a[0], b[1], dims)


def dot2(a, b, dims):
    return dot(a[0], b, dims) + dot(a[1], b, dims)


def lane_ids(shape):
    return lax.broadcasted_iota(jnp.int32, shape, len(shape) - 1)


def half(rolled, plain, side):
    lanes = lane_ids(plain.shape)
    if side == 0:
        return jnp.where(lanes < STATE, plain, 0.0)
    return jnp.where(lanes >= STATE, rolled, 0.0)


def by_head(value, chunk):
    first = chunk * PER_CHUNK
    return jnp.concatenate(
        [jnp.broadcast_to(value[first + at : first + at + 1, :], (HEADDIM, LANES)) for at in range(PER_CHUNK)], axis=0
    )


def head_sums(value):
    return jnp.sum(value.reshape(PER_CHUNK, HEADDIM, LANES), axis=1)


def fetch_packs(layers, pack_refs, pack_buf, sems):
    mine = lax.axis_index("section")
    for at in layers:
        away = lax.rem(mine - at + SECTIONS, SECTIONS)
        for k in range(SECTIONS):

            @pl.when(away == k)
            def _():
                pltpu.make_async_copy(pack_refs[k], pack_buf.at[at], sems.at[at]).start()


def wait_packs(layers, pack_refs, pack_buf, sems):
    for at in layers:
        pltpu.make_async_copy(pack_refs[0], pack_buf.at[at], sems.at[at]).wait()


def wide(a, b):
    return jnp.concatenate([a, b], axis=1)


def folded(value):
    return value[:, 0:LANES] + value[:, LANES:]


class Layer:
    def __init__(self, pack_ref, layer, family):
        base = FAMILIES * ROWS
        both = pack_ref[layer, family * ROWS : (family + 1) * ROWS, :]
        turned = pltpu.roll(both, STATE, 1)
        self.b = (half(both, both, 0), half(turned, turned, 1))
        self.c = (half(turned, turned, 0), half(both, both, 1))
        self.step = pack_ref[layer, base + family * GROUP : base + (family + 1) * GROUP, :]
        self.decay = pack_ref[layer, base + 2 * GROUP : base + 3 * GROUP, :]
        gain = pack_ref[layer, base + 3 * GROUP : base + 4 * GROUP, :]
        row = lax.broadcasted_iota(jnp.int32, (ROWS, ROWS), 0)
        col = lax.broadcasted_iota(jnp.int32, (ROWS, ROWS), 1)
        self.row, self.col = row, col
        upper = jnp.where(row <= col, 1.0, 0.0).astype(BF16)
        drop = -self.decay * self.step
        first = drop.astype(BF16)
        rest = drop - first.astype(F32)
        second = rest.astype(BF16)
        third = (rest - second.astype(F32)).astype(BF16)
        logs = dot(first, upper, NN) + dot(second, upper, NN) + dot(third, upper, NN)
        carried = jnp.exp(logs)
        scale = self.step * jnp.exp(-logs)
        total = jnp.sum(jnp.where(lane_ids(carried.shape) == ROWS - 1, carried, 0.0), axis=1, keepdims=True)
        self.total = jnp.broadcast_to(total, (GROUP, LANES))
        self.carried, self.scale, self.gain = carried, scale, gain
        read = dot3(split(self.c[0]), split(self.b[0]), NT)
        self.read = jnp.where(row >= col, read, 0.0)


def phase_a(family, upper_at, high, low, send_ref):
    c_pair = split(jnp.concatenate([high.c[0], low.c[1]], axis=0))
    c_both = split(low.c[0] + low.c[1])
    c_pair_wide, c_both_wide = wide(*c_pair), wide(*c_both)
    b_turned = jnp.transpose(high.b[0])[0:STATE]
    b_tile = jnp.concatenate([b_turned] * PER_CHUNK, axis=0)
    read = high.read.astype(BF16)
    mixed = low.carried * high.scale
    lanes = lane_ids((STATE // 2, LANES))
    for chunk in range(COLS // CHUNK):
        rows = slice(chunk * CHUNK, (chunk + 1) * CHUNK)
        upstream = upper_at(rows)
        hat2 = split(by_head(high.carried, chunk) * upstream)
        pulled = dot(hat2[0], read, NN)
        low_up = by_head(high.gain, chunk) * upstream + by_head(high.scale, chunk) * pulled
        low_hat2 = split(by_head(low.carried, chunk) * low_up)
        both = tuple(jnp.concatenate([a, b], axis=1) for a, b in zip(hat2, low_hat2))
        begin = (folded(dot(both[0], c_pair_wide, NN)) + dot(both[1], c_pair[0], NN)).astype(BF16)
        response = split(by_head(mixed, chunk) * b_tile)
        move = folded(dot(response[0], c_both_wide, NN)) + dot(response[1], c_both[0], NN)
        for inner in range(PER_CHUNK):
            head = family * GROUP + chunk * PER_CHUNK + inner
            top = inner * HEADDIM
            send_ref[head, 0:HEADDIM, :] = begin[top : top + HEADDIM, :]
            first = move[top : top + 32, :]
            second = move[top + 32 : top + 64, :]
            send_ref[head, HEADDIM : HEADDIM + 32, :] = jnp.where(lanes < STATE, first, second).astype(BF16)
    totals = jnp.where(lane_ids((GROUP, LANES)) < STATE, high.total, low.total)
    total_high = totals.astype(BF16).astype(F32)
    total_low = totals - total_high
    place = lax.broadcasted_iota(jnp.int32, (16, LANES), 0)
    for inner in range(GROUP):
        one = jnp.broadcast_to(total_high[inner : inner + 1, :], (16, LANES))
        two = jnp.broadcast_to(total_low[inner : inner + 1, :], (16, LANES))
        block = jnp.where(place == 0, one, jnp.where(place == 1, two, 0.0))
        send_ref[family * GROUP + inner, 96:112, :] = block.astype(BF16)


def phase_b(family, side, layer, upper_at, end_ref, put_grad):
    b2 = split(jnp.transpose(layer.b[side]))
    read = layer.read.astype(BF16)
    weights = jnp.concatenate([wide(read, jnp.zeros_like(read)), wide(*b2)], axis=0)
    for chunk in range(COLS // CHUNK):
        rows = slice(chunk * CHUNK, (chunk + 1) * CHUNK)
        upstream = upper_at(rows)
        first = family * GROUP + chunk * PER_CHUNK
        ends = end_ref[first : first + PER_CHUNK].reshape(CHUNK, LANES)
        hat = (by_head(layer.carried, chunk) * upstream).astype(BF16)
        pulled = folded(dot(wide(hat, ends), weights, NN))
        grad = by_head(layer.gain, chunk) * upstream + by_head(layer.scale, chunk) * pulled
        put_grad(rows, grad.astype(BF16))


def phase_c(family, side, layer, upper_at, saved_ref, end_ref, want):
    grads = grad_step = small = None
    b_one, c_one = layer.b[side].astype(BF16), layer.c[side].astype(BF16)
    b_turned = jnp.transpose(layer.b[side]).astype(BF16)
    read = layer.read.astype(BF16)
    weights = jnp.concatenate([jnp.transpose(layer.read), jnp.transpose(layer.c[side])], axis=0).astype(BF16)
    pulls = jnp.concatenate([wide(read, jnp.zeros_like(read)), wide(b_turned, b_turned)], axis=0)
    left = jnp.zeros((ROWS, ROWS + LANES), F32)
    grad_in = jnp.zeros((ROWS, LANES), F32)
    flow, worth, ending, skips = [], [], [], []
    lanes = lane_ids((CHUNK, LANES))
    for chunk in range(COLS // CHUNK):
        rows = slice(chunk * CHUNK, (chunk + 1) * CHUNK)
        upstream = upper_at(rows)
        x = saved_ref[family, rows, :].astype(F32)
        hat = by_head(layer.carried, chunk) * upstream
        hat_one = hat.astype(BF16)
        x_hat = by_head(layer.scale, chunk) * x
        x_one = x_hat.astype(BF16)
        first = family * GROUP + chunk * PER_CHUNK
        ends = end_ref[first : first + PER_CHUNK].reshape(CHUNK, LANES)
        top = COLS + (chunk % 2) * CHUNK
        packed = saved_ref[family, top : top + CHUNK, :].astype(F32)
        if (chunk < 2) != (side == 0):
            packed = pltpu.roll(packed, STATE, 1)
        saved = jnp.where((lanes < STATE) == (side == 0), packed, 0.0)
        x_saved = jnp.concatenate([x_one, saved.astype(BF16)], axis=1)
        if "grads" in want:
            left = left + dot(hat_one, x_saved, TN)
            grad_in = grad_in + dot(x_one, ends, TN)
        if "rates" not in want:
            continue
        both = dot(wide(hat_one, ends), pulls, NN)
        pulled, end_in = both[:, 0:LANES], both[:, LANES:]
        forward = dot(x_saved, weights, NN)
        x_pulled = x_hat * pulled
        worth.append(head_sums(x_pulled))
        flow.append(head_sums(hat * forward - x_pulled))
        ending.append(head_sums(x_hat * end_in + ends.astype(F32) * saved))
        skips.append(head_sums(x * upstream))
    if "grads" in want:
        pairs, grad_out = left[:, 0:ROWS], left[:, ROWS:]
        pairs = jnp.where(layer.row >= layer.col, pairs, 0.0).astype(BF16)
        grad_out = grad_out + dot(pairs, b_one, NN)
        grad_in = grad_in + dot(pairs, c_one, TN)
        lanes = lane_ids((ROWS, LANES))
        if side == 0:
            grads = jnp.where(lanes < STATE, grad_in, pltpu.roll(grad_out, STATE, 1))
        else:
            grads = jnp.where(lanes < STATE, pltpu.roll(grad_in, STATE, 1), grad_out)
    if "rates" in want:
        flow, worth, ending, skips = (jnp.concatenate(part, axis=0) for part in (flow, worth, ending, skips))
        later = jnp.where(layer.row >= layer.col, 1.0, 0.0).astype(BF16)
        rate = dot2(split(flow), later, NN) + jnp.sum(ending, axis=1, keepdims=True)
        grad_step = worth / layer.step - layer.decay * rate
        decay_part = jnp.sum(-layer.step * rate, axis=1, keepdims=True)
        skip_part = jnp.sum(skips, axis=1, keepdims=True)
        place = lane_ids((GROUP, LANES))
        small = jnp.where(place == 0, decay_part, jnp.where(place == 1, skip_part, 0.0))
    return grads, grad_step, small


def first_kernel(high_at, after, *refs):
    lengths_ref, cot_ref = refs[:2]
    pack_refs = refs[2:6]
    send_ref, up_ref, cot_buf, up_buf, send_buf, pack_ref, sems, pack_sem = refs[6 + after :]
    layers = (high_at, high_at - 1)
    fetch_packs(layers, pack_refs, pack_ref, pack_sem)
    mine = lax.axis_index("section")
    branch = lax.axis_index("branch")
    at = pl.multiple_of(mine * COLS, COLS)
    copy = pltpu.make_async_copy(cot_ref.at[:, :, pl.ds(at, COLS)], cot_buf, sems.at[3])
    copy.start()
    wait_packs(layers, pack_refs, pack_ref, pack_sem)
    ready = [[Layer(pack_ref, at, family) for at in layers] for family in range(FAMILIES)]
    copy.wait()
    copies = []
    for family in range(FAMILIES):
        slot = jnp.clip(branch - BRANCHES // 2, 0, BRANCHES // 2 - 1)
        limit = jnp.where(branch >= BRANCHES // 2, lengths_ref[family, slot], ROWS)

        def upper_at(rows):
            at = lane_ids((CHUNK, ROWS))
            value = jnp.where(at < limit, jnp.transpose(cot_buf[family, :, rows].astype(F32)), 0.0)
            up_buf[family, rows, :] = value.astype(BF16)
            return value

        phase_a(family, upper_at, *ready[family], send_buf)
        heads = pl.ds(family * GROUP, GROUP)
        copies.append(pltpu.make_async_copy(send_buf.at[heads], send_ref.at[heads], sems.at[family]))
        copies[-1].start()
    copies.append(pltpu.make_async_copy(up_buf, up_ref, sems.at[2]))
    copies[-1].start()
    for copy in copies:
        copy.wait()


def later_kernel(high_at, goes_on, after, *refs):
    pack_refs = refs[:4]
    up_ref, end_ref = refs[4:6]
    refs = refs[6 + after :]
    grad_refs, keep_refs = refs[0:4], refs[4:6]
    rest = refs[6:]
    if goes_on:
        send_ref, grad_buf, up_buf, end_buf, pack_ref, grad_sem, keep_sem, in_sem, pack_sem, send_buf, send_sem = rest
    else:
        grad_buf, up_buf, end_buf, pack_ref, grad_sem, keep_sem, in_sem, pack_sem = rest
    layers = range(high_at, high_at - (4 if goes_on else 2), -1)
    fetch_packs(layers[:2], pack_refs, pack_ref, pack_sem)
    ins = [
        pltpu.make_async_copy(up_ref, up_buf, in_sem.at[0]),
        pltpu.make_async_copy(end_ref, end_buf, in_sem.at[1]),
    ]
    for copy in ins:
        copy.start()
    fetch_packs(layers[2:], pack_refs, pack_ref, pack_sem)
    mine = lax.axis_index("section")
    wait_packs(layers[:2], pack_refs, pack_ref, pack_sem)
    ready = {at: Layer(pack_ref, high_at - at[0], at[1]) for at in ((0, 0), (0, 1))}
    for copy in ins:
        copy.wait()
    for side in range(2):
        layer_at = high_at - side
        for family in range(FAMILIES):

            def upper_at(rows):
                if side == 0:
                    return up_buf[family, rows, :].astype(F32)
                return grad_buf[0, family, rows, :].astype(F32)

            def put_grad(rows, value):
                grad_buf[side, family, rows, :] = value

            layer = ready.get((side, family)) or Layer(pack_ref, layer_at, family)
            phase_b(family, side, layer, upper_at, end_buf, put_grad)
        ahead = lax.rem(layer_at - mine + SECTIONS, SECTIONS)
        for k in range(SECTIONS):

            @pl.when(ahead == k)
            def _():
                pltpu.make_async_copy(grad_buf.at[side], grad_refs[k], grad_sem.at[side]).start()

    copies = [pltpu.make_async_copy(grad_buf.at[side], keep_refs[side], keep_sem.at[side]) for side in range(2)]
    for copy in copies:
        copy.start()
    if goes_on:
        wait_packs(layers[2:], pack_refs, pack_ref, pack_sem)
        for family in range(FAMILIES):

            def upper_at(rows):
                return grad_buf[1, family, rows, :].astype(F32)

            high = Layer(pack_ref, high_at - 2, family)
            low = Layer(pack_ref, high_at - 3, family)
            phase_a(family, upper_at, high, low, send_buf)
            heads = pl.ds(family * GROUP, GROUP)
            copies.append(pltpu.make_async_copy(send_buf.at[heads], send_ref.at[heads], send_sem.at[family]))
            copies[-1].start()
    for copy in copies:
        copy.wait()
    for side in range(2):
        pltpu.make_async_copy(grad_buf.at[side], grad_refs[0], grad_sem.at[side]).wait()


def other_kernel(high_at, sides, want, after, *refs):
    pack_refs, up_refs, end_ref, saved_refs = refs[:4], refs[4:6], refs[6], refs[7:11]
    refs = refs[11:]
    final = want == ("grads",)
    if final:
        held_refs, steps_ref, refs = refs[0:2], refs[2], refs[3:]
    elif len(sides) == 2:
        small_refs, refs = refs[0:2], refs[2:]
    refs = refs[after:]
    part_refs, refs = (refs[:4], refs[4:]) if final else (refs[:1], refs[1:])
    if not final:
        rate_ref, refs = refs[0], refs[1:]
    saved_buf, up_buf, end_buf, part_buf, pack_ref = refs[:5]
    saved_sem, up_sem, part_sem, end_sem, pack_sem = refs[5:]
    mine = lax.axis_index("section")
    layers = [high_at - side for side in sides]
    fetch_packs(layers, pack_refs, pack_ref, pack_sem)
    ends = pltpu.make_async_copy(end_ref, end_buf, end_sem.at[0])
    ends.start()
    for side in sides:
        away = lax.rem(mine - (high_at - side) + SECTIONS, SECTIONS)
        pltpu.make_async_copy(up_refs[side], up_buf.at[side], up_sem.at[side]).start()
        for k in range(SECTIONS):

            @pl.when(away == k)
            def _():
                pltpu.make_async_copy(saved_refs[k], saved_buf.at[side], saved_sem.at[side]).start()

    def hand_on(source, layer_at):
        to = [part.at[pl.ds(0, GRAD_ROWS)] for part in part_refs] if final else part_refs
        copies = [pltpu.make_async_copy(source, part, part_sem.at[layer_at]) for part in to]
        if final:
            ahead = lax.rem(layer_at - mine + SECTIONS, SECTIONS)
            for k in range(SECTIONS):

                @pl.when(ahead == k)
                def _():
                    copies[k].start()
        else:
            copies[0].start()
        moved.append(copies[0])

    moved = []
    steps = slice(FAMILIES * ROWS, GRAD_ROWS)
    if final:
        for side in range(2):
            hand_on(held_refs[side], high_at + 2 - side)
            pltpu.make_async_copy(steps_ref.at[side], part_buf.at[side, steps], end_sem.at[1 + side]).start()
    wait_packs(layers, pack_refs, pack_ref, pack_sem)
    ready = [Layer(pack_ref, layers[0], family) for family in range(FAMILIES)]
    ends.wait()
    smalls_of = []
    for side in sides:
        pltpu.make_async_copy(up_refs[side], up_buf.at[side], up_sem.at[side]).wait()
        pltpu.make_async_copy(saved_refs[0], saved_buf.at[side], saved_sem.at[side]).wait()
        smalls = jnp.zeros((GROUP, LANES), F32)
        for family in range(FAMILIES):

            def upper_at(rows):
                return up_buf[side, family, rows, :].astype(F32)

            layer = ready[family] if side == sides[0] else Layer(pack_ref, high_at - side, family)
            grads, grad_step, small = phase_c(family, side, layer, upper_at, saved_buf.at[side], end_buf, want)
            if "grads" in want:
                part_buf[side, family * ROWS : (family + 1) * ROWS, :] = grads.astype(BF16)
            if "rates" in want:
                below = FAMILIES * ROWS + family * GROUP
                part_buf[side, below : below + GROUP, :] = grad_step.astype(BF16)
                smalls = smalls + small
        if final:
            pltpu.make_async_copy(steps_ref.at[side], part_buf.at[side, steps], end_sem.at[1 + side]).wait()
        if "grads" in want:
            hand_on(part_buf.at[side], high_at - side)
        else:
            moved.append(pltpu.make_async_copy(part_buf.at[side, steps], part_refs[0].at[side], part_sem.at[side]))
            moved[-1].start()
        smalls_of.append(smalls)
    if final:
        pass
    elif len(sides) == 2:
        blocks = smalls_of[::-1] + [small_refs[1][...], small_refs[0][...]]
        turned = jnp.transpose(jnp.concatenate(blocks + [jnp.zeros((STATE, LANES), F32)], axis=0))
        row = turned[0:1] + pltpu.roll(turned[1:2], STATE, 1)
        rate_ref[...] = jnp.broadcast_to(row[None], (BRANCHES, 1, LANES))
    else:
        rate_ref[...] = smalls_of[0]
    for copy in moved:
        copy.wait()


def chain_kernel(*refs):
    got_ref, end_ref = refs[0], refs[-1]
    lanes = lane_ids((STATE // 2, LANES))
    prompt = BRANCHES // 2
    fork = jnp.zeros((HEADDIM, LANES), F32)
    for at in range(prompt, BRANCHES):
        fork = fork + got_ref[at, 0:HEADDIM, :].astype(F32)
    plain, extra = fork, jnp.zeros((HEADDIM, LANES), F32)
    blank = jnp.zeros((STATE, LANES), F32)
    for at in range(prompt - 1, -1, -1):
        tail = got_ref[at, 96:112, :].astype(F32)
        total = tail[0:1, :] + tail[1:2, :]
        plain = total * plain
        extra = total * extra
        end_ref[at, :, :] = (plain + extra).astype(BF16)
        if at == 0:
            break
        packed = got_ref[at, HEADDIM : HEADDIM + 32, :].astype(F32)
        turned = pltpu.roll(packed, STATE, 1)
        move = jnp.concatenate(
            [jnp.where(lanes >= STATE, turned, 0.0), jnp.where(lanes >= STATE, packed, 0.0), blank], axis=0
        ).astype(BF16)
        extra = extra + dot2(split(plain), move, NN)
        plain = plain + got_ref[at, 0:HEADDIM, :].astype(F32)
    for at in range(prompt, BRANCHES):
        end_ref[at, :, :] = jnp.zeros((HEADDIM, LANES), BF16)


def pack_kernel(*refs):
    sources, decay_ref, gain_ref = refs[0:3], refs[3], refs[4]
    pack_refs = refs[5:9]
    in_ref, out_ref, step_ref, both_ref, rate_ref, sems, send_sems = refs[9:]
    copies = [
        pltpu.make_async_copy(source.at[0], to, sems.at[at])
        for at, (source, to) in enumerate(zip(sources, (in_ref, out_ref, step_ref)))
    ]
    for copy in copies:
        copy.start()
    mine = lax.axis_index("section")
    base = FAMILIES * ROWS
    rate_ref[0] = jnp.transpose(jnp.broadcast_to(decay_ref[...], (LANES, SECTIONS * GROUP)))
    rate_ref[1] = jnp.transpose(jnp.broadcast_to(gain_ref[...], (LANES, SECTIONS * GROUP)))
    for copy in copies:
        copy.wait()
    for k in range(SECTIONS):
        heads = pl.ds(pl.multiple_of(lax.rem(mine + k, SECTIONS) * GROUP, GROUP), GROUP)
        for family in range(FAMILIES):
            both_ref[k, base + family * GROUP : base + (family + 1) * GROUP, :] = step_ref[family, heads, :]
        both_ref[k, base + 2 * GROUP : base + 3 * GROUP, :] = rate_ref[0, heads, :]
        both_ref[k, base + 3 * GROUP : base + 4 * GROUP, :] = rate_ref[1, heads, :]
    for family in range(FAMILIES):
        turned = jnp.transpose(jnp.concatenate([in_ref[family], out_ref[family]], axis=0))
        for k in range(SECTIONS):
            both_ref[k, family * ROWS : (family + 1) * ROWS, :] = turned
    copies = []
    for k in range(SECTIONS):
        copies.append(pltpu.make_async_copy(both_ref.at[k], pack_refs[k], send_sems.at[k]))
        copies[-1].start()
    for copy in copies:
        copy.wait()


def sort_kernel(at_ref, *refs):
    for x_ref, s_ref, o_ref in zip(refs[0:4], refs[4:8], refs[8:12]):
        o_ref[0, 0:COLS] = jnp.transpose(x_ref[0, 0])
        whole = s_ref[0, 0, 0].reshape(COLS, STATE)
        o_ref[0, COLS:SAVED_ROWS] = jnp.concatenate([whole[: COLS // 2], whole[COLS // 2 :]], axis=1).astype(BF16)


def fetch_home(early, late, to, sems):
    mine = lax.axis_index("section")
    for is_early, pieces in ((True, early), (False, late)):

        @pl.when((mine >= 2) == is_early)
        def _():
            for k in range(SECTIONS):
                source = lax.rem(mine - k + SECTIONS, SECTIONS)
                pltpu.make_async_copy(pieces[k], to(source), sems.at[k]).start()

    for k in range(SECTIONS):
        pltpu.make_async_copy(early[k], to(k), sems.at[k]).wait()


def home_small_kernel(*refs):
    piece_refs = refs[:4]
    in_ref, out_ref, step_ref, decay_ref, skip_ref, part_ref, part_sem = refs[-7:]
    mine = lax.axis_index("section")
    for k in range(SECTIONS):
        source = lax.rem(mine - k + SECTIONS, SECTIONS)
        pltpu.make_async_copy(piece_refs[k], part_ref.at[source], part_sem.at[k]).start()
    for k in range(SECTIONS):
        pltpu.make_async_copy(piece_refs[k], part_ref.at[k], part_sem.at[k]).wait()
    for family in range(FAMILIES):
        rows = slice(family * ROWS, (family + 1) * ROWS)
        total = part_ref[0, rows, :].astype(F32)
        for k in range(1, SECTIONS):
            total = total + part_ref[k, rows, :].astype(F32)
        turned = jnp.transpose(total)
        in_ref[0, family] = turned[0:STATE]
        out_ref[0, family] = turned[STATE:]
        below = FAMILIES * ROWS + family * GROUP
        for k in range(SECTIONS):
            step_ref[0, family, k * GROUP : (k + 1) * GROUP, :] = part_ref[k, below : below + GROUP, :].astype(F32)
    section = (lane_ids((8, LANES)) & (STATE - 1)) >> 4
    total = jnp.zeros((8, LANES), F32)
    for at in range(SECTIONS):
        tail = part_ref[at, GRAD_ROWS:HOME_ROWS, :].astype(F32)
        row = jnp.broadcast_to(tail[0:1] + tail[1:2], (8, LANES))
        shift = lax.rem(at - mine + SECTIONS, SECTIONS) * GROUP
        ahead, behind = pltpu.roll(row, shift, 1), pltpu.roll(row, shift + STATE, 1)
        low = (lane_ids((8, LANES)) & (STATE - 1)) >= shift
        total = jnp.where(section == at, jnp.where(low, ahead, behind), total)
    decay_ref[...] = total[0:1, 0:STATE]
    skip_ref[...] = total[0:1, STATE:]


def home_grad_kernel(*refs):
    early, late = refs[0:4], refs[4:8]
    grad_ref, turned_buf, grad_buf, grad_sem, out_sem = refs[8:]
    fetch_home(early, late, lambda source: turned_buf.at[source], grad_sem)
    outs = []
    for source in range(SECTIONS):
        cols = slice(source * COLS, (source + 1) * COLS)
        for family in range(FAMILIES):
            grad_buf[family, :, cols] = jnp.transpose(turned_buf[source, family])
        outs.append(
            pltpu.make_async_copy(
                grad_buf.at[:, :, pl.ds(source * COLS, COLS)],
                grad_ref.at[0, :, :, pl.ds(source * COLS, COLS)],
                out_sem.at[source],
            )
        )
        outs[-1].start()
    for out in outs:
        out.wait()


def rate_sum_kernel(scale, *refs):
    got_ref, part_refs, buf, sems = refs[0], refs[5:9], refs[9], refs[10]
    total = got_ref[0]
    for at in range(1, BRANCHES):
        total = total + got_ref[at]
    total = jnp.broadcast_to(total * scale, (16, LANES))
    high = total.astype(BF16).astype(F32)
    place = lax.broadcasted_iota(jnp.int32, (16, LANES), 0)
    buf[...] = jnp.where(place == 0, high, jnp.where(place == 1, total - high, 0.0)).astype(BF16)
    copies = [
        pltpu.make_async_copy(buf, part_refs[to].at[pl.ds(GRAD_ROWS, 16)], sems.at[to]) for to in range(SECTIONS)
    ]
    for copy in copies:
        copy.start()
    for copy in copies:
        copy.wait()


ALL = ("grads", "rates")
VM = pl.BlockSpec(memory_space=pltpu.VMEM)
SM = pl.BlockSpec(memory_space=pltpu.SMEM)
ANY = pl.BlockSpec(memory_space=pl.ANY)
HBM = pl.BlockSpec(memory_space=pltpu.HBM)
PARAMS = pltpu.CompilerParams(vmem_limit_bytes=VMEM_LIMIT)
SMALL_PARAMS = pltpu.CompilerParams(vmem_limit_bytes=32 * 1024 * 1024)


PACKS = pltpu.VMEM((SECTIONS, PACK_ROWS, LANES), F32)


def shape(dims, dtype):
    return jax.ShapeDtypeStruct(dims, dtype)


def cost(flops):
    return pl.CostEstimate(flops=flops, bytes_accessed=4_000_000, transcendentals=0)


def sems(count):
    return pltpu.SemaphoreType.DMA((count,))


def pack_small(state_in, state_out, step_size, decay_rate, skip_gain):
    turned = [jnp.transpose(value, (0, 1, 3, 2)) for value in (state_in, state_out, step_size)]
    return pl.pallas_call(
        pack_kernel,
        out_shape=[shape((PACK_ROWS, LANES), F32)] * SECTIONS,
        in_specs=[ANY] * 3 + [VM] * 2,
        out_specs=[HBM] * SECTIONS,
        scratch_shapes=[
            pltpu.VMEM((FAMILIES, STATE, ROWS), F32),
            pltpu.VMEM((FAMILIES, STATE, ROWS), F32),
            pltpu.VMEM((FAMILIES, SECTIONS * GROUP, ROWS), F32),
            pltpu.VMEM((SECTIONS, PACK_ROWS, LANES), F32),
            pltpu.VMEM((2, SECTIONS * GROUP, LANES), F32),
            sems(3),
            sems(4),
        ],
        compiler_params=PARAMS,
        name="pack_small",
    )(*turned, decay_rate, skip_gain)


def sort_heads(layer_input, saved_states):
    mine = jnp.full((1,), lax.axis_index("section"), jnp.int32)

    def x_spec(k):
        return pl.BlockSpec(
            (1, 1, ROWS, COLS), lambda f, at: (0, f, 0, lax.rem(at[0] + k, SECTIONS))
        )

    def s_spec(k):
        return pl.BlockSpec(
            (1, 1, 1, GROUP, HEADDIM, STATE), lambda f, at: (0, f, 0, lax.rem(at[0] + k, SECTIONS), 0, 0)
        )

    return pl.pallas_call(
        sort_kernel,
        grid_spec=pltpu.PrefetchScalarGridSpec(
            num_scalar_prefetch=1,
            grid=(FAMILIES,),
            in_specs=[x_spec(k) for k in range(SECTIONS)] + [s_spec(k) for k in range(SECTIONS)],
            out_specs=[pl.BlockSpec((1, SAVED_ROWS, LANES), lambda f, at: (f, 0, 0))] * SECTIONS,
        ),
        out_shape=[shape((FAMILIES, SAVED_ROWS, LANES), BF16)] * SECTIONS,
        compiler_params=PARAMS,
        cost_estimate=cost(4_000_000_000),
        name="sort_heads",
    )(mine, *([layer_input] * SECTIONS), *([saved_states] * SECTIONS))


def first_phase(high_at, lengths, cotangent, packs, after):
    return pl.pallas_call(
        functools.partial(first_kernel, high_at, len(after)),
        out_shape=[
            shape((BRANCHES, SEND_ROWS, LANES), BF16),
            shape((FAMILIES, COLS, ROWS), BF16),
        ],
        in_specs=[SM] + [ANY] * (5 + len(after)),
        out_specs=[HBM, HBM],
        scratch_shapes=[
            pltpu.VMEM((FAMILIES, ROWS, COLS), BF16),
            pltpu.VMEM((FAMILIES, COLS, ROWS), BF16),
            pltpu.VMEM((BRANCHES, SEND_ROWS, LANES), BF16),
            PACKS,
            sems(4),
            sems(4),
        ],
        compiler_params=PARAMS,
        name="first_phase",
    )(lengths, cotangent, *packs, *after)


def later_phase(high_at, goes_on, packs, upstream, ends, after):
    outs = [shape((FAMILIES, COLS, ROWS), BF16)] * 4
    outs += [shape((FAMILIES, COLS, ROWS), BF16)] * 2
    scratch = [
        pltpu.VMEM((2, FAMILIES, COLS, ROWS), BF16),
        pltpu.VMEM((FAMILIES, COLS, ROWS), BF16),
        pltpu.VMEM((BRANCHES, HEADDIM, LANES), BF16),
        PACKS,
        sems(2),
        sems(2),
        sems(2),
        sems(4),
    ]
    if goes_on:
        outs += [shape((BRANCHES, SEND_ROWS, LANES), BF16)]
        scratch += [pltpu.VMEM((BRANCHES, SEND_ROWS, LANES), BF16), sems(2)]
    return pl.pallas_call(
        functools.partial(later_kernel, high_at, goes_on, len(after)),
        out_shape=outs,
        in_specs=[ANY] * (6 + len(after)),
        out_specs=[HBM] * len(outs),
        scratch_shapes=scratch,
        compiler_params=PARAMS,
        name="later_phase",
    )(*packs, upstream, ends, *after)


def other_phase(high_at, sides, want, packs, ups, ends, saved, held, after):
    if want == ("grads",):
        outs = [shape((HOME_ROWS, LANES), BF16)] * SECTIONS
        extra, specs = [ANY] * 3, [HBM] * SECTIONS
    elif len(sides) == 2:
        outs = [shape((2, FAMILIES * GROUP, LANES), BF16), shape((BRANCHES, 1, LANES), F32)]
        extra, specs = [VM] * 2, [HBM, VM]
    else:
        outs = [shape((GRAD_ROWS, LANES), BF16), shape((GROUP, LANES), F32)]
        extra, specs = [], [HBM, VM]
    return pl.pallas_call(
        functools.partial(other_kernel, high_at, sides, want, len(after)),
        out_shape=outs,
        in_specs=[ANY] * 11 + extra + [ANY] * len(after),
        out_specs=specs,
        scratch_shapes=[
            pltpu.VMEM((2, FAMILIES, SAVED_ROWS, LANES), BF16),
            pltpu.VMEM((2, FAMILIES, COLS, ROWS), BF16),
            pltpu.VMEM((BRANCHES, HEADDIM, LANES), BF16),
            pltpu.VMEM((2, GRAD_ROWS, LANES), BF16),
            PACKS,
            sems(2),
            sems(2),
            sems(4),
            sems(3),
            sems(4),
        ],
        compiler_params=PARAMS,
        cost_estimate=cost(6_000_000_000 if len(want) == 2 else 5_000_000_000),
        name="other_phase",
    )(*packs, *ups, ends, *saved, *held, *after)


def chain(got, after):
    return pl.pallas_call(
        chain_kernel,
        out_shape=shape((BRANCHES, HEADDIM, LANES), BF16),
        in_specs=[VM] + [ANY] * len(after),
        out_specs=VM,
        compiler_params=SMALL_PARAMS,
        name="chain",
    )(got, *after)


def home_small(parts, after):
    return pl.pallas_call(
        home_small_kernel,
        out_shape=[
            shape((1, FAMILIES, STATE, ROWS), F32),
            shape((1, FAMILIES, STATE, ROWS), F32),
            shape((1, FAMILIES, SECTIONS * GROUP, ROWS), F32),
            shape((1, SECTIONS * GROUP), F32),
            shape((1, SECTIONS * GROUP), F32),
        ],
        in_specs=[ANY] * (4 + len(after)),
        out_specs=[VM] * 5,
        scratch_shapes=[pltpu.VMEM((SECTIONS, HOME_ROWS, LANES), BF16), sems(SECTIONS)],
        compiler_params=PARAMS,
        name="home_small",
    )(*parts, *after)


def home_grad(early, late):
    return pl.pallas_call(
        home_grad_kernel,
        out_shape=shape((1, FAMILIES, ROWS, SECTIONS * COLS), BF16),
        in_specs=[ANY] * 8,
        out_specs=HBM,
        scratch_shapes=[
            pltpu.VMEM((SECTIONS, FAMILIES, COLS, ROWS), BF16),
            pltpu.VMEM((FAMILIES, ROWS, SECTIONS * COLS), BF16),
            sems(SECTIONS),
            sems(SECTIONS),
        ],
        compiler_params=PARAMS,
        cost_estimate=cost(3_000_000_000),
        name="home_grad",
    )(*early, *late)


def rate_sum(got, parts, scale):
    return pl.pallas_call(
        functools.partial(rate_sum_kernel, scale),
        out_shape=[shape((HOME_ROWS, LANES), BF16)] * SECTIONS,
        in_specs=[VM] + [HBM] * SECTIONS,
        out_specs=[HBM] * SECTIONS,
        scratch_shapes=[pltpu.VMEM((16, LANES), BF16), sems(SECTIONS)],
        input_output_aliases={1 + k: k for k in range(SECTIONS)},
        compiler_params=PARAMS,
        name="rate_sum",
    )(got, *parts)


def swap(value, axis):
    return lax.all_to_all(value, axis, 0, 0, tiled=True)


def send_on(value, k, targets):
    pairs = [(i, (i + k) % SECTIONS) for i in range(SECTIONS) if (i + k) % SECTIONS in targets]
    return lax.ppermute(value, "section", pairs)


def send_home(pieces, targets):
    return [pieces[0]] + [send_on(pieces[k], k, targets) for k in range(1, SECTIONS)]


def exchange(send, after):
    return swap(chain(swap(send, "branch"), after), "branch")


def shards(
    layer_input,
    cotangent,
    state_in,
    state_out,
    step_size,
    saved_states,
    decay_rate,
    skip_gain,
    lengths,
):
    grad_scale = 1.0 / math.sqrt(FAMILIES * ROWS * BRANCHES * HEADDIM)
    everyone = tuple(range(SECTIONS))
    packs = pack_small(state_in, state_out, step_size, decay_rate, skip_gain)
    packs = [packs[0]] + [send_on(packs[k], k, everyone) for k in range(1, SECTIONS)]
    saved = sort_heads(layer_input, saved_states)
    top, upstream = first_phase(3, lengths, cotangent, packs, [saved[0]])
    saved = [saved[0]] + [send_on(saved[k], k, everyone) for k in range(1, SECTIONS)]
    ends = exchange(top, [])
    early = later_phase(3, True, packs, upstream, ends, [saved[1], saved[3]])
    early_grads = send_home(early[:4], (2, 3))
    ups = (upstream, early[4])
    part_a, small_a = other_phase(3, (0,), ALL, packs, ups, ends, saved, [], [])
    next_ends = exchange(early[6], [])
    part_b, small_b = other_phase(3, (1,), ALL, packs, ups, ends, saved, [], [])
    late = later_phase(1, False, packs, early[5], next_ends, early_grads[1:] + [part_b])
    late_grads = send_home(late[:4], (0, 1))
    ups = (early[5], late[4])
    steps, rates = other_phase(1, (0, 1), ("rates",), packs, ups, next_ends, saved, [small_a, small_b], [])
    parts = other_phase(1, (0, 1), ("grads",), packs, ups, next_ends, saved, [part_a, part_b, steps], [])
    parts = send_home(rate_sum(swap(rates, "branch"), parts, grad_scale), everyone)
    grad = home_grad(early_grads, late_grads)
    *others, decay_sum, skip_sum = home_small(parts, [grad])
    others = tuple(jnp.transpose(value, (0, 1, 3, 2)) for value in others)
    return (grad,) + others + (decay_sum, skip_sum)


def solution(mesh):
    placed = (
        P("section", None, "branch", None),
        P(None, "branch", None),
        P("section", None, "branch", None),
        P("section", None, "branch", None),
        P("section", None, "branch", None),
        P("section", None, "branch", None, None, None),
        P("section", None),
        P("section", None),
        P(),
    )
    return jax.shard_map(
        shards,
        mesh=mesh,
        in_specs=placed,
        out_specs=(
            P("section", None, "branch", None),
            P("section", None, "branch", None),
            P("section", None, "branch", None),
            P("section", None, "branch", None),
            P("section", None),
            P("section", None),
        ),
        check_vma=False,
    )
```

```python
import functools
import math

import jax
import jax.numpy as jnp
from jax import lax
from jax.experimental import pallas as pl
from jax.experimental.pallas import tpu as pltpu
from jax.sharding import PartitionSpec as P

F32 = jnp.float32
BF16 = jnp.bfloat16

SECTIONS = 4
FAMILIES = 2
ROWS = 128
STATE = 64
HEADDIM = 64
GROUP = 16
COLS = GROUP * HEADDIM
LANES = 128
CHUNK = 512
PER_CHUNK = CHUNK // HEADDIM
BRANCHES = 32
SEND_ROWS = 112
PACK_ROWS = FAMILIES * ROWS + 4 * GROUP
GRAD_ROWS = FAMILIES * (ROWS + GROUP)
HOME_ROWS = GRAD_ROWS + 16
SAVED_ROWS = COLS + COLS // 2
VMEM_LIMIT = 63 * 1024 * 1024

NN = (((1,), (0,)), ((), ()))
NT = (((1,), (1,)), ((), ()))
TN = (((0,), (0,)), ((), ()))


def dot(a, b, dims):
    return lax.dot_general(a, b, dims, preferred_element_type=F32)


def split(a):
    high = a.astype(BF16)
    return high, (a - high.astype(F32)).astype(BF16)


def dot3(a, b, dims):
    return dot(a[0], b[0], dims) + dot(a[1], b[0], dims) + dot(a[0], b[1], dims)


def dot2(a, b, dims):
    return dot(a[0], b, dims) + dot(a[1], b, dims)


def lane_ids(shape):
    return lax.broadcasted_iota(jnp.int32, shape, len(shape) - 1)


def half(rolled, plain, side):
    lanes = lane_ids(plain.shape)
    if side == 0:
        return jnp.where(lanes < STATE, plain, 0.0)
    return jnp.where(lanes >= STATE, rolled, 0.0)


def by_head(value, chunk):
    first = chunk * PER_CHUNK
    return jnp.concatenate(
        [jnp.broadcast_to(value[first + at : first + at + 1, :], (HEADDIM, LANES)) for at in range(PER_CHUNK)], axis=0
    )


def head_sums(value):
    return jnp.sum(value.reshape(PER_CHUNK, HEADDIM, LANES), axis=1)


def fetch_packs(layers, pack_refs, pack_buf, sems):
    mine = lax.axis_index("section")
    for at in layers:
        away = lax.rem(mine - at + SECTIONS, SECTIONS)
        for k in range(SECTIONS):

            @pl.when(away == k)
            def _():
                pltpu.make_async_copy(pack_refs[k], pack_buf.at[at], sems.at[at]).start()


def wait_packs(layers, pack_refs, pack_buf, sems):
    for at in layers:
        pltpu.make_async_copy(pack_refs[0], pack_buf.at[at], sems.at[at]).wait()


def wide(a, b):
    return jnp.concatenate([a, b], axis=1)


def folded(value):
    return value[:, 0:LANES] + value[:, LANES:]


class Layer:
    def __init__(self, pack_ref, layer, family):
        base = FAMILIES * ROWS
        both = pack_ref[layer, family * ROWS : (family + 1) * ROWS, :]
        turned = pltpu.roll(both, STATE, 1)
        self.b = (half(both, both, 0), half(turned, turned, 1))
        self.c = (half(turned, turned, 0), half(both, both, 1))
        self.step = pack_ref[layer, base + family * GROUP : base + (family + 1) * GROUP, :]
        self.decay = pack_ref[layer, base + 2 * GROUP : base + 3 * GROUP, :]
        gain = pack_ref[layer, base + 3 * GROUP : base + 4 * GROUP, :]
        row = lax.broadcasted_iota(jnp.int32, (ROWS, ROWS), 0)
        col = lax.broadcasted_iota(jnp.int32, (ROWS, ROWS), 1)
        self.row, self.col = row, col
        upper = jnp.where(row <= col, 1.0, 0.0).astype(BF16)
        drop = -self.decay * self.step
        first = drop.astype(BF16)
        rest = drop - first.astype(F32)
        second = rest.astype(BF16)
        third = (rest - second.astype(F32)).astype(BF16)
        logs = dot(first, upper, NN) + dot(second, upper, NN) + dot(third, upper, NN)
        carried = jnp.exp(logs)
        scale = self.step * jnp.exp(-logs)
        total = jnp.sum(jnp.where(lane_ids(carried.shape) == ROWS - 1, carried, 0.0), axis=1, keepdims=True)
        self.total = jnp.broadcast_to(total, (GROUP, LANES))
        self.carried, self.scale, self.gain = carried, scale, gain
        read = dot3(split(self.c[0]), split(self.b[0]), NT)
        self.read = jnp.where(row >= col, read, 0.0)


def phase_a(family, upper_at, high, low, send_ref):
    c_pair = split(jnp.concatenate([high.c[0], low.c[1]], axis=0))
    c_both = split(low.c[0] + low.c[1])
    c_pair_wide, c_both_wide = wide(*c_pair), wide(*c_both)
    b_turned = jnp.transpose(high.b[0])[0:STATE]
    b_tile = jnp.concatenate([b_turned] * PER_CHUNK, axis=0)
    read = high.read.astype(BF16)
    mixed = low.carried * high.scale
    lanes = lane_ids((STATE // 2, LANES))
    for chunk in range(COLS // CHUNK):
        rows = slice(chunk * CHUNK, (chunk + 1) * CHUNK)
        upstream = upper_at(rows)
        hat2 = split(by_head(high.carried, chunk) * upstream)
        pulled = dot(hat2[0], read, NN)
        low_up = by_head(high.gain, chunk) * upstream + by_head(high.scale, chunk) * pulled
        low_hat2 = split(by_head(low.carried, chunk) * low_up)
        both = tuple(jnp.concatenate([a, b], axis=1) for a, b in zip(hat2, low_hat2))
        begin = (folded(dot(both[0], c_pair_wide, NN)) + dot(both[1], c_pair[0], NN)).astype(BF16)
        response = split(by_head(mixed, chunk) * b_tile)
        move = folded(dot(response[0], c_both_wide, NN)) + dot(response[1], c_both[0], NN)
        for inner in range(PER_CHUNK):
            head = family * GROUP + chunk * PER_CHUNK + inner
            top = inner * HEADDIM
            send_ref[head, 0:HEADDIM, :] = begin[top : top + HEADDIM, :]
            first = move[top : top + 32, :]
            second = move[top + 32 : top + 64, :]
            send_ref[head, HEADDIM : HEADDIM + 32, :] = jnp.where(lanes < STATE, first, second).astype(BF16)
    totals = jnp.where(lane_ids((GROUP, LANES)) < STATE, high.total, low.total)
    total_high = totals.astype(BF16).astype(F32)
    total_low = totals - total_high
    place = lax.broadcasted_iota(jnp.int32, (16, LANES), 0)
    for inner in range(GROUP):
        one = jnp.broadcast_to(total_high[inner : inner + 1, :], (16, LANES))
        two = jnp.broadcast_to(total_low[inner : inner + 1, :], (16, LANES))
        block = jnp.where(place == 0, one, jnp.where(place == 1, two, 0.0))
        send_ref[family * GROUP + inner, 96:112, :] = block.astype(BF16)


def phase_b(family, side, layer, upper_at, end_ref, put_grad):
    b2 = split(jnp.transpose(layer.b[side]))
    read = layer.read.astype(BF16)
    weights = jnp.concatenate([wide(read, jnp.zeros_like(read)), wide(*b2)], axis=0)
    for chunk in range(COLS // CHUNK):
        rows = slice(chunk * CHUNK, (chunk + 1) * CHUNK)
        upstream = upper_at(rows)
        first = family * GROUP + chunk * PER_CHUNK
        ends = end_ref[first : first + PER_CHUNK].reshape(CHUNK, LANES)
        hat = (by_head(layer.carried, chunk) * upstream).astype(BF16)
        pulled = folded(dot(wide(hat, ends), weights, NN))
        grad = by_head(layer.gain, chunk) * upstream + by_head(layer.scale, chunk) * pulled
        put_grad(rows, grad.astype(BF16))


def phase_c(family, side, layer, upper_at, saved_ref, end_ref, want):
    grads = grad_step = small = None
    b_one, c_one = layer.b[side].astype(BF16), layer.c[side].astype(BF16)
    b_turned = jnp.transpose(layer.b[side]).astype(BF16)
    read = layer.read.astype(BF16)
    weights = jnp.concatenate([jnp.transpose(layer.read), jnp.transpose(layer.c[side])], axis=0).astype(BF16)
    pulls = jnp.concatenate([wide(read, jnp.zeros_like(read)), wide(b_turned, b_turned)], axis=0)
    left = jnp.zeros((ROWS, ROWS + LANES), F32)
    grad_in = jnp.zeros((ROWS, LANES), F32)
    flow, worth, ending, skips = [], [], [], []
    lanes = lane_ids((CHUNK, LANES))
    for chunk in range(COLS // CHUNK):
        rows = slice(chunk * CHUNK, (chunk + 1) * CHUNK)
        upstream = upper_at(rows)
        x = saved_ref[family, rows, :].astype(F32)
        hat = by_head(layer.carried, chunk) * upstream
        hat_one = hat.astype(BF16)
        x_hat = by_head(layer.scale, chunk) * x
        x_one = x_hat.astype(BF16)
        first = family * GROUP + chunk * PER_CHUNK
        ends = end_ref[first : first + PER_CHUNK].reshape(CHUNK, LANES)
        top = COLS + chunk * CHUNK % (COLS // 2)
        packed = saved_ref[family, top : top + CHUNK, :].astype(F32)
        if (chunk * CHUNK < COLS // 2) != (side == 0):
            packed = pltpu.roll(packed, STATE, 1)
        saved = jnp.where((lanes < STATE) == (side == 0), packed, 0.0)
        x_saved = jnp.concatenate([x_one, saved.astype(BF16)], axis=1)
        if "grads" in want:
            left = left + dot(hat_one, x_saved, TN)
            grad_in = grad_in + dot(x_one, ends, TN)
        if "rates" not in want:
            continue
        both = dot(wide(hat_one, ends), pulls, NN)
        pulled, end_in = both[:, 0:LANES], both[:, LANES:]
        forward = dot(x_saved, weights, NN)
        x_pulled = x_hat * pulled
        worth.append(head_sums(x_pulled))
        flow.append(head_sums(hat * forward - x_pulled))
        ending.append(head_sums(x_hat * end_in + ends.astype(F32) * saved))
        skips.append(head_sums(x * upstream))
    if "grads" in want:
        pairs, grad_out = left[:, 0:ROWS], left[:, ROWS:]
        pairs = jnp.where(layer.row >= layer.col, pairs, 0.0).astype(BF16)
        grad_out = grad_out + dot(pairs, b_one, NN)
        grad_in = grad_in + dot(pairs, c_one, TN)
        lanes = lane_ids((ROWS, LANES))
        if side == 0:
            grads = jnp.where(lanes < STATE, grad_in, pltpu.roll(grad_out, STATE, 1))
        else:
            grads = jnp.where(lanes < STATE, pltpu.roll(grad_in, STATE, 1), grad_out)
    if "rates" in want:
        flow, worth, ending, skips = (jnp.concatenate(part, axis=0) for part in (flow, worth, ending, skips))
        later = jnp.where(layer.row >= layer.col, 1.0, 0.0).astype(BF16)
        rate = dot2(split(flow), later, NN) + jnp.sum(ending, axis=1, keepdims=True)
        grad_step = worth / layer.step - layer.decay * rate
        decay_part = jnp.sum(-layer.step * rate, axis=1, keepdims=True)
        skip_part = jnp.sum(skips, axis=1, keepdims=True)
        place = lane_ids((GROUP, LANES))
        small = jnp.where(place == 0, decay_part, jnp.where(place == 1, skip_part, 0.0))
    return grads, grad_step, small


def first_kernel(high_at, after, *refs):
    lengths_ref, cot_ref = refs[:2]
    pack_refs = refs[2:6]
    send_ref, up_ref, cot_buf, up_buf, send_buf, pack_ref, sems, pack_sem = refs[6 + after :]
    layers = (high_at, high_at - 1)
    fetch_packs(layers, pack_refs, pack_ref, pack_sem)
    mine = lax.axis_index("section")
    branch = lax.axis_index("branch")
    at = pl.multiple_of(mine * COLS, COLS)
    copy = pltpu.make_async_copy(cot_ref.at[:, :, pl.ds(at, COLS)], cot_buf, sems.at[3])
    copy.start()
    wait_packs(layers, pack_refs, pack_ref, pack_sem)
    ready = [[Layer(pack_ref, at, family) for at in layers] for family in range(FAMILIES)]
    copy.wait()
    copies = []
    for family in range(FAMILIES):
        slot = jnp.clip(branch - BRANCHES // 2, 0, BRANCHES // 2 - 1)
        limit = jnp.where(branch >= BRANCHES // 2, lengths_ref[family, slot], ROWS)

        def upper_at(rows):
            at = lane_ids((CHUNK, ROWS))
            value = jnp.where(at < limit, jnp.transpose(cot_buf[family, :, rows].astype(F32)), 0.0)
            up_buf[family, rows, :] = value.astype(BF16)
            return value

        phase_a(family, upper_at, *ready[family], send_buf)
        heads = pl.ds(family * GROUP, GROUP)
        copies.append(pltpu.make_async_copy(send_buf.at[heads], send_ref.at[heads], sems.at[family]))
        copies[-1].start()
    copies.append(pltpu.make_async_copy(up_buf, up_ref, sems.at[2]))
    copies[-1].start()
    for copy in copies:
        copy.wait()


def later_kernel(high_at, goes_on, after, *refs):
    pack_refs = refs[:4]
    up_ref, end_ref = refs[4:6]
    refs = refs[6 + after :]
    grad_refs, keep_refs = refs[0:4], refs[4:6]
    rest = refs[6:]
    if goes_on:
        send_ref, grad_buf, up_buf, end_buf, pack_ref, grad_sem, keep_sem, in_sem, pack_sem, send_buf, send_sem = rest
    else:
        grad_buf, up_buf, end_buf, pack_ref, grad_sem, keep_sem, in_sem, pack_sem = rest
    layers = range(high_at, high_at - (4 if goes_on else 2), -1)
    fetch_packs(layers[:2], pack_refs, pack_ref, pack_sem)
    ins = [
        pltpu.make_async_copy(up_ref, up_buf, in_sem.at[0]),
        pltpu.make_async_copy(end_ref, end_buf, in_sem.at[1]),
    ]
    for copy in ins:
        copy.start()
    fetch_packs(layers[2:], pack_refs, pack_ref, pack_sem)
    mine = lax.axis_index("section")
    wait_packs(layers[:2], pack_refs, pack_ref, pack_sem)
    ready = {at: Layer(pack_ref, high_at - at[0], at[1]) for at in ((0, 0), (0, 1))}
    for copy in ins:
        copy.wait()
    for side in range(2):
        layer_at = high_at - side
        for family in range(FAMILIES):

            def upper_at(rows):
                if side == 0:
                    return up_buf[family, rows, :].astype(F32)
                return grad_buf[0, family, rows, :].astype(F32)

            def put_grad(rows, value):
                grad_buf[side, family, rows, :] = value

            layer = ready.get((side, family)) or Layer(pack_ref, layer_at, family)
            phase_b(family, side, layer, upper_at, end_buf, put_grad)
        ahead = lax.rem(layer_at - mine + SECTIONS, SECTIONS)
        for k in range(SECTIONS):

            @pl.when(ahead == k)
            def _():
                pltpu.make_async_copy(grad_buf.at[side], grad_refs[k], grad_sem.at[side]).start()

    copies = [pltpu.make_async_copy(grad_buf.at[side], keep_refs[side], keep_sem.at[side]) for side in range(2)]
    for copy in copies:
        copy.start()
    if goes_on:
        wait_packs(layers[2:], pack_refs, pack_ref, pack_sem)
        for family in range(FAMILIES):

            def upper_at(rows):
                return grad_buf[1, family, rows, :].astype(F32)

            high = Layer(pack_ref, high_at - 2, family)
            low = Layer(pack_ref, high_at - 3, family)
            phase_a(family, upper_at, high, low, send_buf)
            heads = pl.ds(family * GROUP, GROUP)
            copies.append(pltpu.make_async_copy(send_buf.at[heads], send_ref.at[heads], send_sem.at[family]))
            copies[-1].start()
    for copy in copies:
        copy.wait()
    for side in range(2):
        pltpu.make_async_copy(grad_buf.at[side], grad_refs[0], grad_sem.at[side]).wait()


def other_kernel(high_at, sides, want, after, *refs):
    pack_refs, up_refs, end_ref, saved_refs = refs[:4], refs[4:6], refs[6], refs[7:11]
    refs = refs[11:]
    final = want == ("grads",)
    if final:
        held_refs, steps_ref, refs = refs[0:2], refs[2], refs[3:]
    elif len(sides) == 2:
        small_refs, refs = refs[0:2], refs[2:]
    refs = refs[after:]
    part_refs, refs = (refs[:4], refs[4:]) if final else (refs[:1], refs[1:])
    if not final:
        rate_ref, refs = refs[0], refs[1:]
    saved_buf, up_buf, end_buf, part_buf, pack_ref = refs[:5]
    saved_sem, up_sem, part_sem, end_sem, pack_sem = refs[5:]
    mine = lax.axis_index("section")
    layers = [high_at - side for side in sides]
    fetch_packs(layers, pack_refs, pack_ref, pack_sem)
    ends = pltpu.make_async_copy(end_ref, end_buf, end_sem.at[0])
    ends.start()
    for side in sides:
        away = lax.rem(mine - (high_at - side) + SECTIONS, SECTIONS)
        pltpu.make_async_copy(up_refs[side], up_buf.at[side], up_sem.at[side]).start()
        for k in range(SECTIONS):

            @pl.when(away == k)
            def _():
                pltpu.make_async_copy(saved_refs[k], saved_buf.at[side], saved_sem.at[side]).start()

    def hand_on(source, layer_at):
        to = [part.at[pl.ds(0, GRAD_ROWS)] for part in part_refs] if final else part_refs
        copies = [pltpu.make_async_copy(source, part, part_sem.at[layer_at]) for part in to]
        if final:
            ahead = lax.rem(layer_at - mine + SECTIONS, SECTIONS)
            for k in range(SECTIONS):

                @pl.when(ahead == k)
                def _():
                    copies[k].start()
        else:
            copies[0].start()
        moved.append(copies[0])

    moved = []
    steps = slice(FAMILIES * ROWS, GRAD_ROWS)
    if final:
        for side in range(2):
            hand_on(held_refs[side], high_at + 2 - side)
            pltpu.make_async_copy(steps_ref.at[side], part_buf.at[side, steps], end_sem.at[1 + side]).start()
    wait_packs(layers, pack_refs, pack_ref, pack_sem)
    ready = [Layer(pack_ref, layers[0], family) for family in range(FAMILIES)]
    ends.wait()
    smalls_of = []
    for side in sides:
        pltpu.make_async_copy(up_refs[side], up_buf.at[side], up_sem.at[side]).wait()
        pltpu.make_async_copy(saved_refs[0], saved_buf.at[side], saved_sem.at[side]).wait()
        smalls = jnp.zeros((GROUP, LANES), F32)
        for family in range(FAMILIES):

            def upper_at(rows):
                return up_buf[side, family, rows, :].astype(F32)

            layer = ready[family] if side == sides[0] else Layer(pack_ref, high_at - side, family)
            grads, grad_step, small = phase_c(family, side, layer, upper_at, saved_buf.at[side], end_buf, want)
            if "grads" in want:
                part_buf[side, family * ROWS : (family + 1) * ROWS, :] = grads.astype(BF16)
            if "rates" in want:
                below = FAMILIES * ROWS + family * GROUP
                part_buf[side, below : below + GROUP, :] = grad_step.astype(BF16)
                smalls = smalls + small
        if final:
            pltpu.make_async_copy(steps_ref.at[side], part_buf.at[side, steps], end_sem.at[1 + side]).wait()
        if "grads" in want:
            hand_on(part_buf.at[side], high_at - side)
        else:
            moved.append(pltpu.make_async_copy(part_buf.at[side, steps], part_refs[0].at[side], part_sem.at[side]))
            moved[-1].start()
        smalls_of.append(smalls)
    if final:
        pass
    elif len(sides) == 2:
        blocks = smalls_of[::-1] + [small_refs[1][...], small_refs[0][...]]
        turned = jnp.transpose(jnp.concatenate(blocks + [jnp.zeros((STATE, LANES), F32)], axis=0))
        row = turned[0:1] + pltpu.roll(turned[1:2], STATE, 1)
        rate_ref[...] = jnp.broadcast_to(row[None], (BRANCHES, 1, LANES))
    else:
        rate_ref[...] = smalls_of[0]
    for copy in moved:
        copy.wait()


def chain_kernel(*refs):
    got_ref, end_ref = refs[0], refs[-1]
    lanes = lane_ids((STATE // 2, LANES))
    prompt = BRANCHES // 2
    fork = jnp.zeros((HEADDIM, LANES), F32)
    for at in range(prompt, BRANCHES):
        fork = fork + got_ref[at, 0:HEADDIM, :].astype(F32)
    plain, extra = fork, jnp.zeros((HEADDIM, LANES), F32)
    blank = jnp.zeros((STATE, LANES), F32)
    for at in range(prompt - 1, -1, -1):
        tail = got_ref[at, 96:112, :].astype(F32)
        total = tail[0:1, :] + tail[1:2, :]
        plain = total * plain
        extra = total * extra
        end_ref[at, :, :] = (plain + extra).astype(BF16)
        if at == 0:
            break
        packed = got_ref[at, HEADDIM : HEADDIM + 32, :].astype(F32)
        turned = pltpu.roll(packed, STATE, 1)
        move = jnp.concatenate(
            [jnp.where(lanes >= STATE, turned, 0.0), jnp.where(lanes >= STATE, packed, 0.0), blank], axis=0
        ).astype(BF16)
        extra = extra + dot2(split(plain), move, NN)
        plain = plain + got_ref[at, 0:HEADDIM, :].astype(F32)
    for at in range(prompt, BRANCHES):
        end_ref[at, :, :] = jnp.zeros((HEADDIM, LANES), BF16)


def pack_kernel(*refs):
    sources, decay_ref, gain_ref = refs[0:3], refs[3], refs[4]
    pack_refs = refs[5:9]
    in_ref, out_ref, step_ref, both_ref, rate_ref, sems, send_sems = refs[9:]
    copies = [
        pltpu.make_async_copy(source.at[0], to, sems.at[at])
        for at, (source, to) in enumerate(zip(sources, (in_ref, out_ref, step_ref)))
    ]
    for copy in copies:
        copy.start()
    mine = lax.axis_index("section")
    base = FAMILIES * ROWS
    rate_ref[0] = jnp.transpose(jnp.broadcast_to(decay_ref[...], (LANES, SECTIONS * GROUP)))
    rate_ref[1] = jnp.transpose(jnp.broadcast_to(gain_ref[...], (LANES, SECTIONS * GROUP)))
    for copy in copies:
        copy.wait()
    for k in range(SECTIONS):
        heads = pl.ds(pl.multiple_of(lax.rem(mine + k, SECTIONS) * GROUP, GROUP), GROUP)
        for family in range(FAMILIES):
            both_ref[k, base + family * GROUP : base + (family + 1) * GROUP, :] = step_ref[family, heads, :]
        both_ref[k, base + 2 * GROUP : base + 3 * GROUP, :] = rate_ref[0, heads, :]
        both_ref[k, base + 3 * GROUP : base + 4 * GROUP, :] = rate_ref[1, heads, :]
    for family in range(FAMILIES):
        turned = jnp.transpose(jnp.concatenate([in_ref[family], out_ref[family]], axis=0))
        for k in range(SECTIONS):
            both_ref[k, family * ROWS : (family + 1) * ROWS, :] = turned
    copies = []
    for k in range(SECTIONS):
        copies.append(pltpu.make_async_copy(both_ref.at[k], pack_refs[k], send_sems.at[k]))
        copies[-1].start()
    for copy in copies:
        copy.wait()


def sort_kernel(at_ref, *refs):
    for x_ref, s_ref, o_ref in zip(refs[0:4], refs[4:8], refs[8:12]):
        o_ref[0, 0:COLS] = jnp.transpose(x_ref[0, 0])
        whole = s_ref[0, 0, 0].reshape(COLS, STATE)
        o_ref[0, COLS:SAVED_ROWS] = jnp.concatenate([whole[: COLS // 2], whole[COLS // 2 :]], axis=1).astype(BF16)


def fetch_home(early, late, to, sems):
    mine = lax.axis_index("section")
    for is_early, pieces in ((True, early), (False, late)):

        @pl.when((mine >= 2) == is_early)
        def _():
            for k in range(SECTIONS):
                source = lax.rem(mine - k + SECTIONS, SECTIONS)
                pltpu.make_async_copy(pieces[k], to(source), sems.at[k]).start()

    for k in range(SECTIONS):
        pltpu.make_async_copy(early[k], to(k), sems.at[k]).wait()


def home_small_kernel(*refs):
    piece_refs = refs[:4]
    in_ref, out_ref, step_ref, decay_ref, skip_ref, part_ref, part_sem = refs[-7:]
    mine = lax.axis_index("section")
    for k in range(SECTIONS):
        source = lax.rem(mine - k + SECTIONS, SECTIONS)
        pltpu.make_async_copy(piece_refs[k], part_ref.at[source], part_sem.at[k]).start()
    for k in range(SECTIONS):
        pltpu.make_async_copy(piece_refs[k], part_ref.at[k], part_sem.at[k]).wait()
    for family in range(FAMILIES):
        rows = slice(family * ROWS, (family + 1) * ROWS)
        total = part_ref[0, rows, :].astype(F32)
        for k in range(1, SECTIONS):
            total = total + part_ref[k, rows, :].astype(F32)
        turned = jnp.transpose(total)
        in_ref[0, family] = turned[0:STATE]
        out_ref[0, family] = turned[STATE:]
        below = FAMILIES * ROWS + family * GROUP
        for k in range(SECTIONS):
            step_ref[0, family, k * GROUP : (k + 1) * GROUP, :] = part_ref[k, below : below + GROUP, :].astype(F32)
    section = (lane_ids((8, LANES)) & (STATE - 1)) >> 4
    total = jnp.zeros((8, LANES), F32)
    for at in range(SECTIONS):
        tail = part_ref[at, GRAD_ROWS:HOME_ROWS, :].astype(F32)
        row = jnp.broadcast_to(tail[0:1] + tail[1:2], (8, LANES))
        shift = lax.rem(at - mine + SECTIONS, SECTIONS) * GROUP
        ahead, behind = pltpu.roll(row, shift, 1), pltpu.roll(row, shift + STATE, 1)
        low = (lane_ids((8, LANES)) & (STATE - 1)) >= shift
        total = jnp.where(section == at, jnp.where(low, ahead, behind), total)
    decay_ref[...] = total[0:1, 0:STATE]
    skip_ref[...] = total[0:1, STATE:]


def home_grad_kernel(*refs):
    early, late = refs[0:4], refs[4:8]
    grad_ref, turned_buf, grad_buf, grad_sem, out_sem = refs[8:]
    fetch_home(early, late, lambda source: turned_buf.at[source], grad_sem)
    outs = []
    for source in range(SECTIONS):
        cols = slice(source * COLS, (source + 1) * COLS)
        for family in range(FAMILIES):
            grad_buf[family, :, cols] = jnp.transpose(turned_buf[source, family])
        outs.append(
            pltpu.make_async_copy(
                grad_buf.at[:, :, pl.ds(source * COLS, COLS)],
                grad_ref.at[0, :, :, pl.ds(source * COLS, COLS)],
                out_sem.at[source],
            )
        )
        outs[-1].start()
    for out in outs:
        out.wait()


def rate_sum_kernel(scale, *refs):
    got_ref, part_refs, buf, sems = refs[0], refs[5:9], refs[9], refs[10]
    total = got_ref[0]
    for at in range(1, BRANCHES):
        total = total + got_ref[at]
    total = jnp.broadcast_to(total * scale, (16, LANES))
    high = total.astype(BF16).astype(F32)
    place = lax.broadcasted_iota(jnp.int32, (16, LANES), 0)
    buf[...] = jnp.where(place == 0, high, jnp.where(place == 1, total - high, 0.0)).astype(BF16)
    copies = [
        pltpu.make_async_copy(buf, part_refs[to].at[pl.ds(GRAD_ROWS, 16)], sems.at[to]) for to in range(SECTIONS)
    ]
    for copy in copies:
        copy.start()
    for copy in copies:
        copy.wait()


ALL = ("grads", "rates")
VM = pl.BlockSpec(memory_space=pltpu.VMEM)
SM = pl.BlockSpec(memory_space=pltpu.SMEM)
ANY = pl.BlockSpec(memory_space=pl.ANY)
HBM = pl.BlockSpec(memory_space=pltpu.HBM)
PARAMS = pltpu.CompilerParams(vmem_limit_bytes=VMEM_LIMIT)
SMALL_PARAMS = pltpu.CompilerParams(vmem_limit_bytes=32 * 1024 * 1024)


PACKS = pltpu.VMEM((SECTIONS, PACK_ROWS, LANES), F32)


def shape(dims, dtype):
    return jax.ShapeDtypeStruct(dims, dtype)


def cost(flops):
    return pl.CostEstimate(flops=flops, bytes_accessed=4_000_000, transcendentals=0)


def sems(count):
    return pltpu.SemaphoreType.DMA((count,))


def pack_small(state_in, state_out, step_size, decay_rate, skip_gain):
    turned = [jnp.transpose(value, (0, 1, 3, 2)) for value in (state_in, state_out, step_size)]
    return pl.pallas_call(
        pack_kernel,
        out_shape=[shape((PACK_ROWS, LANES), F32)] * SECTIONS,
        in_specs=[ANY] * 3 + [VM] * 2,
        out_specs=[HBM] * SECTIONS,
        scratch_shapes=[
            pltpu.VMEM((FAMILIES, STATE, ROWS), F32),
            pltpu.VMEM((FAMILIES, STATE, ROWS), F32),
            pltpu.VMEM((FAMILIES, SECTIONS * GROUP, ROWS), F32),
            pltpu.VMEM((SECTIONS, PACK_ROWS, LANES), F32),
            pltpu.VMEM((2, SECTIONS * GROUP, LANES), F32),
            sems(3),
            sems(4),
        ],
        compiler_params=PARAMS,
        name="pack_small",
    )(*turned, decay_rate, skip_gain)


def sort_heads(layer_input, saved_states):
    mine = jnp.full((1,), lax.axis_index("section"), jnp.int32)

    def x_spec(k):
        return pl.BlockSpec(
            (1, 1, ROWS, COLS), lambda f, at: (0, f, 0, lax.rem(at[0] + k, SECTIONS))
        )

    def s_spec(k):
        return pl.BlockSpec(
            (1, 1, 1, GROUP, HEADDIM, STATE), lambda f, at: (0, f, 0, lax.rem(at[0] + k, SECTIONS), 0, 0)
        )

    return pl.pallas_call(
        sort_kernel,
        grid_spec=pltpu.PrefetchScalarGridSpec(
            num_scalar_prefetch=1,
            grid=(FAMILIES,),
            in_specs=[x_spec(k) for k in range(SECTIONS)] + [s_spec(k) for k in range(SECTIONS)],
            out_specs=[pl.BlockSpec((1, SAVED_ROWS, LANES), lambda f, at: (f, 0, 0))] * SECTIONS,
        ),
        out_shape=[shape((FAMILIES, SAVED_ROWS, LANES), BF16)] * SECTIONS,
        compiler_params=PARAMS,
        cost_estimate=cost(4_000_000_000),
        name="sort_heads",
    )(mine, *([layer_input] * SECTIONS), *([saved_states] * SECTIONS))


def first_phase(high_at, lengths, cotangent, packs, after):
    return pl.pallas_call(
        functools.partial(first_kernel, high_at, len(after)),
        out_shape=[
            shape((BRANCHES, SEND_ROWS, LANES), BF16),
            shape((FAMILIES, COLS, ROWS), BF16),
        ],
        in_specs=[SM] + [ANY] * (5 + len(after)),
        out_specs=[HBM, HBM],
        scratch_shapes=[
            pltpu.VMEM((FAMILIES, ROWS, COLS), BF16),
            pltpu.VMEM((FAMILIES, COLS, ROWS), BF16),
            pltpu.VMEM((BRANCHES, SEND_ROWS, LANES), BF16),
            PACKS,
            sems(4),
            sems(4),
        ],
        compiler_params=PARAMS,
        name="first_phase",
    )(lengths, cotangent, *packs, *after)


def later_phase(high_at, goes_on, packs, upstream, ends, after):
    outs = [shape((FAMILIES, COLS, ROWS), BF16)] * 4
    outs += [shape((FAMILIES, COLS, ROWS), BF16)] * 2
    scratch = [
        pltpu.VMEM((2, FAMILIES, COLS, ROWS), BF16),
        pltpu.VMEM((FAMILIES, COLS, ROWS), BF16),
        pltpu.VMEM((BRANCHES, HEADDIM, LANES), BF16),
        PACKS,
        sems(2),
        sems(2),
        sems(2),
        sems(4),
    ]
    if goes_on:
        outs += [shape((BRANCHES, SEND_ROWS, LANES), BF16)]
        scratch += [pltpu.VMEM((BRANCHES, SEND_ROWS, LANES), BF16), sems(2)]
    return pl.pallas_call(
        functools.partial(later_kernel, high_at, goes_on, len(after)),
        out_shape=outs,
        in_specs=[ANY] * (6 + len(after)),
        out_specs=[HBM] * len(outs),
        scratch_shapes=scratch,
        compiler_params=PARAMS,
        name="later_phase",
    )(*packs, upstream, ends, *after)


def other_phase(high_at, sides, want, packs, ups, ends, saved, held, after):
    if want == ("grads",):
        outs = [shape((HOME_ROWS, LANES), BF16)] * SECTIONS
        extra, specs = [ANY] * 3, [HBM] * SECTIONS
    elif len(sides) == 2:
        outs = [shape((2, FAMILIES * GROUP, LANES), BF16), shape((BRANCHES, 1, LANES), F32)]
        extra, specs = [VM] * 2, [HBM, VM]
    else:
        outs = [shape((GRAD_ROWS, LANES), BF16), shape((GROUP, LANES), F32)]
        extra, specs = [], [HBM, VM]
    return pl.pallas_call(
        functools.partial(other_kernel, high_at, sides, want, len(after)),
        out_shape=outs,
        in_specs=[ANY] * 11 + extra + [ANY] * len(after),
        out_specs=specs,
        scratch_shapes=[
            pltpu.VMEM((2, FAMILIES, SAVED_ROWS, LANES), BF16),
            pltpu.VMEM((2, FAMILIES, COLS, ROWS), BF16),
            pltpu.VMEM((BRANCHES, HEADDIM, LANES), BF16),
            pltpu.VMEM((2, GRAD_ROWS, LANES), BF16),
            PACKS,
            sems(2),
            sems(2),
            sems(4),
            sems(3),
            sems(4),
        ],
        compiler_params=PARAMS,
        cost_estimate=cost(6_000_000_000 if len(want) == 2 else 5_000_000_000),
        name="other_phase",
    )(*packs, *ups, ends, *saved, *held, *after)


def chain(got, after):
    return pl.pallas_call(
        chain_kernel,
        out_shape=shape((BRANCHES, HEADDIM, LANES), BF16),
        in_specs=[VM] + [ANY] * len(after),
        out_specs=VM,
        compiler_params=SMALL_PARAMS,
        name="chain",
    )(got, *after)


def home_small(parts, after):
    return pl.pallas_call(
        home_small_kernel,
        out_shape=[
            shape((1, FAMILIES, STATE, ROWS), F32),
            shape((1, FAMILIES, STATE, ROWS), F32),
            shape((1, FAMILIES, SECTIONS * GROUP, ROWS), F32),
            shape((1, SECTIONS * GROUP), F32),
            shape((1, SECTIONS * GROUP), F32),
        ],
        in_specs=[ANY] * (4 + len(after)),
        out_specs=[VM] * 5,
        scratch_shapes=[pltpu.VMEM((SECTIONS, HOME_ROWS, LANES), BF16), sems(SECTIONS)],
        compiler_params=PARAMS,
        name="home_small",
    )(*parts, *after)


def home_grad(early, late):
    return pl.pallas_call(
        home_grad_kernel,
        out_shape=shape((1, FAMILIES, ROWS, SECTIONS * COLS), BF16),
        in_specs=[ANY] * 8,
        out_specs=HBM,
        scratch_shapes=[
            pltpu.VMEM((SECTIONS, FAMILIES, COLS, ROWS), BF16),
            pltpu.VMEM((FAMILIES, ROWS, SECTIONS * COLS), BF16),
            sems(SECTIONS),
            sems(SECTIONS),
        ],
        compiler_params=PARAMS,
        cost_estimate=cost(3_000_000_000),
        name="home_grad",
    )(*early, *late)


def rate_sum(got, parts, scale):
    return pl.pallas_call(
        functools.partial(rate_sum_kernel, scale),
        out_shape=[shape((HOME_ROWS, LANES), BF16)] * SECTIONS,
        in_specs=[VM] + [HBM] * SECTIONS,
        out_specs=[HBM] * SECTIONS,
        scratch_shapes=[pltpu.VMEM((16, LANES), BF16), sems(SECTIONS)],
        input_output_aliases={1 + k: k for k in range(SECTIONS)},
        compiler_params=PARAMS,
        name="rate_sum",
    )(got, *parts)


def swap(value, axis):
    return lax.all_to_all(value, axis, 0, 0, tiled=True)


def send_on(value, k, targets):
    pairs = [(i, (i + k) % SECTIONS) for i in range(SECTIONS) if (i + k) % SECTIONS in targets]
    return lax.ppermute(value, "section", pairs)


def send_home(pieces, targets):
    return [pieces[0]] + [send_on(pieces[k], k, targets) for k in range(1, SECTIONS)]


def exchange(send, after):
    return swap(chain(swap(send, "branch"), after), "branch")


def shards(
    layer_input,
    cotangent,
    state_in,
    state_out,
    step_size,
    saved_states,
    decay_rate,
    skip_gain,
    lengths,
):
    grad_scale = 1.0 / math.sqrt(FAMILIES * ROWS * BRANCHES * HEADDIM)
    everyone = tuple(range(SECTIONS))
    packs = pack_small(state_in, state_out, step_size, decay_rate, skip_gain)
    packs = [packs[0]] + [send_on(packs[k], k, everyone) for k in range(1, SECTIONS)]
    saved = sort_heads(layer_input, saved_states)
    top, upstream = first_phase(3, lengths, cotangent, packs, [saved[0]])
    saved = [saved[0]] + [send_on(saved[k], k, everyone) for k in range(1, SECTIONS)]
    ends = exchange(top, [])
    early = later_phase(3, True, packs, upstream, ends, [saved[1], saved[3]])
    early_grads = send_home(early[:4], (2, 3))
    ups = (upstream, early[4])
    part_a, small_a = other_phase(3, (0,), ALL, packs, ups, ends, saved, [], [])
    next_ends = exchange(early[6], [])
    part_b, small_b = other_phase(3, (1,), ALL, packs, ups, ends, saved, [], [])
    late = later_phase(1, False, packs, early[5], next_ends, early_grads[1:] + [part_b])
    late_grads = send_home(late[:4], (0, 1))
    ups = (early[5], late[4])
    steps, rates = other_phase(1, (0, 1), ("rates",), packs, ups, next_ends, saved, [small_a, small_b], [])
    parts = other_phase(1, (0, 1), ("grads",), packs, ups, next_ends, saved, [part_a, part_b, steps], [])
    parts = send_home(rate_sum(swap(rates, "branch"), parts, grad_scale), everyone)
    grad = home_grad(early_grads, late_grads)
    *others, decay_sum, skip_sum = home_small(parts, [grad])
    others = tuple(jnp.transpose(value, (0, 1, 3, 2)) for value in others)
    return (grad,) + others + (decay_sum, skip_sum)


def solution(mesh):
    placed = (
        P("section", None, "branch", None),
        P(None, "branch", None),
        P("section", None, "branch", None),
        P("section", None, "branch", None),
        P("section", None, "branch", None),
        P("section", None, "branch", None, None, None),
        P("section", None),
        P("section", None),
        P(),
    )
    return jax.shard_map(
        shards,
        mesh=mesh,
        in_specs=placed,
        out_specs=(
            P("section", None, "branch", None),
            P("section", None, "branch", None),
            P("section", None, "branch", None),
            P("section", None, "branch", None),
            P("section", None),
            P("section", None),
        ),
        check_vma=False,
    )
```
